32 devices in a mesh: seq: 2 (over y), exp: 16 (over z, x, core).
Axes of the slice: x: 2, y: 2, z: 4, core: 2. Of those that a mesh axis runs over, the one named last changes fastest.
Arguments:
- tokens: bfloat16 [2048, 4096], P(('seq', 'exp')), may hold values from -6 to 6
- norm_gain: float32 [4096], replicated, may hold values from 0.1 to 1.9
- queries: bfloat16 [2048, 2048], P(('seq', 'exp')), may hold values from -24 to 24
- attn_keys: bfloat16 [2048, 2048], P(('seq', 'exp')), may hold values from -4.5 to 4.5
- attn_values: bfloat16 [2048, 2048], P(('seq', 'exp')), may hold values from -6 to 6
- expert_ids: int32 [2048, 2], P(('seq', 'exp')), may hold values from 0 to 63, all different within a row; in each aligned block of 64 rows (0 to 63, 64 to 127, ...) at most 2 rows name the same one
- route_weights: float32 [2048, 2], P(('seq', 'exp')), may hold values from 0.1 to 1
- gate_proj: bfloat16 [64, 1408, 4096], P('exp', 'seq'), may hold values from -0.09375 to 0.09375
- up_proj: bfloat16 [64, 1408, 4096], P('exp', 'seq'), may hold values from -0.09375 to 0.09375
- down_proj: bfloat16 [64, 1408, 4096], P('exp', 'seq'), may hold values from -0.15625 to 0.15625
Outputs:
- attention: bfloat16 [2048, 2048], P(('seq', 'exp'))
- expert_mix: bfloat16 [2048, 4096], P(('seq', 'exp'))
The draws below stay inside these ranges and needn't reach their ends.
Inputs may be any that keep to these rules, and one draw needn't show every extreme that they name: `expert_ids`: the two experts of a token differ. Among the rows of one device (64 consecutive tokens, aligned), every expert is named exactly 2 times.
All inputs are finite; a program needn't handle non-finite values.
Results may differ from the reference program's by a relative error of at most 0.015.
Values may be sent and summed in bfloat16 or wider, within the bound.
No kernel may reach another device: no remote copies, remote signals or barrier semaphores. Data moves between devices by JAX's collectives and lax.ppermute only.
A program may use at most 128 MiB of HBM per device.

```python
import math
import jax
import jax.numpy as jnp
import numpy as np
from jax import lax

D = 4096
FF = 1408
EXPERTS = 64
HEADS = 32
HDIM = 64
SUMS = 64
CAP = 2
TOK_DEV = 64
TOKENS = 2048
SEG_LEN = 512
SEGS = 4
BLK = 8
ATT = 2048
FF_DEV = 704
N_SEQ = 2


def key_parts(key):
    base_key = jax.random.fold_in(key, 71)
    key_one = jax.random.fold_in(base_key, 0)
    drawn_vals = jnp.clip(jax.random.normal(key_one, (TOKENS, ATT), jnp.float32), -4.5, 4.5)
    return drawn_vals


def draw_attn_keys(key, part):
    drawn_vals = key_parts(key)
    return drawn_vals.astype(jnp.bfloat16)


def draw_queries(key, part):
    query_key = jax.random.fold_in(key, 29)
    query_vals = jnp.clip(jax.random.normal(query_key, (TOKENS, ATT), jnp.float32), -6.0, 6.0)
    return query_vals.astype(jnp.bfloat16)


def block_levels(key, extent, shards, least, largest):
    gain, own = 1.0, jax.random.fold_in(key, 6)
    for dim, blocks in shards:
        draws = jnp.exp(jax.random.uniform(jax.random.fold_in(own, dim), (blocks,), jnp.float32, least / len(shards), largest / len(shards)))
        gain = gain * jnp.repeat(draws, extent[dim] // blocks).reshape([-1 if axis == dim else 1 for axis in range(len(extent))])
    return gain


def routed_block(own_key, own, number, rows, count, top, bound, skew):
    order = jax.random.permutation(own_key, count)
    packed, common = portions_of(count, rows * top, bound, skew, True), portions_of(count, rows * top, bound, skew, False)
    places = jnp.arange(count)

    def named(sizes, rotation):
        used = int((sizes > 0).sum())
        fixed = max(1, used // 4)
        moved = fixed + (places - fixed + rotation * (used - fixed)) % max(1, count - fixed)
        return jnp.zeros((count,), jnp.int32).at[order[jnp.where(places < fixed, places, moved)]].set(jnp.asarray(sizes, jnp.int32))

    sizes = jnp.where(number % 4 == 0, named(packed, number // 4), named(common, number - number // 4 - 1))
    mixed = jax.random.permutation(jax.random.fold_in(own, 3), count)
    source_of, taker = mixed[0:count // 2 * 2:2], mixed[1:count // 2 * 2:2]
    room = jnp.minimum(sizes[source_of] - 1, bound - sizes[taker]) // 2
    room = jnp.where((source_of == order[0]) | (taker == order[0]) | (sizes[taker] == 0), 0, jnp.maximum(room, 0))
    moved = jax.random.randint(jax.random.fold_in(own, 4), (count // 2,), 0, 1 << 20) % (room + 1)
    sizes = sizes.at[source_of].add(-moved).at[taker].add(moved)
    items = jnp.searchsorted(jnp.cumsum(sizes), jnp.arange(rows * top), side="right").astype(jnp.int32)
    table = items.reshape(top, rows).T
    table = table[jax.random.permutation(jax.random.fold_in(own, 1), rows)]
    rotation = jax.random.randint(jax.random.fold_in(own, 2), (rows, 1), 0, top)
    return jnp.take_along_axis(table, (jnp.arange(top)[None, :] + rotation) % top, axis=1)


def portions_of(count, total, bound, lean, full):
    loads = [(1 << 20) // math.isqrt(rank ** lean) + 1 for rank in range(1, count + 1)]
    largest = bound if full else min(bound, max(-(-total // count), total * loads[0] // sum(loads)))
    least = 1 if total - largest >= count - 1 else 0
    given, spare = [largest] + [least] * (count - 1), total - largest - least * (count - 1)
    while spare > 0:
        free = [i for i in range(1, count) if given[i] < largest] or [i for i in range(1, count) if given[i] < bound]
        pool, remaining = sum([loads[i] for i in free]), spare
        for i in free:
            more = min(bound - given[i], max(1, remaining * loads[i] // pool), spare)
            given[i] = given[i] + more
            spare = spare - more
    return np.array(given)


def scatter_about(stream_key, dims, width, most, shards=(), kind=jnp.bfloat16):
    values = jax.random.normal(stream_key, dims, jnp.float32) * width
    if len(shards) > 0:
        values = block_levels(stream_key, dims, shards, -0.22, 0.18) * values
    return jnp.clip(values, min=-most, max=most).astype(kind)


def setup_inputs(seed: int = 0) -> dict:
    keys = jax.random.split(jax.random.key(seed), 11)
    tokens = scatter_about(keys[0], (TOKENS, D), 1.0, 6.0, ((0, 32),))
    norm_gain = jnp.clip(1.0 + 0.18 * jax.random.normal(keys[1], (D,), jnp.float32), 0.1, 1.9)
    queries = draw_queries(jax.random.fold_in(keys[10], 71), 0)
    attn_keys = draw_attn_keys(jax.random.fold_in(keys[10], 71), 0)
    attn_values = scatter_about(keys[4], (TOKENS, ATT), 1.0, 6.0, ((0, 32),))
    expert_ids_keys = jax.random.split(jax.random.fold_in(keys[5], 1), TOKENS // TOK_DEV)
    expert_ids_turns = jax.random.permutation(jax.random.fold_in(keys[5], 3), TOKENS // TOK_DEV)
    expert_ids = jax.vmap(lambda own, number: routed_block(jax.random.fold_in(keys[5], 2), own, number, TOK_DEV, EXPERTS, 2, CAP, 2))(expert_ids_keys, expert_ids_turns).reshape((TOKENS, 2))
    route_weights = jnp.clip(0.1 + 0.9 * jax.random.uniform(keys[6], (TOKENS, 2), jnp.float32) ** block_levels(keys[6], (TOKENS, 2), ((0, 32),), -0.2, 0.2), 0.1, 1.0)
    gate_proj = scatter_about(keys[7], (EXPERTS, FF, D), D ** -0.5, 0.09375, ((0, 16), (1, 2)))
    up_proj = scatter_about(keys[8], (EXPERTS, FF, D), D ** -0.5, 0.09375, ((0, 16), (1, 2)))
    down_proj = scatter_about(keys[9], (EXPERTS, FF, D), FF ** -0.5, 0.15625, ((0, 16), (1, 2)))
    return dict(tokens=tokens, norm_gain=norm_gain, queries=queries, attn_keys=attn_keys, attn_values=attn_values, expert_ids=expert_ids, route_weights=route_weights, gate_proj=gate_proj, up_proj=up_proj, down_proj=down_proj)


EPS = 1e-05
NEG = -1e+30
HIGH = lax.Precision.HIGHEST

def normalize(tokens, norm_gain):
    values = tokens.astype(jnp.float32)
    inv_rms = lax.rsqrt(lax.optimization_barrier(jnp.mean(values * values, axis=-1, keepdims=True)) + EPS)
    return (values * inv_rms * norm_gain.astype(jnp.float32)).astype(jnp.bfloat16)

def summarize(block_vals):
    values = block_vals.astype(jnp.float32).reshape(SEGS, SUMS, BLK, HDIM)
    summed = lax.optimization_barrier(jnp.sum(values, axis=2)) * (1.0 / math.sqrt(BLK))
    return summed.astype(jnp.bfloat16).reshape(SEGS * SUMS, 1, HDIM)

def attend(query_blk, seg_keys, seg_values, sum_keys, sum_values, segment):
    score_scale = 1.0 / math.sqrt(HDIM)
    query_f = query_blk.astype(jnp.float32)
    local_sc = jnp.einsum('qhd,khd->hqk', query_f, seg_keys.astype(jnp.float32), precision=HIGH) * score_scale
    summ_sc = jnp.einsum('qhd,khd->hqk', query_f, sum_keys.astype(jnp.float32), precision=HIGH) * score_scale
    query_pos = jnp.arange(query_blk.shape[0], dtype=jnp.int32)
    key_pos = jnp.arange(seg_keys.shape[0], dtype=jnp.int32)
    local_ok = key_pos[None, :] <= query_pos[:, None]
    summ_ok = jnp.arange(sum_keys.shape[0], dtype=jnp.int32) // SUMS < segment
    local_sc = jnp.where(local_ok[None], local_sc, NEG)
    summ_sc = jnp.where(summ_ok[None, None], summ_sc, NEG)
    top_sc = jnp.maximum(lax.optimization_barrier(jnp.max(local_sc, axis=-1, keepdims=True)), lax.optimization_barrier(jnp.max(summ_sc, axis=-1, keepdims=True)))
    local_ex = jnp.exp(local_sc - top_sc)
    summ_ex = jnp.exp(summ_sc - top_sc)
    totals = lax.optimization_barrier(jnp.sum(local_ex, axis=-1, keepdims=True)) + lax.optimization_barrier(jnp.sum(summ_ex, axis=-1, keepdims=True))
    local_wt = (local_ex / totals).astype(jnp.bfloat16).astype(jnp.float32)
    summ_wt = (summ_ex / totals).astype(jnp.bfloat16).astype(jnp.float32)
    mixed_out = jnp.einsum('hqk,khd->qhd', local_wt, seg_values.astype(jnp.float32), precision=HIGH)
    return mixed_out + jnp.einsum('hqk,khd->qhd', summ_wt, sum_values.astype(jnp.float32), precision=HIGH)

def reference(tokens, norm_gain, queries, attn_keys, attn_values, expert_ids, route_weights, gate_proj, up_proj, down_proj):
    normed = normalize(tokens, norm_gain)

    def heads_major(array):
        return array.reshape(SEGS, SEG_LEN, HEADS, HDIM).transpose(2, 0, 1, 3)

    def per_head(inputs):
        head_q, head_k, head_v = inputs
        sum_keys = summarize(head_k)
        sum_values = summarize(head_v)

        def per_seg(seg_index):
            return attend(head_q[seg_index][:, None, :], head_k[seg_index][:, None, :], head_v[seg_index][:, None, :], sum_keys, sum_values, seg_index)
        return lax.map(per_seg, jnp.arange(SEGS, dtype=jnp.int32))
    head_out = lax.map(per_head, (heads_major(queries), heads_major(attn_keys), heads_major(attn_values)))
    head_out = head_out.astype(jnp.bfloat16)[:, :, :, 0, :]
    attention = head_out.transpose(1, 2, 0, 3).reshape(TOKENS, HEADS * HDIM)
    block_count = TOKENS // TOK_DEV
    id_blocks = expert_ids.reshape(block_count, TOK_DEV * 2)
    onehot = (id_blocks[:, :, None] == jnp.arange(EXPERTS, dtype=jnp.int32)[None, None, :]).astype(jnp.int32)
    before = jnp.cumsum(onehot, axis=1) - onehot
    slot_ids = lax.optimization_barrier(jnp.sum(before * onehot, axis=2))
    row_pos = jnp.arange(block_count, dtype=jnp.int32)[:, None] * CAP + slot_ids
    token_of = (jnp.arange(TOKENS * 2, dtype=jnp.int32) // 2).reshape(block_count, TOK_DEV * 2)
    row_table = jnp.full((EXPERTS, block_count * CAP), TOKENS, jnp.int32)
    row_table = row_table.at[id_blocks.reshape(-1), row_pos.reshape(-1)].set(token_of.reshape(-1))
    weight_table = jnp.zeros((EXPERTS, block_count * CAP), jnp.float32)
    weight_table = weight_table.at[id_blocks.reshape(-1), row_pos.reshape(-1)].set(route_weights.reshape(-1).astype(jnp.float32))
    padded = jnp.concatenate([normed, jnp.zeros((1, D), jnp.bfloat16)], axis=0)

    def per_expert(running, inputs):
        table_e, weight_e, gate_e, up_e, down_e = inputs
        rows_e = padded[table_e]
        gate_act = jnp.dot(rows_e, gate_e.T, preferred_element_type=jnp.float32)
        up_act = jnp.dot(rows_e, up_e.T, preferred_element_type=jnp.float32)
        hidden = (jax.nn.silu(gate_act) * up_act).astype(jnp.bfloat16)
        piece_list = []
        for block_index in range(N_SEQ):
            lower = block_index * FF_DEV
            piece = jnp.dot(hidden[:, lower:lower + FF_DEV], down_e[lower:lower + FF_DEV], preferred_element_type=jnp.float32)
            piece_list.append(lax.optimization_barrier(piece.astype(jnp.bfloat16)).astype(jnp.float32))
        total_sum = piece_list[0]
        for piece in piece_list[1:]:
            total_sum = total_sum + piece
        expert_out = lax.optimization_barrier(total_sum.astype(jnp.bfloat16)).astype(jnp.float32)
        running = running.at[table_e].add(weight_e[:, None] * expert_out, mode='drop')
        return (running, None)
    running, unused = lax.scan(per_expert, jnp.zeros((TOKENS, D), jnp.float32), (row_table, weight_table, gate_proj, up_proj, down_proj))
    return (attention, running.astype(jnp.bfloat16))
```

```python
import functools
import math

import jax
import jax.numpy as jnp
from jax import lax
from jax.experimental import pallas as pl
from jax.experimental.pallas import tpu as pltpu
from jax.sharding import PartitionSpec as P

EXPERTS = 64
HDIM = 64
SUMS = 64
SEG_DEV = 2
CAP = 2
CHUNKS = 2

EPS = 1e-05
NEG = -1e30
F32 = jnp.float32
BF16 = jnp.bfloat16

VMEM = pl.BlockSpec(memory_space=pltpu.VMEM)
ANY = pl.BlockSpec(memory_space=pl.ANY)
SMEM = pl.BlockSpec(memory_space=pltpu.SMEM)


def params(mib):
    return pltpu.CompilerParams(vmem_limit_bytes=mib * 2**20)


def as_row(column):
    n = column.shape[0]
    eye = lax.broadcasted_iota(jnp.int32, (n, n), 0) == lax.broadcasted_iota(jnp.int32, (n, n), 1)
    return jnp.sum(jnp.where(eye, column, 0), axis=0, keepdims=True)


def slots(ids):
    n = ids.shape[0]
    columns = [ids[:, 0:1], ids[:, 1:2]]
    rows = [as_row(column) for column in columns]
    earlier = lax.broadcasted_iota(jnp.int32, (n, n), 1) < lax.broadcasted_iota(jnp.int32, (n, n), 0)
    found = []
    for column in columns:
        same = (rows[0] == column) | (rows[1] == column)
        before = jnp.sum(jnp.where(same & earlier, 1, 0), axis=1, keepdims=True)
        found.append(column * CAP + before)
    return found


def prep_kernel(tok_ref, gain_ref, ids_ref, *out_refs):
    n = tok_ref.shape[0]
    values = tok_ref[...].astype(F32)
    inv_rms = lax.rsqrt(jnp.mean(values * values, axis=-1, keepdims=True) + EPS)
    normed = (values * inv_rms * gain_ref[...]).astype(BF16)
    first, second = [as_row(column) for column in slots(ids_ref[...])]
    place = lax.broadcasted_iota(jnp.int32, (EXPERTS * CAP, n), 0)
    pick = jnp.where((place == first) | (place == second), 1.0, 0.0).astype(BF16)
    rows = jnp.dot(pick, normed, preferred_element_type=F32)
    dests, step = out_refs[0].shape[0], out_refs[0].shape[1]
    for dest in range(dests):
        for chunk, out_ref in enumerate(out_refs):
            lower = (dest * len(out_refs) + chunk) * step
            out_ref[dest] = rows[lower : lower + step].astype(BF16)


def pack_kernel(q_ref, k_ref, v_ref, out_ref):
    width = out_ref.shape[3]
    for dest in range(out_ref.shape[0]):
        for which, ref in enumerate((q_ref, k_ref, v_ref)):
            out_ref[dest, which] = ref[:, dest * width : (dest + 1) * width]


def sums_kernel(block, recv_ref, out_ref):
    sources, _, tokens, width = recv_ref.shape
    per_source = tokens // block
    total = sources * tokens
    row = lax.broadcasted_iota(jnp.int32, (total // block, total), 0)
    column = lax.broadcasted_iota(jnp.int32, (total // block, total), 1)
    member = jnp.where(column // block == row, 1.0, 0.0).astype(BF16)
    for which in (1, 2):
        values = recv_ref[:, which].reshape(total, width)
        summed = jnp.dot(member, values, preferred_element_type=F32) * (1.0 / math.sqrt(block))
        out_ref[which - 1] = summed.astype(BF16)


def attend_kernel(query_rows, seg_ref, recv_ref, *refs):
    sum_refs, out_ref = refs[:-1], refs[-1]
    sources, _, tokens, width = recv_ref.shape
    seg_len = sources * tokens
    query, key, value = (recv_ref[:, which].reshape(seg_len, width) for which in range(3))
    sum_keys = jnp.concatenate([ref[0] for ref in sum_refs], axis=0)
    sum_values = jnp.concatenate([ref[1] for ref in sum_refs], axis=0)
    sum_total = sum_keys.shape[0]
    scale = 1.0 / math.sqrt(HDIM)
    seen = seg_ref[0] * SUMS
    lane = lax.broadcasted_iota(jnp.int32, (1, width), 1)
    nt = (((1,), (1,)), ((), ()))
    for first in range(0, seg_len, query_rows):
        last = first + query_rows
        local_ok = (
            lax.broadcasted_iota(jnp.int32, (query_rows, last), 1)
            <= lax.broadcasted_iota(jnp.int32, (query_rows, last), 0) + first
        )
        summ_ok = lax.broadcasted_iota(jnp.int32, (query_rows, sum_total), 1) < seen
        mixed = jnp.zeros((query_rows, width), F32)
        for head in range(width // HDIM):
            mine = (lane >= head * HDIM) & (lane < (head + 1) * HDIM)
            rows = jnp.where(mine, query[first:last], jnp.zeros((), BF16))
            local_sc = lax.dot_general(rows, key[:last], nt, preferred_element_type=F32) * scale
            summ_sc = lax.dot_general(rows, sum_keys, nt, preferred_element_type=F32) * scale
            local_sc = jnp.where(local_ok, local_sc, NEG)
            summ_sc = jnp.where(summ_ok, summ_sc, NEG)
            top = jnp.maximum(
                jnp.max(local_sc, axis=-1, keepdims=True), jnp.max(summ_sc, axis=-1, keepdims=True)
            )
            local_ex = jnp.exp(local_sc - top)
            summ_ex = jnp.exp(summ_sc - top)
            inv = 1.0 / (
                jnp.sum(local_ex, axis=-1, keepdims=True) + jnp.sum(summ_ex, axis=-1, keepdims=True)
            )
            got = jnp.dot((local_ex * inv).astype(BF16), value[:last], preferred_element_type=F32)
            got += jnp.dot((summ_ex * inv).astype(BF16), sum_values, preferred_element_type=F32)
            mixed = jnp.where(mine, got, mixed)
        out_ref[first:last] = mixed.astype(BF16)


def ffn_kernel(base, planes, *refs):
    row_refs, (gate_ref, up_ref, down_ref) = refs[:planes], refs[planes : planes + 3]
    out_refs = refs[planes + 3 : 2 * planes + 3]
    buf, x_ref, y_ref, sem = refs[2 * planes + 3 :]
    sources, step, width = row_refs[0].shape
    experts = step // CAP
    copies = []
    for expert in range(experts):
        for which, ref in enumerate((gate_ref, up_ref, down_ref)):
            at = expert * 3 + which
            copy = pltpu.make_async_copy(ref.at[base + expert], buf.at[at], sem.at[at])
            copy.start()
            copies.append(copy)
    total = planes * sources * step
    for plane in range(planes):
        for source in range(sources):
            lower = (plane * sources + source) * step
            y_ref[lower : lower + step] = row_refs[plane][source].astype(F32)
    to = lax.broadcasted_iota(jnp.int32, (total, total), 0)
    frm = lax.broadcasted_iota(jnp.int32, (total, total), 1)
    per = total // experts
    order = (to % per // CAP) * step + (to // per) * CAP + to % CAP
    sort = jnp.where(frm == order, 1.0, 0.0).astype(BF16)
    x_ref[...] = jnp.dot(sort, y_ref[...].astype(BF16), preferred_element_type=F32).astype(BF16)
    nt = (((1,), (1,)), ((), ()))
    for expert in range(experts):
        rows = x_ref[expert * per : (expert + 1) * per]
        copies[expert * 3].wait()
        gate = lax.dot_general(rows, buf[expert * 3], nt, preferred_element_type=F32)
        copies[expert * 3 + 1].wait()
        up = lax.dot_general(rows, buf[expert * 3 + 1], nt, preferred_element_type=F32)
        hidden = (gate / (1.0 + jnp.exp(-gate)) * up).astype(BF16)
        copies[expert * 3 + 2].wait()
        piece = jnp.dot(hidden, buf[expert * 3 + 2], preferred_element_type=F32)
        x_ref[expert * per : (expert + 1) * per] = piece.astype(BF16)
    inverse = (to // step) * CAP + (to % step // CAP) * per + to % CAP
    unsort = jnp.where(frm == inverse, 1.0, 0.0).astype(BF16)
    y_ref[...] = jnp.dot(unsort, x_ref[...], preferred_element_type=F32)
    for plane in range(planes):
        for source in range(sources):
            lower = (plane * sources + source) * step
            out_refs[plane][source] = y_ref[lower : lower + step].astype(BF16)


def mix_kernel(ids_ref, weight_ref, *refs):
    in_refs, out_ref, y_ref = refs[:-2], refs[-2], refs[-1]
    dests, step = in_refs[0].shape[0], in_refs[0].shape[1]
    for dest in range(dests):
        for chunk, ref in enumerate(in_refs):
            lower = (dest * len(in_refs) + chunk) * step
            y_ref[lower : lower + step] = ref[dest].astype(F32)
    rows = y_ref[...].astype(BF16)
    n = ids_ref.shape[0]
    place = lax.broadcasted_iota(jnp.int32, (n, EXPERTS * CAP), 1)
    total = None
    for k, column in enumerate(slots(ids_ref[...])):
        pick = jnp.where(place == column, 1.0, 0.0).astype(BF16)
        part = weight_ref[:, k : k + 1] * jnp.dot(pick, rows, preferred_element_type=F32)
        total = part if total is None else total + part
    out_ref[...] = total.astype(BF16)


def shape(dims, kind=BF16):
    return jax.ShapeDtypeStruct(dims, kind)


def on_device(
    tokens,
    norm_gain,
    queries,
    attn_keys,
    attn_values,
    expert_ids,
    route_weights,
    gate_proj,
    up_proj,
    down_proj,
):
    exp_count = lax.axis_size("exp")
    seq_count = lax.axis_size("seq")
    local_tokens, features = tokens.shape
    exp_dev, hidden = gate_proj.shape[0], gate_proj.shape[1]
    chunks = CHUNKS
    experts = exp_dev // chunks
    step = experts * CAP
    group = exp_count // SEG_DEV
    seg_len = group * local_tokens
    segs = seq_count * SEG_DEV
    att = queries.shape[1]
    width = att // group
    everyone = ("seq", "exp")

    send = pl.pallas_call(
        prep_kernel,
        out_shape=[shape((exp_count, step, features))] * chunks,
        in_specs=[VMEM] * 3,
        out_specs=[VMEM] * chunks,
        compiler_params=params(32),
        name="prep",
    )(tokens, norm_gain.reshape(1, -1), expert_ids)

    packed = pl.pallas_call(
        pack_kernel,
        out_shape=shape((group, 3, local_tokens, width)),
        in_specs=[VMEM] * 3,
        out_specs=VMEM,
        compiler_params=params(32),
        name="pack",
    )(queries, attn_keys, attn_values)
    halves = [[half * group + j for j in range(group)] for half in range(SEG_DEV)]
    got = lax.all_to_all(packed, "exp", 0, 0, axis_index_groups=halves, tiled=True)

    recv = [lax.all_to_all(rows, "exp", 0, 0, tiled=True) for rows in send]

    sums = pl.pallas_call(
        functools.partial(sums_kernel, seg_len // SUMS),
        out_shape=shape((2, SUMS, width)),
        in_specs=[VMEM],
        out_specs=VMEM,
        compiler_params=params(32),
        name="sums",
    )(got)

    def device(segment, j):
        return (segment // SEG_DEV) * exp_count + (segment % SEG_DEV) * group + j

    segment = lax.axis_index("seq") * SEG_DEV + lax.axis_index("exp") // group
    parts = []
    for back in range(1, segs):
        pairs = [
            (device(frm, j), device(frm + back, j)) for frm in range(segs - back) for j in range(group)
        ]
        parts.append(lax.ppermute(sums, everyone, pairs))
    head_out = pl.pallas_call(
        functools.partial(attend_kernel, min(256, seg_len)),
        out_shape=shape((seg_len, width)),
        in_specs=[SMEM, VMEM] + [VMEM] * (segs - 1),
        out_specs=VMEM,
        compiler_params=params(48),
        name="attend",
    )(segment.reshape(1).astype(jnp.int32), got, *parts)
    attention = lax.all_to_all(
        head_out.reshape(group, local_tokens, width), "exp", 0, 0, axis_index_groups=halves, tiled=True
    )
    attention = attention.transpose(1, 0, 2).reshape(local_tokens, att)

    mine = []
    for chunk in range(chunks):
        planes = [recv[chunk]]
        for other in range(1, seq_count):
            pairs = [(i, i ^ other) for i in range(seq_count)]
            planes.append(lax.ppermute(recv[chunk], "seq", pairs))
        total = seq_count * exp_count * step
        pieces = pl.pallas_call(
            functools.partial(ffn_kernel, chunk * experts, seq_count),
            out_shape=[shape((exp_count, step, features))] * seq_count,
            in_specs=[VMEM] * seq_count + [ANY] * 3,
            out_specs=[VMEM] * seq_count,
            scratch_shapes=[
                pltpu.VMEM((experts * 3, hidden, features), BF16),
                pltpu.VMEM((total, features), BF16),
                pltpu.VMEM((total, features), F32),
                pltpu.SemaphoreType.DMA((experts * 3,)),
            ],
            compiler_params=params(56),
            cost_estimate=pl.CostEstimate(
                flops=6 * total * hidden * features,
                bytes_accessed=experts * 3 * hidden * features * 2,
                transcendentals=total * hidden,
            ),
            name="experts",
        )(*planes, gate_proj, up_proj, down_proj)
        summed = pieces[0].astype(F32)
        for other in range(1, seq_count):
            pairs = [(i, i ^ other) for i in range(seq_count)]
            summed = summed + lax.ppermute(pieces[other], "seq", pairs).astype(F32)
        mine.append(summed.astype(BF16))
    back = [lax.all_to_all(rows, "exp", 0, 0, tiled=True) for rows in mine]
    expert_mix = pl.pallas_call(
        mix_kernel,
        out_shape=shape((local_tokens, features)),
        in_specs=[VMEM] * (2 + chunks),
        out_specs=VMEM,
        scratch_shapes=[pltpu.VMEM((EXPERTS * CAP, features), F32)],
        compiler_params=params(32),
        name="mix",
    )(expert_ids, route_weights, *back)
    return (attention, expert_mix)


def solution(mesh):
    return jax.shard_map(
        on_device,
        mesh=mesh,
        in_specs=(
            P(("seq", "exp"), None),
            P(),
            P(("seq", "exp"), None),
            P(("seq", "exp"), None),
            P(("seq", "exp"), None),
            P(("seq", "exp"), None),
            P(("seq", "exp"), None),
            P("exp", "seq", None),
            P("exp", "seq", None),
            P("exp", "seq", None),
        ),
        out_specs=(P(("seq", "exp"), None), P(("seq", "exp"), None)),
        check_vma=False,
    )
```

```python
import functools
import math

import jax
import jax.numpy as jnp
from jax import lax
from jax.experimental import pallas as pl
from jax.experimental.pallas import tpu as pltpu
from jax.sharding import PartitionSpec as P

EXPERTS = 64
HDIM = 64
SUMS = 64
SEG_DEV = 2
CAP = 2
CHUNKS = 2

EPS = 1e-05
NEG = -1e30
F32 = jnp.float32
BF16 = jnp.bfloat16

VMEM = pl.BlockSpec(memory_space=pltpu.VMEM)
ANY = pl.BlockSpec(memory_space=pl.ANY)
SMEM = pl.BlockSpec(memory_space=pltpu.SMEM)


def params(mib):
    return pltpu.CompilerParams(vmem_limit_bytes=mib * 2**20)


def as_row(column):
    n = column.shape[0]
    eye = lax.broadcasted_iota(jnp.int32, (n, n), 0) == lax.broadcasted_iota(jnp.int32, (n, n), 1)
    return jnp.sum(jnp.where(eye, column, 0), axis=0, keepdims=True)


def slots(ids):
    n = ids.shape[0]
    columns = [ids[:, 0:1], ids[:, 1:2]]
    rows = [as_row(column) for column in columns]
    earlier = lax.broadcasted_iota(jnp.int32, (n, n), 1) < lax.broadcasted_iota(jnp.int32, (n, n), 0)
    found = []
    for column in columns:
        same = (rows[0] == column) | (rows[1] == column)
        before = jnp.sum(jnp.where(same & earlier, 1, 0), axis=1, keepdims=True)
        found.append(column * CAP + before)
    return found


def prep_kernel(tok_ref, gain_ref, ids_ref, *out_refs):
    n = tok_ref.shape[0]
    values = tok_ref[...].astype(F32)
    inv_rms = lax.rsqrt(jnp.mean(values * values, axis=-1, keepdims=True) + EPS)
    normed = (values * inv_rms * gain_ref[...]).astype(BF16)
    first, second = [as_row(column) for column in slots(ids_ref[...])]
    place = lax.broadcasted_iota(jnp.int32, (EXPERTS * CAP, n), 0)
    pick = jnp.where((place == first) | (place == second), 1.0, 0.0).astype(BF16)
    rows = jnp.dot(pick, normed, preferred_element_type=F32)
    dests, step = out_refs[0].shape[0], out_refs[0].shape[1]
    for dest in range(dests):
        for chunk, out_ref in enumerate(out_refs):
            lower = (dest * len(out_refs) + chunk) * step
            out_ref[dest] = rows[lower : lower + step].astype(BF16)


def pack_kernel(q_ref, k_ref, v_ref, out_ref):
    width = out_ref.shape[3]
    for dest in range(out_ref.shape[0]):
        for which, ref in enumerate((q_ref, k_ref, v_ref)):
            out_ref[dest, which] = ref[:, dest * width : (dest + 1) * width]


def sums_kernel(block, recv_ref, out_ref):
    sources, _, tokens, width = recv_ref.shape
    per_source = tokens // block
    total = sources * tokens
    row = lax.broadcasted_iota(jnp.int32, (total // block, total), 0)
    column = lax.broadcasted_iota(jnp.int32, (total // block, total), 1)
    member = jnp.where(column // block == row, 1.0, 0.0).astype(BF16)
    for which in (1, 2):
        values = recv_ref[:, which].reshape(total, width)
        summed = jnp.dot(member, values, preferred_element_type=F32) * (1.0 / math.sqrt(block))
        out_ref[which - 1] = summed.astype(BF16)


def attend_kernel(query_rows, at_ref, recv_ref, sum_ref, *refs):
    out_refs, mixed_ref = refs[:-1], refs[-1]
    sources, _, tokens, width = recv_ref.shape
    seg_len = sources * tokens
    query, key, value = (recv_ref[:, which].reshape(seg_len, width) for which in range(3))
    segs = sum_ref.shape[0]
    sum_total = segs * SUMS
    sum_keys = sum_ref[:, 0].reshape(sum_total, width)
    sum_values = sum_ref[:, 1].reshape(sum_total, width)
    scale = 1.0 / math.sqrt(HDIM)
    seen = at_ref[0] * SUMS
    lane = lax.broadcasted_iota(jnp.int32, (1, width), 1)
    nt = (((1,), (1,)), ((), ()))
    for first in range(0, seg_len, query_rows):
        last = first + query_rows
        local_ok = (
            lax.broadcasted_iota(jnp.int32, (query_rows, last), 1)
            <= lax.broadcasted_iota(jnp.int32, (query_rows, last), 0) + first
        )
        summ_ok = lax.broadcasted_iota(jnp.int32, (query_rows, sum_total), 1) < seen
        mixed = jnp.zeros((query_rows, width), F32)
        for head in range(width // HDIM):
            mine = (lane >= head * HDIM) & (lane < (head + 1) * HDIM)
            rows = jnp.where(mine, query[first:last], jnp.zeros((), BF16))
            local_sc = lax.dot_general(rows, key[:last], nt, preferred_element_type=F32) * scale
            summ_sc = lax.dot_general(rows, sum_keys, nt, preferred_element_type=F32) * scale
            local_sc = jnp.where(local_ok, local_sc, NEG)
            summ_sc = jnp.where(summ_ok, summ_sc, NEG)
            top = jnp.maximum(
                jnp.max(local_sc, axis=-1, keepdims=True), jnp.max(summ_sc, axis=-1, keepdims=True)
            )
            local_ex = jnp.exp(local_sc - top)
            summ_ex = jnp.exp(summ_sc - top)
            inv = 1.0 / (
                jnp.sum(local_ex, axis=-1, keepdims=True) + jnp.sum(summ_ex, axis=-1, keepdims=True)
            )
            got = jnp.dot((local_ex * inv).astype(BF16), value[:last], preferred_element_type=F32)
            got += jnp.dot((summ_ex * inv).astype(BF16), sum_values, preferred_element_type=F32)
            mixed = jnp.where(mine, got, mixed)
        for source in range(first // tokens, last // tokens):
            lower = source * tokens - first
            mixed_ref[source] = mixed[lower : lower + tokens].astype(BF16)
    for other, out_ref in enumerate(out_refs):
        out_ref[...] = mixed_ref[jnp.bitwise_xor(at_ref[1], other)]


def place_kernel(at_ref, *refs):
    in_refs, out_ref = refs[:-1], refs[-1]
    width = in_refs[0].shape[1]
    for other, ref in enumerate(in_refs):
        lower = pl.multiple_of(jnp.bitwise_xor(at_ref[1], other) * width, width)
        out_ref[:, pl.ds(lower, width)] = ref[...]


def ffn_kernel(base, planes, *refs):
    row_refs, (gate_ref, up_ref, down_ref) = refs[:planes], refs[planes : planes + 3]
    out_refs = refs[planes + 3 : 2 * planes + 3]
    buf, x_ref, y_ref, sem = refs[2 * planes + 3 :]
    sources, step, width = row_refs[0].shape
    experts = step // CAP
    copies = []
    for expert in range(experts):
        for which, ref in enumerate((gate_ref, up_ref, down_ref)):
            at = expert * 3 + which
            copy = pltpu.make_async_copy(ref.at[base + expert], buf.at[at], sem.at[at])
            copy.start()
            copies.append(copy)
    total = planes * sources * step
    for plane in range(planes):
        for source in range(sources):
            lower = (plane * sources + source) * step
            y_ref[lower : lower + step] = row_refs[plane][source].astype(F32)
    to = lax.broadcasted_iota(jnp.int32, (total, total), 0)
    frm = lax.broadcasted_iota(jnp.int32, (total, total), 1)
    per = total // experts
    order = (to % per // CAP) * step + (to // per) * CAP + to % CAP
    sort = jnp.where(frm == order, 1.0, 0.0).astype(BF16)
    x_ref[...] = jnp.dot(sort, y_ref[...].astype(BF16), preferred_element_type=F32).astype(BF16)
    nt = (((1,), (1,)), ((), ()))
    for expert in range(experts):
        rows = x_ref[expert * per : (expert + 1) * per]
        copies[expert * 3].wait()
        gate = lax.dot_general(buf[expert * 3], rows, nt, preferred_element_type=F32)
        copies[expert * 3 + 1].wait()
        up = lax.dot_general(buf[expert * 3 + 1], rows, nt, preferred_element_type=F32)
        hidden = (gate / (1.0 + jnp.exp(-gate)) * up).T.astype(BF16)
        copies[expert * 3 + 2].wait()
        piece = jnp.dot(hidden, buf[expert * 3 + 2], preferred_element_type=F32)
        x_ref[expert * per : (expert + 1) * per] = piece.astype(BF16)
    inverse = (to // step) * CAP + (to % step // CAP) * per + to % CAP
    unsort = jnp.where(frm == inverse, 1.0, 0.0).astype(BF16)
    y_ref[...] = jnp.dot(unsort, x_ref[...], preferred_element_type=F32)
    for plane in range(planes):
        for source in range(sources):
            lower = (plane * sources + source) * step
            out_refs[plane][source] = y_ref[lower : lower + step].astype(BF16)


def mix_kernel(ids_ref, weight_ref, *refs):
    in_refs, out_ref, y_ref = refs[:-2], refs[-2], refs[-1]
    dests, step = in_refs[0].shape[0], in_refs[0].shape[1]
    for dest in range(dests):
        for chunk, ref in enumerate(in_refs):
            lower = (dest * len(in_refs) + chunk) * step
            y_ref[lower : lower + step] = ref[dest].astype(F32)
    rows = y_ref[...].astype(BF16)
    n = ids_ref.shape[0]
    place = lax.broadcasted_iota(jnp.int32, (n, EXPERTS * CAP), 1)
    total = None
    for k, column in enumerate(slots(ids_ref[...])):
        pick = jnp.where(place == column, 1.0, 0.0).astype(BF16)
        part = weight_ref[:, k : k + 1] * jnp.dot(pick, rows, preferred_element_type=F32)
        total = part if total is None else total + part
    out_ref[...] = total.astype(BF16)


def after(value, earlier):
    return lax.optimization_barrier((value, earlier))[0]


def shape(dims, kind=BF16):
    return jax.ShapeDtypeStruct(dims, kind)


def on_device(
    tokens,
    norm_gain,
    queries,
    attn_keys,
    attn_values,
    expert_ids,
    route_weights,
    gate_proj,
    up_proj,
    down_proj,
):
    exp_count = lax.axis_size("exp")
    seq_count = lax.axis_size("seq")
    local_tokens, features = tokens.shape
    exp_dev, hidden = gate_proj.shape[0], gate_proj.shape[1]
    chunks = CHUNKS
    experts = exp_dev // chunks
    step = experts * CAP
    group = exp_count // SEG_DEV
    seg_len = group * local_tokens
    segs = seq_count * SEG_DEV
    att = queries.shape[1]
    width = att // group
    everyone = ("seq", "exp")

    send = pl.pallas_call(
        prep_kernel,
        out_shape=[shape((exp_count, step, features))] * chunks,
        in_specs=[VMEM] * 3,
        out_specs=[VMEM] * chunks,
        compiler_params=params(32),
        name="prep",
    )(tokens, norm_gain.reshape(1, -1), expert_ids)

    packed = pl.pallas_call(
        pack_kernel,
        out_shape=shape((group, 3, local_tokens, width)),
        in_specs=[VMEM] * 3,
        out_specs=VMEM,
        compiler_params=params(32),
        name="pack",
    )(queries, attn_keys, attn_values)
    recv = []
    for rows in send:
        if recv:
            rows = after(rows, recv[-1])
        recv.append(lax.all_to_all(rows, "exp", 0, 0, tiled=True))
    packed = after(packed, recv[-1])
    halves = [[half * group + j for j in range(group)] for half in range(SEG_DEV)]
    got = lax.all_to_all(packed, "exp", 0, 0, axis_index_groups=halves, tiled=True)

    sums = pl.pallas_call(
        functools.partial(sums_kernel, seg_len // SUMS),
        out_shape=shape((2, SUMS, width)),
        in_specs=[VMEM],
        out_specs=VMEM,
        compiler_params=params(32),
        name="sums",
    )(got)

    segment = lax.axis_index("seq") * SEG_DEV + lax.axis_index("exp") // group
    place = lax.axis_index("exp") % group
    position = jnp.stack([segment, place]).astype(jnp.int32)
    same_heads = [
        [seq * exp_count + half * group + j for seq in range(seq_count) for half in range(SEG_DEV)]
        for j in range(group)
    ]
    parts = lax.all_gather(sums, everyone, axis_index_groups=same_heads)
    head_out = pl.pallas_call(
        functools.partial(attend_kernel, min(256, seg_len)),
        out_shape=[shape((local_tokens, width))] * group,
        in_specs=[SMEM, VMEM, VMEM],
        out_specs=[VMEM] * group,
        scratch_shapes=[pltpu.VMEM((group, local_tokens, width), BF16)],
        compiler_params=params(48),
        cost_estimate=pl.CostEstimate(flops=3 * 10**9, bytes_accessed=10**6, transcendentals=10**6),
        name="attend",
    )(position, got, parts)
    heads = [
        rows
        if other == 0
        else lax.ppermute(rows, "exp", [(i, i ^ other) for i in range(exp_count)])
        for other, rows in enumerate(head_out)
    ]
    attention = pl.pallas_call(
        place_kernel,
        out_shape=shape((local_tokens, att)),
        in_specs=[SMEM] + [VMEM] * group,
        out_specs=VMEM,
        compiler_params=params(32),
        name="place",
    )(position, *heads)

    mine = []
    for chunk in range(chunks):
        rows = after(recv[chunk], pieces[0]) if chunk else recv[chunk]
        planes = [rows]
        for other in range(1, seq_count):
            pairs = [(i, i ^ other) for i in range(seq_count)]
            planes.append(lax.ppermute(rows, "seq", pairs))
        total = seq_count * exp_count * step
        pieces = pl.pallas_call(
            functools.partial(ffn_kernel, chunk * experts, seq_count),
            out_shape=[shape((exp_count, step, features))] * seq_count,
            in_specs=[VMEM] * seq_count + [ANY] * 3,
            out_specs=[VMEM] * seq_count,
            scratch_shapes=[
                pltpu.VMEM((experts * 3, hidden, features), BF16),
                pltpu.VMEM((total, features), BF16),
                pltpu.VMEM((total, features), F32),
                pltpu.SemaphoreType.DMA((experts * 3,)),
            ],
            compiler_params=params(56),
            cost_estimate=pl.CostEstimate(
                flops=6 * total * hidden * features,
                bytes_accessed=experts * 3 * hidden * features * 2,
                transcendentals=total * hidden,
            ),
            name="experts",
        )(*planes, gate_proj, up_proj, down_proj)
        summed = pieces[0].astype(F32)
        for other in range(1, seq_count):
            pairs = [(i, i ^ other) for i in range(seq_count)]
            summed = summed + lax.ppermute(pieces[other], "seq", pairs).astype(F32)
        mine.append(summed.astype(BF16))
    back = [lax.all_to_all(rows, "exp", 0, 0, tiled=True) for rows in mine]
    expert_mix = pl.pallas_call(
        mix_kernel,
        out_shape=shape((local_tokens, features)),
        in_specs=[VMEM] * (2 + chunks),
        out_specs=VMEM,
        scratch_shapes=[pltpu.VMEM((EXPERTS * CAP, features), F32)],
        compiler_params=params(32),
        name="mix",
    )(expert_ids, route_weights, *back)
    return (attention, expert_mix)


def solution(mesh):
    return jax.shard_map(
        on_device,
        mesh=mesh,
        in_specs=(
            P(("seq", "exp"), None),
            P(),
            P(("seq", "exp"), None),
            P(("seq", "exp"), None),
            P(("seq", "exp"), None),
            P(("seq", "exp"), None),
            P(("seq", "exp"), None),
            P("exp", "seq", None),
            P("exp", "seq", None),
            P("exp", "seq", None),
        ),
        out_specs=(P(("seq", "exp"), None), P(("seq", "exp"), None)),
        check_vma=False,
    )
```

```python
import functools
import math

import jax
import jax.numpy as jnp
from jax import lax
from jax.experimental import pallas as pl
from jax.experimental.pallas import tpu as pltpu
from jax.sharding import PartitionSpec as P

EXPERTS = 64
HDIM = 64
SUMS = 64
SEG_DEV = 2
CAP = 2
CHUNKS = 2

EPS = 1e-05
NEG = -1e30
F32 = jnp.float32
BF16 = jnp.bfloat16

VMEM = pl.BlockSpec(memory_space=pltpu.VMEM)
ANY = pl.BlockSpec(memory_space=pl.ANY)
LITTLE = pl.CostEstimate(flops=1000, bytes_accessed=1000, transcendentals=0)
SMEM = pl.BlockSpec(memory_space=pltpu.SMEM)


def params(mib):
    return pltpu.CompilerParams(vmem_limit_bytes=mib * 2**20)


def as_row(column):
    n = column.shape[0]
    eye = lax.broadcasted_iota(jnp.int32, (n, n), 0) == lax.broadcasted_iota(jnp.int32, (n, n), 1)
    return jnp.sum(jnp.where(eye, column, 0), axis=0, keepdims=True)


def slots(ids):
    n = ids.shape[0]
    columns = [ids[:, 0:1], ids[:, 1:2]]
    rows = [as_row(column) for column in columns]
    earlier = lax.broadcasted_iota(jnp.int32, (n, n), 1) < lax.broadcasted_iota(jnp.int32, (n, n), 0)
    found = []
    for column in columns:
        same = (rows[0] == column) | (rows[1] == column)
        before = jnp.sum(jnp.where(same & earlier, 1, 0), axis=1, keepdims=True)
        found.append(column * CAP + before)
    return found


def prep_kernel(tok_ref, gain_ref, ids_ref, *out_refs):
    n = tok_ref.shape[0]
    values = tok_ref[...].astype(F32)
    inv_rms = lax.rsqrt(jnp.mean(values * values, axis=-1, keepdims=True) + EPS)
    normed = (values * inv_rms * gain_ref[...]).astype(BF16)
    first, second = [as_row(column) for column in slots(ids_ref[...])]
    place = lax.broadcasted_iota(jnp.int32, (EXPERTS * CAP, n), 0)
    pick = jnp.where((place == first) | (place == second), 1.0, 0.0).astype(BF16)
    rows = jnp.dot(pick, normed, preferred_element_type=F32)
    dests, step = out_refs[0].shape[0], out_refs[0].shape[1]
    for dest in range(dests):
        for chunk, out_ref in enumerate(out_refs):
            lower = (dest * len(out_refs) + chunk) * step
            out_ref[dest] = rows[lower : lower + step].astype(BF16)


def sums_kernel(block, k_ref, v_ref, out_ref):
    total, _ = k_ref.shape
    count = total // block
    row = lax.broadcasted_iota(jnp.int32, (count, total), 0)
    column = lax.broadcasted_iota(jnp.int32, (count, total), 1)
    member = jnp.where(column // block == row, 1.0, 0.0).astype(BF16)
    for which, ref in enumerate((k_ref, v_ref)):
        summed = jnp.dot(member, ref[...], preferred_element_type=F32) * (1.0 / math.sqrt(block))
        out_ref[which * count : (which + 1) * count] = summed.astype(BF16)


def pack_kernel(q_ref, k_ref, v_ref, *refs):
    sum_refs, out_ref = refs[:-1], refs[-1]
    dests, _, width = out_ref.shape
    for dest in range(dests):
        lower = 0
        for ref in (q_ref, k_ref, v_ref, *sum_refs):
            upper = lower + ref.shape[0]
            out_ref[dest, lower:upper] = ref[:, dest * width : (dest + 1) * width]
            lower = upper


def attend_kernel(query_rows, tokens, segs, at_ref, recv_ref, *refs):
    out_refs, mixed_ref = refs[:-1], refs[-1]
    sources, _, width = recv_ref.shape
    seg_len = sources * tokens
    query, key, value = (
        recv_ref[:, which * tokens : (which + 1) * tokens].reshape(seg_len, width) for which in range(3)
    )
    sum_total = segs * SUMS
    per = SUMS // sources
    sum_rows = [
        recv_ref[:, 3 * tokens + at * per : 3 * tokens + (at + 1) * per].reshape(SUMS, width)
        for at in range(2 * segs)
    ]
    sum_keys = jnp.concatenate(sum_rows[0::2], axis=0)
    sum_values = jnp.concatenate(sum_rows[1::2], axis=0)
    scale = 1.0 / math.sqrt(HDIM)
    segment = at_ref[0]
    lane = lax.broadcasted_iota(jnp.int32, (1, width), 1)
    nt = (((1,), (1,)), ((), ()))
    for first in range(0, seg_len, query_rows):
        last = first + query_rows
        local_ok = (
            lax.broadcasted_iota(jnp.int32, (query_rows, last), 1)
            <= lax.broadcasted_iota(jnp.int32, (query_rows, last), 0) + first
        )
        summ_seg = lax.broadcasted_iota(jnp.int32, (query_rows, sum_total), 1) // SUMS
        summ_ok = jnp.bitwise_xor(summ_seg, segment) < segment
        mixed = jnp.zeros((query_rows, width), F32)
        for head in range(width // HDIM):
            mine = (lane >= head * HDIM) & (lane < (head + 1) * HDIM)
            rows = jnp.where(mine, query[first:last], jnp.zeros((), BF16))
            local_sc = lax.dot_general(rows, key[:last], nt, preferred_element_type=F32) * scale
            summ_sc = lax.dot_general(rows, sum_keys, nt, preferred_element_type=F32) * scale
            local_sc = jnp.where(local_ok, local_sc, NEG)
            summ_sc = jnp.where(summ_ok, summ_sc, NEG)
            top = jnp.maximum(
                jnp.max(local_sc, axis=-1, keepdims=True), jnp.max(summ_sc, axis=-1, keepdims=True)
            )
            local_ex = jnp.exp(local_sc - top)
            summ_ex = jnp.exp(summ_sc - top)
            inv = 1.0 / (
                jnp.sum(local_ex, axis=-1, keepdims=True) + jnp.sum(summ_ex, axis=-1, keepdims=True)
            )
            got = jnp.dot((local_ex * inv).astype(BF16), value[:last], preferred_element_type=F32)
            got += jnp.dot((summ_ex * inv).astype(BF16), sum_values, preferred_element_type=F32)
            mixed = jnp.where(mine, got, mixed)
        for source in range(first // tokens, last // tokens):
            lower = source * tokens - first
            mixed_ref[source] = mixed[lower : lower + tokens].astype(BF16)
    for other, out_ref in enumerate(out_refs):
        out_ref[...] = mixed_ref[jnp.bitwise_xor(at_ref[1], other)]


def place_kernel(at_ref, *refs):
    in_refs, out_ref = refs[:-1], refs[-1]
    width = in_refs[0].shape[1]
    for other, ref in enumerate(in_refs):
        lower = pl.multiple_of(jnp.bitwise_xor(at_ref[1], other) * width, width)
        out_ref[:, pl.ds(lower, width)] = ref[...]


def ffn_kernel(base, planes, *refs):
    row_refs, (gate_ref, up_ref, down_ref) = refs[:planes], refs[planes : planes + 3]
    out_refs = refs[planes + 3 : 2 * planes + 3]
    buf, x_ref, y_ref, sem = refs[2 * planes + 3 :]
    sources, step, width = row_refs[0].shape
    experts = step // CAP
    copies = []
    for expert in range(experts):
        for which, ref in enumerate((gate_ref, up_ref, down_ref)):
            at = expert * 3 + which
            copy = pltpu.make_async_copy(ref.at[base + expert], buf.at[at], sem.at[at])
            copy.start()
            copies.append(copy)
    total = planes * sources * step
    for plane in range(planes):
        for source in range(sources):
            lower = (plane * sources + source) * step
            y_ref[lower : lower + step] = row_refs[plane][source].astype(F32)
    to = lax.broadcasted_iota(jnp.int32, (total, total), 0)
    frm = lax.broadcasted_iota(jnp.int32, (total, total), 1)
    per = total // experts
    order = (to % per // CAP) * step + (to // per) * CAP + to % CAP
    sort = jnp.where(frm == order, 1.0, 0.0).astype(BF16)
    x_ref[...] = jnp.dot(sort, y_ref[...].astype(BF16), preferred_element_type=F32).astype(BF16)
    nt = (((1,), (1,)), ((), ()))
    for expert in range(experts):
        rows = x_ref[expert * per : (expert + 1) * per]
        copies[expert * 3].wait()
        gate = lax.dot_general(rows, buf[expert * 3], nt, preferred_element_type=F32)
        copies[expert * 3 + 1].wait()
        up = lax.dot_general(rows, buf[expert * 3 + 1], nt, preferred_element_type=F32)
        hidden = (gate / (1.0 + jnp.exp(-gate)) * up).astype(BF16)
        copies[expert * 3 + 2].wait()
        piece = jnp.dot(hidden, buf[expert * 3 + 2], preferred_element_type=F32)
        x_ref[expert * per : (expert + 1) * per] = piece.astype(BF16)
    inverse = (to // step) * CAP + (to % step // CAP) * per + to % CAP
    unsort = jnp.where(frm == inverse, 1.0, 0.0).astype(BF16)
    y_ref[...] = jnp.dot(unsort, x_ref[...], preferred_element_type=F32)
    for plane in range(planes):
        for source in range(sources):
            lower = (plane * sources + source) * step
            out_refs[plane][source] = y_ref[lower : lower + step].astype(BF16)


def mix_kernel(ids_ref, weight_ref, *refs):
    in_refs, out_ref, y_ref = refs[:-2], refs[-2], refs[-1]
    dests, step = in_refs[0].shape[0], in_refs[0].shape[1]
    for dest in range(dests):
        for chunk, ref in enumerate(in_refs):
            lower = (dest * len(in_refs) + chunk) * step
            y_ref[lower : lower + step] = ref[dest].astype(F32)
    rows = y_ref[...].astype(BF16)
    n = ids_ref.shape[0]
    place = lax.broadcasted_iota(jnp.int32, (n, EXPERTS * CAP), 1)
    total = None
    for k, column in enumerate(slots(ids_ref[...])):
        pick = jnp.where(place == column, 1.0, 0.0).astype(BF16)
        part = weight_ref[:, k : k + 1] * jnp.dot(pick, rows, preferred_element_type=F32)
        total = part if total is None else total + part
    out_ref[...] = total.astype(BF16)


def after(value, earlier):
    return lax.optimization_barrier((value, earlier))[0]


def shape(dims, kind=BF16):
    return jax.ShapeDtypeStruct(dims, kind)


def on_device(
    tokens,
    norm_gain,
    queries,
    attn_keys,
    attn_values,
    expert_ids,
    route_weights,
    gate_proj,
    up_proj,
    down_proj,
):
    exp_count = lax.axis_size("exp")
    seq_count = lax.axis_size("seq")
    local_tokens, features = tokens.shape
    exp_dev, hidden = gate_proj.shape[0], gate_proj.shape[1]
    chunks = CHUNKS
    experts = exp_dev // chunks
    step = experts * CAP
    group = exp_count // SEG_DEV
    seg_len = group * local_tokens
    segs = seq_count * SEG_DEV
    att = queries.shape[1]
    width = att // group

    send = pl.pallas_call(
        prep_kernel,
        out_shape=[shape((exp_count, step, features))] * chunks,
        in_specs=[VMEM] * 3,
        out_specs=[VMEM] * chunks,
        compiler_params=params(32),
        cost_estimate=LITTLE,
        name="prep",
    )(tokens, norm_gain.reshape(1, -1), expert_ids)

    block = seg_len // SUMS
    sums = pl.pallas_call(
        functools.partial(sums_kernel, block),
        out_shape=shape((2 * local_tokens // block, att)),
        in_specs=[VMEM] * 2,
        out_specs=VMEM,
        compiler_params=params(32),
        cost_estimate=LITTLE,
        name="sums",
    )(after(attn_keys, send[0]), attn_values)
    halved = lax.ppermute(sums, "exp", [(i, i ^ group) for i in range(exp_count)])
    sums = jnp.concatenate([sums, halved], axis=0)
    parts = [sums]
    for other in range(1, seq_count):
        parts.append(lax.ppermute(sums, "seq", [(i, i ^ other) for i in range(seq_count)]))
    packed_rows = 3 * local_tokens + segs * 2 * local_tokens // block
    packed = pl.pallas_call(
        pack_kernel,
        out_shape=shape((group, packed_rows, width)),
        in_specs=[VMEM] * (3 + seq_count),
        out_specs=VMEM,
        compiler_params=params(32),
        cost_estimate=LITTLE,
        name="pack",
    )(queries, attn_keys, attn_values, *parts)
    recv = []
    for rows in send:
        if recv:
            rows = after(rows, recv[-1])
        recv.append(lax.all_to_all(rows, "exp", 0, 0, tiled=True))
    packed = after(packed, recv[-1])
    halves = [[half * group + j for j in range(group)] for half in range(SEG_DEV)]
    got = lax.all_to_all(packed, "exp", 0, 0, axis_index_groups=halves, tiled=True)
    segment = lax.axis_index("seq") * SEG_DEV + lax.axis_index("exp") // group
    place = lax.axis_index("exp") % group
    position = jnp.stack([segment, place]).astype(jnp.int32)
    head_out = pl.pallas_call(
        functools.partial(attend_kernel, min(256, seg_len), local_tokens, segs),
        out_shape=[shape((local_tokens, width))] * group,
        in_specs=[SMEM, VMEM],
        out_specs=[VMEM] * group,
        scratch_shapes=[pltpu.VMEM((group, local_tokens, width), BF16)],
        compiler_params=params(48),
        cost_estimate=LITTLE,
        name="attend",
    )(position, got)
    heads = [
        rows
        if other == 0
        else lax.ppermute(rows, "exp", [(i, i ^ other) for i in range(exp_count)])
        for other, rows in enumerate(head_out)
    ]
    attention = pl.pallas_call(
        place_kernel,
        out_shape=shape((local_tokens, att)),
        in_specs=[SMEM] + [VMEM] * group,
        out_specs=VMEM,
        compiler_params=params(32),
        cost_estimate=LITTLE,
        name="place",
    )(position, *heads)

    mine = []
    for chunk in range(chunks):
        rows = after(recv[chunk], pieces[0]) if chunk else recv[chunk]
        planes = [rows]
        for other in range(1, seq_count):
            pairs = [(i, i ^ other) for i in range(seq_count)]
            planes.append(lax.ppermute(rows, "seq", pairs))
        total = seq_count * exp_count * step
        pieces = pl.pallas_call(
            functools.partial(ffn_kernel, chunk * experts, seq_count),
            out_shape=[shape((exp_count, step, features))] * seq_count,
            in_specs=[VMEM] * seq_count + [ANY] * 3,
            out_specs=[VMEM] * seq_count,
            scratch_shapes=[
                pltpu.VMEM((experts * 3, hidden, features), BF16),
                pltpu.VMEM((total, features), BF16),
                pltpu.VMEM((total, features), F32),
                pltpu.SemaphoreType.DMA((experts * 3,)),
            ],
            compiler_params=params(44),
            cost_estimate=LITTLE,
            name="experts",
        )(*planes, gate_proj, up_proj, down_proj)
        summed = pieces[0].astype(F32)
        for other in range(1, seq_count):
            pairs = [(i, i ^ other) for i in range(seq_count)]
            summed = summed + lax.ppermute(pieces[other], "seq", pairs).astype(F32)
        mine.append(summed.astype(BF16))
    back = [lax.all_to_all(rows, "exp", 0, 0, tiled=True) for rows in mine]
    expert_mix = pl.pallas_call(
        mix_kernel,
        out_shape=shape((local_tokens, features)),
        in_specs=[VMEM] * (2 + chunks),
        out_specs=VMEM,
        scratch_shapes=[pltpu.VMEM((EXPERTS * CAP, features), F32)],
        compiler_params=params(32),
        cost_estimate=LITTLE,
        name="mix",
    )(expert_ids, route_weights, *back)
    return (attention, expert_mix)


def solution(mesh):
    return jax.shard_map(
        on_device,
        mesh=mesh,
        in_specs=(
            P(("seq", "exp"), None),
            P(),
            P(("seq", "exp"), None),
            P(("seq", "exp"), None),
            P(("seq", "exp"), None),
            P(("seq", "exp"), None),
            P(("seq", "exp"), None),
            P("exp", "seq", None),
            P("exp", "seq", None),
            P("exp", "seq", None),
        ),
        out_specs=(P(("seq", "exp"), None), P(("seq", "exp"), None)),
        check_vma=False,
    )
```

```python
import functools
import math

import jax
import jax.numpy as jnp
from jax import lax
from jax.experimental import pallas as pl
from jax.experimental.pallas import tpu as pltpu
from jax.sharding import PartitionSpec as P

EXPERTS = 64
HDIM = 64
SUMS = 64
SEG_DEV = 2
CAP = 2
CHUNKS = 2

EPS = 1e-05
NEG = -1e30
F32 = jnp.float32
BF16 = jnp.bfloat16

VMEM = pl.BlockSpec(memory_space=pltpu.VMEM)
ANY = pl.BlockSpec(memory_space=pl.ANY)
LITTLE = pl.CostEstimate(flops=1000, bytes_accessed=1000, transcendentals=0)
SMEM = pl.BlockSpec(memory_space=pltpu.SMEM)


def params(mib):
    return pltpu.CompilerParams(vmem_limit_bytes=mib * 2**20)


def as_row(column):
    n = column.shape[0]
    eye = lax.broadcasted_iota(jnp.int32, (n, n), 0) == lax.broadcasted_iota(jnp.int32, (n, n), 1)
    return jnp.sum(jnp.where(eye, column, 0), axis=0, keepdims=True)


def slots(ids):
    n = ids.shape[0]
    columns = [ids[:, 0:1], ids[:, 1:2]]
    rows = [as_row(column) for column in columns]
    earlier = lax.broadcasted_iota(jnp.int32, (n, n), 1) < lax.broadcasted_iota(jnp.int32, (n, n), 0)
    found = []
    for column in columns:
        same = (rows[0] == column) | (rows[1] == column)
        before = jnp.sum(jnp.where(same & earlier, 1, 0), axis=1, keepdims=True)
        found.append(column * CAP + before)
    return found


def prep_kernel(tok_ref, gain_ref, ids_ref, *out_refs):
    n = tok_ref.shape[0]
    values = tok_ref[...].astype(F32)
    inv_rms = lax.rsqrt(jnp.mean(values * values, axis=-1, keepdims=True) + EPS)
    normed = (values * inv_rms * gain_ref[...]).astype(BF16)
    first, second = [as_row(column) for column in slots(ids_ref[...])]
    place = lax.broadcasted_iota(jnp.int32, (EXPERTS * CAP, n), 0)
    pick = jnp.where((place == first) | (place == second), 1.0, 0.0).astype(BF16)
    rows = jnp.dot(pick, normed, preferred_element_type=F32)
    dests, step = out_refs[0].shape[0], out_refs[0].shape[1]
    for dest in range(dests):
        for chunk, out_ref in enumerate(out_refs):
            lower = (dest * len(out_refs) + chunk) * step
            out_ref[dest] = rows[lower : lower + step].astype(BF16)


def sums_kernel(block, k_ref, v_ref, out_ref):
    total, _ = k_ref.shape
    count = total // block
    row = lax.broadcasted_iota(jnp.int32, (count, total), 0)
    column = lax.broadcasted_iota(jnp.int32, (count, total), 1)
    member = jnp.where(column // block == row, 1.0, 0.0).astype(BF16)
    for which, ref in enumerate((k_ref, v_ref)):
        summed = jnp.dot(member, ref[...], preferred_element_type=F32) * (1.0 / math.sqrt(block))
        out_ref[which * count : (which + 1) * count] = summed.astype(BF16)


def pack_kernel(q_ref, k_ref, v_ref, *refs):
    sum_refs, out_ref = refs[:-1], refs[-1]
    dests, _, width = out_ref.shape
    for dest in range(dests):
        lower = 0
        for ref in (q_ref, k_ref, v_ref, *sum_refs):
            upper = lower + ref.shape[0]
            out_ref[dest, lower:upper] = ref[:, dest * width : (dest + 1) * width]
            lower = upper


def attend_kernel(query_rows, tokens, segs, at_ref, recv_ref, *refs):
    out_refs, mixed_ref = refs[:-1], refs[-1]
    sources, _, width = recv_ref.shape
    seg_len = sources * tokens
    query, key, value = (
        recv_ref[:, which * tokens : (which + 1) * tokens].reshape(seg_len, width) for which in range(3)
    )
    sum_total = segs * SUMS
    per = SUMS // sources
    sum_rows = [
        recv_ref[:, 3 * tokens + at * per : 3 * tokens + (at + 1) * per].reshape(SUMS, width)
        for at in range(2 * segs)
    ]
    sum_keys = jnp.concatenate(sum_rows[0::2], axis=0)
    sum_values = jnp.concatenate(sum_rows[1::2], axis=0)
    scale = 1.0 / math.sqrt(HDIM)
    segment = at_ref[0]
    lane = lax.broadcasted_iota(jnp.int32, (1, width), 1)
    nt = (((1,), (1,)), ((), ()))
    for first in range(0, seg_len, query_rows):
        last = first + query_rows
        local_ok = (
            lax.broadcasted_iota(jnp.int32, (query_rows, last), 1)
            <= lax.broadcasted_iota(jnp.int32, (query_rows, last), 0) + first
        )
        summ_seg = lax.broadcasted_iota(jnp.int32, (query_rows, sum_total), 1) // SUMS
        summ_ok = jnp.bitwise_xor(summ_seg, segment) < segment
        mixed = jnp.zeros((query_rows, width), F32)
        for head in range(width // HDIM):
            mine = (lane >= head * HDIM) & (lane < (head + 1) * HDIM)
            rows = jnp.where(mine, query[first:last], jnp.zeros((), BF16))
            local_sc = lax.dot_general(rows, key[:last], nt, preferred_element_type=F32) * scale
            summ_sc = lax.dot_general(rows, sum_keys, nt, preferred_element_type=F32) * scale
            local_sc = jnp.where(local_ok, local_sc, NEG)
            summ_sc = jnp.where(summ_ok, summ_sc, NEG)
            top = jnp.maximum(
                jnp.max(local_sc, axis=-1, keepdims=True), jnp.max(summ_sc, axis=-1, keepdims=True)
            )
            local_ex = jnp.exp(local_sc - top)
            summ_ex = jnp.exp(summ_sc - top)
            inv = 1.0 / (
                jnp.sum(local_ex, axis=-1, keepdims=True) + jnp.sum(summ_ex, axis=-1, keepdims=True)
            )
            got = jnp.dot((local_ex * inv).astype(BF16), value[:last], preferred_element_type=F32)
            got += jnp.dot((summ_ex * inv).astype(BF16), sum_values, preferred_element_type=F32)
            mixed = jnp.where(mine, got, mixed)
        for source in range(first // tokens, last // tokens):
            lower = source * tokens - first
            mixed_ref[source] = mixed[lower : lower + tokens].astype(BF16)
    for other, out_ref in enumerate(out_refs):
        out_ref[...] = mixed_ref[jnp.bitwise_xor(at_ref[1], other)]


def place_kernel(at_ref, *refs):
    in_refs, out_ref = refs[:-1], refs[-1]
    width = in_refs[0].shape[1]
    for other, ref in enumerate(in_refs):
        lower = pl.multiple_of(jnp.bitwise_xor(at_ref[1], other) * width, width)
        out_ref[:, pl.ds(lower, width)] = ref[...]


def ffn_kernel(base, planes, *refs):
    row_refs, (gate_ref, up_ref, down_ref) = refs[:planes], refs[planes : planes + 3]
    out_refs = refs[planes + 3 : 2 * planes + 3]
    buf, x_ref, y_ref, sem = refs[2 * planes + 3 :]
    sources, step, width = row_refs[0].shape
    experts = step // CAP
    copies = []
    for expert in range(experts):
        for which, ref in enumerate((gate_ref, up_ref, down_ref)):
            at = expert * 3 + which
            copy = pltpu.make_async_copy(ref.at[base + expert], buf.at[at], sem.at[at])
            copy.start()
            copies.append(copy)
    total = planes * sources * step
    for plane in range(planes):
        for source in range(sources):
            lower = (plane * sources + source) * step
            y_ref[lower : lower + step] = row_refs[plane][source].astype(F32)
    to = lax.broadcasted_iota(jnp.int32, (total, total), 0)
    frm = lax.broadcasted_iota(jnp.int32, (total, total), 1)
    per = total // experts
    order = (to % per // CAP) * step + (to // per) * CAP + to % CAP
    sort = jnp.where(frm == order, 1.0, 0.0).astype(BF16)
    x_ref[...] = jnp.dot(sort, y_ref[...].astype(BF16), preferred_element_type=F32).astype(BF16)
    nt = (((1,), (1,)), ((), ()))
    for expert in range(experts):
        rows = x_ref[expert * per : (expert + 1) * per]
        copies[expert * 3].wait()
        gate = lax.dot_general(rows, buf[expert * 3], nt, preferred_element_type=F32)
        copies[expert * 3 + 1].wait()
        up = lax.dot_general(rows, buf[expert * 3 + 1], nt, preferred_element_type=F32)
        hidden = (gate / (1.0 + jnp.exp(-gate)) * up).astype(BF16)
        copies[expert * 3 + 2].wait()
        piece = jnp.dot(hidden, buf[expert * 3 + 2], preferred_element_type=F32)
        x_ref[expert * per : (expert + 1) * per] = piece.astype(BF16)
    inverse = (to // step) * CAP + (to % step // CAP) * per + to % CAP
    unsort = jnp.where(frm == inverse, 1.0, 0.0).astype(BF16)
    y_ref[...] = jnp.dot(unsort, x_ref[...], preferred_element_type=F32)
    for plane in range(planes):
        for source in range(sources):
            lower = (plane * sources + source) * step
            out_refs[plane][source] = y_ref[lower : lower + step].astype(BF16)


def mix_kernel(ids_ref, weight_ref, *refs):
    in_refs, out_ref, y_ref = refs[:-2], refs[-2], refs[-1]
    dests, step = in_refs[0].shape[0], in_refs[0].shape[1]
    for dest in range(dests):
        for chunk, ref in enumerate(in_refs):
            lower = (dest * len(in_refs) + chunk) * step
            y_ref[lower : lower + step] = ref[dest].astype(F32)
    rows = y_ref[...].astype(BF16)
    n = ids_ref.shape[0]
    place = lax.broadcasted_iota(jnp.int32, (n, EXPERTS * CAP), 1)
    total = None
    for k, column in enumerate(slots(ids_ref[...])):
        pick = jnp.where(place == column, 1.0, 0.0).astype(BF16)
        part = weight_ref[:, k : k + 1] * jnp.dot(pick, rows, preferred_element_type=F32)
        total = part if total is None else total + part
    out_ref[...] = total.astype(BF16)


def after(value, earlier):
    return lax.optimization_barrier((value, earlier))[0]


def shape(dims, kind=BF16):
    return jax.ShapeDtypeStruct(dims, kind)


def on_device(
    tokens,
    norm_gain,
    queries,
    attn_keys,
    attn_values,
    expert_ids,
    route_weights,
    gate_proj,
    up_proj,
    down_proj,
):
    exp_count = lax.axis_size("exp")
    seq_count = lax.axis_size("seq")
    local_tokens, features = tokens.shape
    exp_dev, hidden = gate_proj.shape[0], gate_proj.shape[1]
    chunks = CHUNKS
    experts = exp_dev // chunks
    step = experts * CAP
    group = exp_count // SEG_DEV
    seg_len = group * local_tokens
    segs = seq_count * SEG_DEV
    att = queries.shape[1]
    width = att // group

    send = pl.pallas_call(
        prep_kernel,
        out_shape=[shape((exp_count, step, features))] * chunks,
        in_specs=[VMEM] * 3,
        out_specs=[VMEM] * chunks,
        compiler_params=params(32),
        cost_estimate=LITTLE,
        name="prep",
    )(tokens, norm_gain.reshape(1, -1), expert_ids)

    block = seg_len // SUMS
    sums = pl.pallas_call(
        functools.partial(sums_kernel, block),
        out_shape=shape((2 * local_tokens // block, att)),
        in_specs=[VMEM] * 2,
        out_specs=VMEM,
        compiler_params=params(32),
        cost_estimate=LITTLE,
        name="sums",
    )(after(attn_keys, send[0]), attn_values)
    halved = lax.ppermute(sums, "exp", [(i, i ^ group) for i in range(exp_count)])
    sums = jnp.concatenate([sums, halved], axis=0)
    parts = [sums]
    for other in range(1, seq_count):
        parts.append(lax.ppermute(sums, "seq", [(i, i ^ other) for i in range(seq_count)]))
    packed_rows = 3 * local_tokens + segs * 2 * local_tokens // block
    packed = pl.pallas_call(
        pack_kernel,
        out_shape=shape((group, packed_rows, width)),
        in_specs=[VMEM] * (3 + seq_count),
        out_specs=VMEM,
        compiler_params=params(32),
        cost_estimate=LITTLE,
        name="pack",
    )(queries, attn_keys, attn_values, *parts)
    recv = []
    for rows in send:
        if recv:
            rows = after(after(rows, recv[-1]), parts)
        recv.append(lax.all_to_all(rows, "exp", 0, 0, tiled=True))
    packed = after(packed, recv[-1])
    halves = [[half * group + j for j in range(group)] for half in range(SEG_DEV)]
    got = lax.all_to_all(packed, "exp", 0, 0, axis_index_groups=halves, tiled=True)
    segment = lax.axis_index("seq") * SEG_DEV + lax.axis_index("exp") // group
    place = lax.axis_index("exp") % group
    position = jnp.stack([segment, place]).astype(jnp.int32)
    done, mine = [], []
    for chunk in range(chunks):
        planes = [after(recv[chunk], recv[-1])]
        for other in range(1, seq_count):
            pairs = [(i, i ^ other) for i in range(seq_count)]
            planes.append(lax.ppermute(recv[chunk], "seq", pairs))
        total = seq_count * exp_count * step
        pieces = pl.pallas_call(
            functools.partial(ffn_kernel, chunk * experts, seq_count),
            out_shape=[shape((exp_count, step, features))] * seq_count,
            in_specs=[VMEM] * seq_count + [ANY] * 3,
            out_specs=[VMEM] * seq_count,
            scratch_shapes=[
                pltpu.VMEM((experts * 3, hidden, features), BF16),
                pltpu.VMEM((total, features), BF16),
                pltpu.VMEM((total, features), F32),
                pltpu.SemaphoreType.DMA((experts * 3,)),
            ],
            compiler_params=params(44),
            cost_estimate=LITTLE,
            name="experts",
        )(*planes, gate_proj, up_proj, down_proj)
        done.append(pieces)
    for chunk, pieces in enumerate(done):
        summed = after(pieces[0], done[-1][0]).astype(F32)
        for other in range(1, seq_count):
            pairs = [(i, i ^ other) for i in range(seq_count)]
            summed = summed + lax.ppermute(pieces[other], "seq", pairs).astype(F32)
        mine.append(summed.astype(BF16))
    got = after(got, mine[0])
    head_out = pl.pallas_call(
        functools.partial(attend_kernel, min(256, seg_len), local_tokens, segs),
        out_shape=[shape((local_tokens, width))] * group,
        in_specs=[SMEM, VMEM],
        out_specs=[VMEM] * group,
        scratch_shapes=[pltpu.VMEM((group, local_tokens, width), BF16)],
        compiler_params=params(48),
        cost_estimate=LITTLE,
        name="attend",
    )(position, got)
    heads = [
        rows
        if other == 0
        else lax.ppermute(rows, "exp", [(i, i ^ other) for i in range(exp_count)])
        for other, rows in enumerate(head_out)
    ]
    attention = pl.pallas_call(
        place_kernel,
        out_shape=shape((local_tokens, att)),
        in_specs=[SMEM] + [VMEM] * group,
        out_specs=VMEM,
        compiler_params=params(32),
        cost_estimate=LITTLE,
        name="place",
    )(position, *heads)

    back = [lax.all_to_all(rows, "exp", 0, 0, tiled=True) for rows in mine]
    expert_mix = pl.pallas_call(
        mix_kernel,
        out_shape=shape((local_tokens, features)),
        in_specs=[VMEM] * (2 + chunks),
        out_specs=VMEM,
        scratch_shapes=[pltpu.VMEM((EXPERTS * CAP, features), F32)],
        compiler_params=params(32),
        cost_estimate=LITTLE,
        name="mix",
    )(expert_ids, route_weights, *back)
    return (attention, expert_mix)


def solution(mesh):
    return jax.shard_map(
        on_device,
        mesh=mesh,
        in_specs=(
            P(("seq", "exp"), None),
            P(),
            P(("seq", "exp"), None),
            P(("seq", "exp"), None),
            P(("seq", "exp"), None),
            P(("seq", "exp"), None),
            P(("seq", "exp"), None),
            P("exp", "seq", None),
            P("exp", "seq", None),
            P("exp", "seq", None),
        ),
        out_specs=(P(("seq", "exp"), None), P(("seq", "exp"), None)),
        check_vma=False,
    )
```

```python
import functools
import math

import jax
import jax.numpy as jnp
from jax import lax
from jax.experimental import pallas as pl
from jax.experimental.pallas import tpu as pltpu
from jax.sharding import PartitionSpec as P

EXPERTS = 64
HDIM = 64
SUMS = 64
SEG_DEV = 2
CAP = 2
CHUNKS = 2

EPS = 1e-05
NEG = -1e30
F32 = jnp.float32
BF16 = jnp.bfloat16

VMEM = pl.BlockSpec(memory_space=pltpu.VMEM)
ANY = pl.BlockSpec(memory_space=pl.ANY)
LITTLE = pl.CostEstimate(flops=1000, bytes_accessed=1000, transcendentals=0)
SMEM = pl.BlockSpec(memory_space=pltpu.SMEM)


def params(mib):
    return pltpu.CompilerParams(vmem_limit_bytes=mib * 2**20)


def as_row(column):
    n = column.shape[0]
    eye = lax.broadcasted_iota(jnp.int32, (n, n), 0) == lax.broadcasted_iota(jnp.int32, (n, n), 1)
    return jnp.sum(jnp.where(eye, column, 0), axis=0, keepdims=True)


def slots(ids):
    n = ids.shape[0]
    columns = [ids[:, 0:1], ids[:, 1:2]]
    rows = [as_row(column) for column in columns]
    earlier = lax.broadcasted_iota(jnp.int32, (n, n), 1) < lax.broadcasted_iota(jnp.int32, (n, n), 0)
    found = []
    for column in columns:
        same = (rows[0] == column) | (rows[1] == column)
        before = jnp.sum(jnp.where(same & earlier, 1, 0), axis=1, keepdims=True)
        found.append(column * CAP + before)
    return found


def prep_kernel(tok_ref, gain_ref, ids_ref, *out_refs):
    n = tok_ref.shape[0]
    values = tok_ref[...].astype(F32)
    inv_rms = lax.rsqrt(jnp.mean(values * values, axis=-1, keepdims=True) + EPS)
    normed = (values * inv_rms * gain_ref[...]).astype(BF16)
    first, second = [as_row(column) for column in slots(ids_ref[...])]
    place = lax.broadcasted_iota(jnp.int32, (EXPERTS * CAP, n), 0)
    pick = jnp.where((place == first) | (place == second), 1.0, 0.0).astype(BF16)
    rows = jnp.dot(pick, normed, preferred_element_type=F32)
    dests, step = out_refs[0].shape[0], out_refs[0].shape[1]
    for dest in range(dests):
        for chunk, out_ref in enumerate(out_refs):
            lower = (dest * len(out_refs) + chunk) * step
            out_ref[dest] = rows[lower : lower + step].astype(BF16)


def sums_kernel(block, k_ref, v_ref, out_ref):
    total, _ = k_ref.shape
    count = total // block
    row = lax.broadcasted_iota(jnp.int32, (count, total), 0)
    column = lax.broadcasted_iota(jnp.int32, (count, total), 1)
    member = jnp.where(column // block == row, 1.0, 0.0).astype(BF16)
    for which, ref in enumerate((k_ref, v_ref)):
        summed = jnp.dot(member, ref[...], preferred_element_type=F32) * (1.0 / math.sqrt(block))
        out_ref[which * count : (which + 1) * count] = summed.astype(BF16)


def pack_kernel(q_ref, k_ref, v_ref, *refs):
    sum_refs, out_ref = refs[:-1], refs[-1]
    dests, _, width = out_ref.shape
    for dest in range(dests):
        lower = 0
        for ref in (q_ref, k_ref, v_ref, *sum_refs):
            upper = lower + ref.shape[0]
            out_ref[dest, lower:upper] = ref[:, dest * width : (dest + 1) * width]
            lower = upper


def attend_kernel(query_rows, tokens, segs, at_ref, recv_ref, *refs):
    out_refs, mixed_ref = refs[:-1], refs[-1]
    sources, _, width = recv_ref.shape
    seg_len = sources * tokens
    query, key, value = (
        recv_ref[:, which * tokens : (which + 1) * tokens].reshape(seg_len, width) for which in range(3)
    )
    sum_total = segs * SUMS
    per = SUMS // sources
    sum_rows = [
        recv_ref[:, 3 * tokens + at * per : 3 * tokens + (at + 1) * per].reshape(SUMS, width)
        for at in range(2 * segs)
    ]
    sum_keys = jnp.concatenate(sum_rows[0::2], axis=0)
    sum_values = jnp.concatenate(sum_rows[1::2], axis=0)
    scale = 1.0 / math.sqrt(HDIM)
    segment = at_ref[0]
    lane = lax.broadcasted_iota(jnp.int32, (1, width), 1)
    nt = (((1,), (1,)), ((), ()))
    for first in range(0, seg_len, query_rows):
        last = first + query_rows
        local_ok = (
            lax.broadcasted_iota(jnp.int32, (query_rows, last), 1)
            <= lax.broadcasted_iota(jnp.int32, (query_rows, last), 0) + first
        )
        summ_seg = lax.broadcasted_iota(jnp.int32, (query_rows, sum_total), 1) // SUMS
        summ_ok = jnp.bitwise_xor(summ_seg, segment) < segment
        mixed = jnp.zeros((query_rows, width), F32)
        for head in range(width // HDIM):
            mine = (lane >= head * HDIM) & (lane < (head + 1) * HDIM)
            rows = jnp.where(mine, query[first:last], jnp.zeros((), BF16))
            local_sc = lax.dot_general(rows, key[:last], nt, preferred_element_type=F32) * scale
            summ_sc = lax.dot_general(rows, sum_keys, nt, preferred_element_type=F32) * scale
            local_sc = jnp.where(local_ok, local_sc, NEG)
            summ_sc = jnp.where(summ_ok, summ_sc, NEG)
            top = jnp.maximum(
                jnp.max(local_sc, axis=-1, keepdims=True), jnp.max(summ_sc, axis=-1, keepdims=True)
            )
            local_ex = jnp.exp(local_sc - top)
            summ_ex = jnp.exp(summ_sc - top)
            inv = 1.0 / (
                jnp.sum(local_ex, axis=-1, keepdims=True) + jnp.sum(summ_ex, axis=-1, keepdims=True)
            )
            got = jnp.dot((local_ex * inv).astype(BF16), value[:last], preferred_element_type=F32)
            got += jnp.dot((summ_ex * inv).astype(BF16), sum_values, preferred_element_type=F32)
            mixed = jnp.where(mine, got, mixed)
        for source in range(first // tokens, last // tokens):
            lower = source * tokens - first
            mixed_ref[source] = mixed[lower : lower + tokens].astype(BF16)
    for other, out_ref in enumerate(out_refs):
        out_ref[...] = mixed_ref[jnp.bitwise_xor(at_ref[1], other)]


def place_kernel(at_ref, *refs):
    in_refs, out_ref = refs[:-1], refs[-1]
    width = in_refs[0].shape[1]
    for other, ref in enumerate(in_refs):
        lower = pl.multiple_of(jnp.bitwise_xor(at_ref[1], other) * width, width)
        out_ref[:, pl.ds(lower, width)] = ref[...]


def ffn_kernel(base, planes, *refs):
    row_refs, (gate_ref, up_ref, down_ref) = refs[:planes], refs[planes : planes + 3]
    out_refs = refs[planes + 3 : 2 * planes + 3]
    buf, x_ref, y_ref, sem = refs[2 * planes + 3 :]
    sources, step, width = row_refs[0].shape
    experts = step // CAP
    copies = []
    for expert in range(experts):
        for which, ref in enumerate((gate_ref, up_ref, down_ref)):
            at = expert * 3 + which
            copy = pltpu.make_async_copy(ref.at[base + expert], buf.at[at], sem.at[at])
            copy.start()
            copies.append(copy)
    total = planes * sources * step
    for plane in range(planes):
        for source in range(sources):
            lower = (plane * sources + source) * step
            y_ref[lower : lower + step] = row_refs[plane][source].astype(F32)
    to = lax.broadcasted_iota(jnp.int32, (total, total), 0)
    frm = lax.broadcasted_iota(jnp.int32, (total, total), 1)
    per = total // experts
    order = (to % per // CAP) * step + (to // per) * CAP + to % CAP
    sort = jnp.where(frm == order, 1.0, 0.0).astype(BF16)
    x_ref[...] = jnp.dot(sort, y_ref[...].astype(BF16), preferred_element_type=F32).astype(BF16)
    nt = (((1,), (1,)), ((), ()))
    for expert in range(experts):
        rows = x_ref[expert * per : (expert + 1) * per]
        copies[expert * 3].wait()
        gate = lax.dot_general(rows, buf[expert * 3], nt, preferred_element_type=F32)
        copies[expert * 3 + 1].wait()
        up = lax.dot_general(rows, buf[expert * 3 + 1], nt, preferred_element_type=F32)
        hidden = (gate / (1.0 + jnp.exp(-gate)) * up).astype(BF16)
        copies[expert * 3 + 2].wait()
        piece = jnp.dot(hidden, buf[expert * 3 + 2], preferred_element_type=F32)
        x_ref[expert * per : (expert + 1) * per] = piece.astype(BF16)
    inverse = (to // step) * CAP + (to % step // CAP) * per + to % CAP
    unsort = jnp.where(frm == inverse, 1.0, 0.0).astype(BF16)
    y_ref[...] = jnp.dot(unsort, x_ref[...], preferred_element_type=F32)
    for plane in range(planes):
        for source in range(sources):
            lower = (plane * sources + source) * step
            out_refs[plane][source] = y_ref[lower : lower + step].astype(BF16)


def mix_kernel(ids_ref, weight_ref, *refs):
    in_refs, out_ref, y_ref = refs[:-2], refs[-2], refs[-1]
    dests, step = in_refs[0].shape[0], in_refs[0].shape[1]
    for dest in range(dests):
        for chunk, ref in enumerate(in_refs):
            lower = (dest * len(in_refs) + chunk) * step
            y_ref[lower : lower + step] = ref[dest].astype(F32)
    rows = y_ref[...].astype(BF16)
    n = ids_ref.shape[0]
    place = lax.broadcasted_iota(jnp.int32, (n, EXPERTS * CAP), 1)
    total = None
    for k, column in enumerate(slots(ids_ref[...])):
        pick = jnp.where(place == column, 1.0, 0.0).astype(BF16)
        part = weight_ref[:, k : k + 1] * jnp.dot(pick, rows, preferred_element_type=F32)
        total = part if total is None else total + part
    out_ref[...] = total.astype(BF16)


def after(value, earlier):
    return lax.optimization_barrier((value, earlier))[0]


def shape(dims, kind=BF16):
    return jax.ShapeDtypeStruct(dims, kind)


def on_device(
    tokens,
    norm_gain,
    queries,
    attn_keys,
    attn_values,
    expert_ids,
    route_weights,
    gate_proj,
    up_proj,
    down_proj,
):
    exp_count = lax.axis_size("exp")
    seq_count = lax.axis_size("seq")
    local_tokens, features = tokens.shape
    exp_dev, hidden = gate_proj.shape[0], gate_proj.shape[1]
    chunks = CHUNKS
    experts = exp_dev // chunks
    step = experts * CAP
    group = exp_count // SEG_DEV
    seg_len = group * local_tokens
    segs = seq_count * SEG_DEV
    att = queries.shape[1]
    width = att // group

    send = pl.pallas_call(
        prep_kernel,
        out_shape=[shape((exp_count, step, features))] * chunks,
        in_specs=[VMEM] * 3,
        out_specs=[VMEM] * chunks,
        compiler_params=params(32),
        cost_estimate=LITTLE,
        name="prep",
    )(tokens, norm_gain.reshape(1, -1), expert_ids)

    block = seg_len // SUMS
    sums = pl.pallas_call(
        functools.partial(sums_kernel, block),
        out_shape=shape((2 * local_tokens // block, att)),
        in_specs=[VMEM] * 2,
        out_specs=VMEM,
        compiler_params=params(32),
        cost_estimate=LITTLE,
        name="sums",
    )(after(attn_keys, send[0]), attn_values)
    halved = lax.ppermute(sums, "exp", [(i, i ^ group) for i in range(exp_count)])
    sums = jnp.concatenate([sums, halved], axis=0)
    parts = [sums]
    for other in range(1, seq_count):
        parts.append(lax.ppermute(sums, "seq", [(i, i ^ other) for i in range(seq_count)]))
    packed_rows = 3 * local_tokens + segs * 2 * local_tokens // block
    packed = pl.pallas_call(
        pack_kernel,
        out_shape=shape((group, packed_rows, width)),
        in_specs=[VMEM] * (3 + seq_count),
        out_specs=VMEM,
        compiler_params=params(32),
        cost_estimate=LITTLE,
        name="pack",
    )(queries, attn_keys, attn_values, *parts)
    recv = []
    for rows in send:
        if recv:
            rows = after(rows, recv[-1])
        recv.append(lax.all_to_all(rows, "exp", 0, 0, tiled=True))
    packed = after(packed, recv[-1])
    halves = [[half * group + j for j in range(group)] for half in range(SEG_DEV)]
    got = lax.all_to_all(packed, "exp", 0, 0, axis_index_groups=halves, tiled=True)
    segment = lax.axis_index("seq") * SEG_DEV + lax.axis_index("exp") // group
    place = lax.axis_index("exp") % group
    position = jnp.stack([segment, place]).astype(jnp.int32)
    done, mine = [], []
    for chunk in range(chunks):
        planes = [after(after(recv[chunk], recv[-1]), parts)]
        for other in range(1, seq_count):
            pairs = [(i, i ^ other) for i in range(seq_count)]
            planes.append(lax.ppermute(recv[chunk], "seq", pairs))
        total = seq_count * exp_count * step
        pieces = pl.pallas_call(
            functools.partial(ffn_kernel, chunk * experts, seq_count),
            out_shape=[shape((exp_count, step, features))] * seq_count,
            in_specs=[VMEM] * seq_count + [ANY] * 3,
            out_specs=[VMEM] * seq_count,
            scratch_shapes=[
                pltpu.VMEM((experts * 3, hidden, features), BF16),
                pltpu.VMEM((total, features), BF16),
                pltpu.VMEM((total, features), F32),
                pltpu.SemaphoreType.DMA((experts * 3,)),
            ],
            compiler_params=params(44),
            cost_estimate=LITTLE,
            name="experts",
        )(*planes, gate_proj, up_proj, down_proj)
        done.append(pieces)
    for chunk, pieces in enumerate(done):
        summed = after(after(pieces[0], done[-1][0]), got).astype(F32)
        for other in range(1, seq_count):
            pairs = [(i, i ^ other) for i in range(seq_count)]
            summed = summed + lax.ppermute(pieces[other], "seq", pairs).astype(F32)
        mine.append(summed.astype(BF16))
    got = after(got, mine[0])
    head_out = pl.pallas_call(
        functools.partial(attend_kernel, min(256, seg_len), local_tokens, segs),
        out_shape=[shape((local_tokens, width))] * group,
        in_specs=[SMEM, VMEM],
        out_specs=[VMEM] * group,
        scratch_shapes=[pltpu.VMEM((group, local_tokens, width), BF16)],
        compiler_params=params(48),
        cost_estimate=LITTLE,
        name="attend",
    )(position, got)
    heads = [
        rows
        if other == 0
        else lax.ppermute(rows, "exp", [(i, i ^ other) for i in range(exp_count)])
        for other, rows in enumerate(head_out)
    ]
    attention = pl.pallas_call(
        place_kernel,
        out_shape=shape((local_tokens, att)),
        in_specs=[SMEM] + [VMEM] * group,
        out_specs=VMEM,
        compiler_params=params(32),
        cost_estimate=LITTLE,
        name="place",
    )(position, *heads)

    mine[-1] = after(mine[-1], head_out[0])
    back = [lax.all_to_all(rows, "exp", 0, 0, tiled=True) for rows in mine]
    expert_mix = pl.pallas_call(
        mix_kernel,
        out_shape=shape((local_tokens, features)),
        in_specs=[VMEM] * (2 + chunks),
        out_specs=VMEM,
        scratch_shapes=[pltpu.VMEM((EXPERTS * CAP, features), F32)],
        compiler_params=params(32),
        cost_estimate=LITTLE,
        name="mix",
    )(expert_ids, route_weights, *back)
    return (attention, expert_mix)


def solution(mesh):
    return jax.shard_map(
        on_device,
        mesh=mesh,
        in_specs=(
            P(("seq", "exp"), None),
            P(),
            P(("seq", "exp"), None),
            P(("seq", "exp"), None),
            P(("seq", "exp"), None),
            P(("seq", "exp"), None),
            P(("seq", "exp"), None),
            P("exp", "seq", None),
            P("exp", "seq", None),
            P("exp", "seq", None),
        ),
        out_specs=(P(("seq", "exp"), None), P(("seq", "exp"), None)),
        check_vma=False,
    )
```

```python
import functools
import math

import jax
import jax.numpy as jnp
from jax import lax
from jax.experimental import pallas as pl
from jax.experimental.pallas import tpu as pltpu
from jax.sharding import PartitionSpec as P

EXPERTS = 64
HDIM = 64
SUMS = 64
SEG_DEV = 2
CAP = 2
CHUNKS = 2

EPS = 1e-05
NEG = -1e30
F32 = jnp.float32
BF16 = jnp.bfloat16

VMEM = pl.BlockSpec(memory_space=pltpu.VMEM)
ANY = pl.BlockSpec(memory_space=pl.ANY)
LITTLE = pl.CostEstimate(flops=1000, bytes_accessed=1000, transcendentals=0)
SMEM = pl.BlockSpec(memory_space=pltpu.SMEM)


def params(mib):
    return pltpu.CompilerParams(vmem_limit_bytes=mib * 2**20)


def as_row(column):
    n = column.shape[0]
    eye = lax.broadcasted_iota(jnp.int32, (n, n), 0) == lax.broadcasted_iota(jnp.int32, (n, n), 1)
    return jnp.sum(jnp.where(eye, column, 0), axis=0, keepdims=True)


def slots(ids):
    n = ids.shape[0]
    columns = [ids[:, 0:1], ids[:, 1:2]]
    rows = [as_row(column) for column in columns]
    earlier = lax.broadcasted_iota(jnp.int32, (n, n), 1) < lax.broadcasted_iota(jnp.int32, (n, n), 0)
    found = []
    for column in columns:
        same = (rows[0] == column) | (rows[1] == column)
        before = jnp.sum(jnp.where(same & earlier, 1, 0), axis=1, keepdims=True)
        found.append(column * CAP + before)
    return found


def prep_kernel(tok_ref, gain_ref, ids_ref, *out_refs):
    n = tok_ref.shape[0]
    values = tok_ref[...].astype(F32)
    inv_rms = lax.rsqrt(jnp.mean(values * values, axis=-1, keepdims=True) + EPS)
    normed = (values * inv_rms * gain_ref[...]).astype(BF16)
    first, second = [as_row(column) for column in slots(ids_ref[...])]
    place = lax.broadcasted_iota(jnp.int32, (EXPERTS * CAP, n), 0)
    pick = jnp.where((place == first) | (place == second), 1.0, 0.0).astype(BF16)
    rows = jnp.dot(pick, normed, preferred_element_type=F32)
    dests, step = out_refs[0].shape[0], out_refs[0].shape[1]
    for dest in range(dests):
        for chunk, out_ref in enumerate(out_refs):
            lower = (dest * len(out_refs) + chunk) * step
            out_ref[dest] = rows[lower : lower + step].astype(BF16)


def sums_kernel(block, k_ref, v_ref, out_ref):
    total, _ = k_ref.shape
    count = total // block
    row = lax.broadcasted_iota(jnp.int32, (count, total), 0)
    column = lax.broadcasted_iota(jnp.int32, (count, total), 1)
    member = jnp.where(column // block == row, 1.0, 0.0).astype(BF16)
    for which, ref in enumerate((k_ref, v_ref)):
        summed = jnp.dot(member, ref[...], preferred_element_type=F32) * (1.0 / math.sqrt(block))
        out_ref[which * count : (which + 1) * count] = summed.astype(BF16)


def pack_kernel(q_ref, k_ref, v_ref, *refs):
    sum_refs, out_ref = refs[:-1], refs[-1]
    dests, _, width = out_ref.shape
    for dest in range(dests):
        lower = 0
        for ref in (q_ref, k_ref, v_ref, *sum_refs):
            upper = lower + ref.shape[0]
            out_ref[dest, lower:upper] = ref[:, dest * width : (dest + 1) * width]
            lower = upper


def attend_kernel(query_rows, tokens, segs, at_ref, recv_ref, *refs):
    out_refs, mixed_ref = refs[:-1], refs[-1]
    sources, _, width = recv_ref.shape
    seg_len = sources * tokens
    query, key, value = (
        recv_ref[:, which * tokens : (which + 1) * tokens].reshape(seg_len, width) for which in range(3)
    )
    sum_total = segs * SUMS
    per = SUMS // sources
    sum_rows = [
        recv_ref[:, 3 * tokens + at * per : 3 * tokens + (at + 1) * per].reshape(SUMS, width)
        for at in range(2 * segs)
    ]
    sum_keys = jnp.concatenate(sum_rows[0::2], axis=0)
    sum_values = jnp.concatenate(sum_rows[1::2], axis=0)
    scale = 1.0 / math.sqrt(HDIM)
    segment = at_ref[0]
    lane = lax.broadcasted_iota(jnp.int32, (1, width), 1)
    nt = (((1,), (1,)), ((), ()))
    for first in range(0, seg_len, query_rows):
        last = first + query_rows
        local_ok = (
            lax.broadcasted_iota(jnp.int32, (query_rows, last), 1)
            <= lax.broadcasted_iota(jnp.int32, (query_rows, last), 0) + first
        )
        summ_seg = lax.broadcasted_iota(jnp.int32, (query_rows, sum_total), 1) // SUMS
        summ_ok = jnp.bitwise_xor(summ_seg, segment) < segment
        mixed = jnp.zeros((query_rows, width), F32)
        for head in range(width // HDIM):
            mine = (lane >= head * HDIM) & (lane < (head + 1) * HDIM)
            rows = jnp.where(mine, query[first:last], jnp.zeros((), BF16))
            local_sc = lax.dot_general(rows, key[:last], nt, preferred_element_type=F32) * scale
            summ_sc = lax.dot_general(rows, sum_keys, nt, preferred_element_type=F32) * scale
            local_sc = jnp.where(local_ok, local_sc, NEG)
            summ_sc = jnp.where(summ_ok, summ_sc, NEG)
            top = jnp.maximum(
                jnp.max(local_sc, axis=-1, keepdims=True), jnp.max(summ_sc, axis=-1, keepdims=True)
            )
            local_ex = jnp.exp(local_sc - top)
            summ_ex = jnp.exp(summ_sc - top)
            inv = 1.0 / (
                jnp.sum(local_ex, axis=-1, keepdims=True) + jnp.sum(summ_ex, axis=-1, keepdims=True)
            )
            got = jnp.dot((local_ex * inv).astype(BF16), value[:last], preferred_element_type=F32)
            got += jnp.dot((summ_ex * inv).astype(BF16), sum_values, preferred_element_type=F32)
            mixed = jnp.where(mine, got, mixed)
        for source in range(first // tokens, last // tokens):
            lower = source * tokens - first
            mixed_ref[source] = mixed[lower : lower + tokens].astype(BF16)
    for other, out_ref in enumerate(out_refs):
        out_ref[...] = mixed_ref[jnp.bitwise_xor(at_ref[1], other)]


def place_kernel(at_ref, *refs):
    in_refs, out_ref = refs[:-1], refs[-1]
    width = in_refs[0].shape[1]
    for other, ref in enumerate(in_refs):
        lower = pl.multiple_of(jnp.bitwise_xor(at_ref[1], other) * width, width)
        out_ref[:, pl.ds(lower, width)] = ref[...]


def ffn_kernel(base, planes, *refs):
    row_refs, (gate_ref, up_ref, down_ref) = refs[:planes], refs[planes : planes + 3]
    out_refs = refs[planes + 3 : 2 * planes + 3]
    buf, x_ref, y_ref, sem = refs[2 * planes + 3 :]
    sources, step, width = row_refs[0].shape
    experts = step // CAP
    copies = []
    for expert in range(experts):
        for which, ref in enumerate((gate_ref, up_ref, down_ref)):
            at = expert * 3 + which
            copy = pltpu.make_async_copy(ref.at[base + expert], buf.at[at], sem.at[at])
            copy.start()
            copies.append(copy)
    total = planes * sources * step
    for plane in range(planes):
        for source in range(sources):
            lower = (plane * sources + source) * step
            y_ref[lower : lower + step] = row_refs[plane][source].astype(F32)
    to = lax.broadcasted_iota(jnp.int32, (total, total), 0)
    frm = lax.broadcasted_iota(jnp.int32, (total, total), 1)
    per = total // experts
    order = (to % per // CAP) * step + (to // per) * CAP + to % CAP
    sort = jnp.where(frm == order, 1.0, 0.0).astype(BF16)
    x_ref[...] = jnp.dot(sort, y_ref[...].astype(BF16), preferred_element_type=F32).astype(BF16)
    nt = (((1,), (1,)), ((), ()))
    for expert in range(experts):
        rows = x_ref[expert * per : (expert + 1) * per]
        copies[expert * 3].wait()
        gate = lax.dot_general(rows, buf[expert * 3], nt, preferred_element_type=F32)
        copies[expert * 3 + 1].wait()
        up = lax.dot_general(rows, buf[expert * 3 + 1], nt, preferred_element_type=F32)
        hidden = (gate / (1.0 + jnp.exp(-gate)) * up).astype(BF16)
        copies[expert * 3 + 2].wait()
        piece = jnp.dot(hidden, buf[expert * 3 + 2], preferred_element_type=F32)
        x_ref[expert * per : (expert + 1) * per] = piece.astype(BF16)
    inverse = (to // step) * CAP + (to % step // CAP) * per + to % CAP
    unsort = jnp.where(frm == inverse, 1.0, 0.0).astype(BF16)
    y_ref[...] = jnp.dot(unsort, x_ref[...], preferred_element_type=F32)
    for plane in range(planes):
        for source in range(sources):
            lower = (plane * sources + source) * step
            out_refs[plane][source] = y_ref[lower : lower + step].astype(BF16)


def mix_kernel(ids_ref, weight_ref, *refs):
    in_refs, out_ref, y_ref = refs[:-2], refs[-2], refs[-1]
    dests, step = in_refs[0].shape[0], in_refs[0].shape[1]
    for dest in range(dests):
        for chunk, ref in enumerate(in_refs):
            lower = (dest * len(in_refs) + chunk) * step
            y_ref[lower : lower + step] = ref[dest].astype(F32)
    rows = y_ref[...].astype(BF16)
    n = ids_ref.shape[0]
    place = lax.broadcasted_iota(jnp.int32, (n, EXPERTS * CAP), 1)
    total = None
    for k, column in enumerate(slots(ids_ref[...])):
        pick = jnp.where(place == column, 1.0, 0.0).astype(BF16)
        part = weight_ref[:, k : k + 1] * jnp.dot(pick, rows, preferred_element_type=F32)
        total = part if total is None else total + part
    out_ref[...] = total.astype(BF16)


def after(value, earlier):
    return lax.optimization_barrier((value, earlier))[0]


def shape(dims, kind=BF16):
    return jax.ShapeDtypeStruct(dims, kind)


def on_device(
    tokens,
    norm_gain,
    queries,
    attn_keys,
    attn_values,
    expert_ids,
    route_weights,
    gate_proj,
    up_proj,
    down_proj,
):
    exp_count = lax.axis_size("exp")
    seq_count = lax.axis_size("seq")
    local_tokens, features = tokens.shape
    exp_dev, hidden = gate_proj.shape[0], gate_proj.shape[1]
    chunks = CHUNKS
    experts = exp_dev // chunks
    step = experts * CAP
    group = exp_count // SEG_DEV
    seg_len = group * local_tokens
    segs = seq_count * SEG_DEV
    att = queries.shape[1]
    width = att // group

    send = pl.pallas_call(
        prep_kernel,
        out_shape=[shape((exp_count, step, features))] * chunks,
        in_specs=[VMEM] * 3,
        out_specs=[VMEM] * chunks,
        compiler_params=params(32),
        cost_estimate=LITTLE,
        name="prep",
    )(tokens, norm_gain.reshape(1, -1), expert_ids)

    def device(segment, j):
        return (segment // SEG_DEV) * exp_count + (segment % SEG_DEV) * group + j

    block = seg_len // SUMS
    sums = pl.pallas_call(
        functools.partial(sums_kernel, block),
        out_shape=shape((2 * local_tokens // block, att)),
        in_specs=[VMEM] * 2,
        out_specs=VMEM,
        compiler_params=params(32),
        cost_estimate=LITTLE,
        name="sums",
    )(after(attn_keys, send[0]), attn_values)
    parts = [sums]
    for other in range(1, segs):
        pairs = []
        for segment in range(segs):
            for j in range(group):
                pairs.append((device(segment, j), device(segment ^ other, j)))
        parts.append(lax.ppermute(sums, ("seq", "exp"), pairs))
    packed_rows = 3 * local_tokens + segs * 2 * local_tokens // block
    packed = pl.pallas_call(
        pack_kernel,
        out_shape=shape((group, packed_rows, width)),
        in_specs=[VMEM] * (3 + segs),
        out_specs=VMEM,
        compiler_params=params(32),
        cost_estimate=LITTLE,
        name="pack",
    )(queries, attn_keys, attn_values, *parts)
    recv = []
    for rows in send:
        if recv:
            rows = after(after(rows, recv[-1]), sums)
        recv.append(lax.all_to_all(rows, "exp", 0, 0, tiled=True))
    packed = after(packed, recv[-1])
    halves = [[half * group + j for j in range(group)] for half in range(SEG_DEV)]
    got = lax.all_to_all(packed, "exp", 0, 0, axis_index_groups=halves, tiled=True)
    segment = lax.axis_index("seq") * SEG_DEV + lax.axis_index("exp") // group
    place = lax.axis_index("exp") % group
    position = jnp.stack([segment, place]).astype(jnp.int32)
    done, mine = [], []
    for chunk in range(chunks):
        planes = [after(recv[chunk], recv[-1])]
        for other in range(1, seq_count):
            pairs = [(i, i ^ other) for i in range(seq_count)]
            planes.append(lax.ppermute(recv[chunk], "seq", pairs))
        total = seq_count * exp_count * step
        pieces = pl.pallas_call(
            functools.partial(ffn_kernel, chunk * experts, seq_count),
            out_shape=[shape((exp_count, step, features))] * seq_count,
            in_specs=[VMEM] * seq_count + [ANY] * 3,
            out_specs=[VMEM] * seq_count,
            scratch_shapes=[
                pltpu.VMEM((experts * 3, hidden, features), BF16),
                pltpu.VMEM((total, features), BF16),
                pltpu.VMEM((total, features), F32),
                pltpu.SemaphoreType.DMA((experts * 3,)),
            ],
            compiler_params=params(44),
            cost_estimate=LITTLE,
            name="experts",
        )(*planes, gate_proj, up_proj, down_proj)
        done.append(pieces)
    for chunk, pieces in enumerate(done):
        summed = after(after(pieces[0], done[-1][0]), got).astype(F32)
        for other in range(1, seq_count):
            pairs = [(i, i ^ other) for i in range(seq_count)]
            summed = summed + lax.ppermute(pieces[other], "seq", pairs).astype(F32)
        mine.append(summed.astype(BF16))
    got = after(got, mine[0])
    head_out = pl.pallas_call(
        functools.partial(attend_kernel, min(256, seg_len), local_tokens, segs),
        out_shape=[shape((local_tokens, width))] * group,
        in_specs=[SMEM, VMEM],
        out_specs=[VMEM] * group,
        scratch_shapes=[pltpu.VMEM((group, local_tokens, width), BF16)],
        compiler_params=params(48),
        cost_estimate=LITTLE,
        name="attend",
    )(position, got)
    heads = [
        rows
        if other == 0
        else lax.ppermute(rows, "exp", [(i, i ^ other) for i in range(exp_count)])
        for other, rows in enumerate(head_out)
    ]
    attention = pl.pallas_call(
        place_kernel,
        out_shape=shape((local_tokens, att)),
        in_specs=[SMEM] + [VMEM] * group,
        out_specs=VMEM,
        compiler_params=params(32),
        cost_estimate=LITTLE,
        name="place",
    )(position, *heads)

    mine[-1] = after(mine[-1], head_out[0])
    back = [lax.all_to_all(rows, "exp", 0, 0, tiled=True) for rows in mine]
    expert_mix = pl.pallas_call(
        mix_kernel,
        out_shape=shape((local_tokens, features)),
        in_specs=[VMEM] * (2 + chunks),
        out_specs=VMEM,
        scratch_shapes=[pltpu.VMEM((EXPERTS * CAP, features), F32)],
        compiler_params=params(32),
        cost_estimate=LITTLE,
        name="mix",
    )(expert_ids, route_weights, *back)
    return (attention, expert_mix)


def solution(mesh):
    return jax.shard_map(
        on_device,
        mesh=mesh,
        in_specs=(
            P(("seq", "exp"), None),
            P(),
            P(("seq", "exp"), None),
            P(("seq", "exp"), None),
            P(("seq", "exp"), None),
            P(("seq", "exp"), None),
            P(("seq", "exp"), None),
            P("exp", "seq", None),
            P("exp", "seq", None),
            P("exp", "seq", None),
        ),
        out_specs=(P(("seq", "exp"), None), P(("seq", "exp"), None)),
        check_vma=False,
    )
```

```python
import functools
import math

import jax
import jax.numpy as jnp
from jax import lax
from jax.experimental import pallas as pl
from jax.experimental.pallas import tpu as pltpu
from jax.sharding import PartitionSpec as P

EXPERTS = 64
HDIM = 64
SUMS = 64
SEG_DEV = 2
CAP = 2
CHUNKS = 2

EPS = 1e-05
NEG = -1e30
F32 = jnp.float32
BF16 = jnp.bfloat16

VMEM = pl.BlockSpec(memory_space=pltpu.VMEM)
ANY = pl.BlockSpec(memory_space=pl.ANY)
LITTLE = pl.CostEstimate(flops=1000, bytes_accessed=1000, transcendentals=0)
SMEM = pl.BlockSpec(memory_space=pltpu.SMEM)


def params(mib):
    return pltpu.CompilerParams(vmem_limit_bytes=mib * 2**20)


def as_column(row):
    n = row.shape[1]
    eye = lax.broadcasted_iota(jnp.int32, (n, n), 0) == lax.broadcasted_iota(jnp.int32, (n, n), 1)
    return jnp.sum(jnp.where(eye, row, jnp.zeros((), row.dtype)), axis=1, keepdims=True)


def slots(ids):
    n = ids.shape[1]
    rows = [ids[0:1], ids[1:2]]
    columns = [as_column(row) for row in rows]
    earlier = lax.broadcasted_iota(jnp.int32, (n, n), 0) < lax.broadcasted_iota(jnp.int32, (n, n), 1)
    found = []
    for row in rows:
        same = (columns[0] == row) | (columns[1] == row)
        before = jnp.sum(jnp.where(same & earlier, 1, 0), axis=0, keepdims=True)
        found.append(row * CAP + before)
    return found


def prep_kernel(block, tok_hbm, gain_ref, ids_ref, k_hbm, v_hbm, *refs):
    out_refs, sum_ref, (tok_ref, k_ref, v_ref, sem) = refs[:-5], refs[-5], refs[-4:]
    copies = [
        pltpu.make_async_copy(frm, to, sem.at[at])
        for at, (frm, to) in enumerate(((tok_hbm, tok_ref), (k_hbm, k_ref), (v_hbm, v_ref)))
    ]
    for copy in copies:
        copy.start()
    n = tok_ref.shape[0]
    first, second = slots(ids_ref[...])
    place = lax.broadcasted_iota(jnp.int32, (EXPERTS * CAP, n), 0)
    pick = jnp.where((place == first) | (place == second), 1.0, 0.0).astype(BF16)
    copies[0].wait()
    values = tok_ref[...].astype(F32)
    inv_rms = lax.rsqrt(jnp.mean(values * values, axis=-1, keepdims=True) + EPS)
    normed = (values * inv_rms * gain_ref[...]).astype(BF16)
    rows = jnp.dot(pick, normed, preferred_element_type=F32)
    dests, step = out_refs[0].shape[0], out_refs[0].shape[1]
    for dest in range(dests):
        for chunk, out_ref in enumerate(out_refs):
            lower = (dest * len(out_refs) + chunk) * step
            out_ref[dest] = rows[lower : lower + step].astype(BF16)
    count = n // block
    row = lax.broadcasted_iota(jnp.int32, (count, n), 0)
    column = lax.broadcasted_iota(jnp.int32, (count, n), 1)
    member = jnp.where(column // block == row, 1.0, 0.0).astype(BF16)
    for which, ref in enumerate((k_ref, v_ref)):
        copies[which + 1].wait()
        summed = jnp.dot(member, ref[...], preferred_element_type=F32) * (1.0 / math.sqrt(block))
        sum_ref[which * count : (which + 1) * count] = summed.astype(BF16)


def pack_kernel(q_hbm, k_hbm, v_hbm, *refs):
    sum_refs, out_ref, sem = refs[:-2], refs[-2], refs[-1]
    dests, _, width = out_ref.shape
    tokens = q_hbm.shape[0]
    copies = []
    for dest in range(dests):
        for which, ref in enumerate((q_hbm, k_hbm, v_hbm)):
            copies.append(
                pltpu.make_async_copy(
                    ref.at[:, pl.ds(dest * width, width)],
                    out_ref.at[dest, pl.ds(which * tokens, tokens)],
                    sem.at[dest * 3 + which],
                )
            )
    for copy in copies:
        copy.start()
    for dest in range(dests):
        lower = 3 * tokens
        for ref in sum_refs:
            upper = lower + ref.shape[0]
            out_ref[dest, lower:upper] = ref[:, dest * width : (dest + 1) * width]
            lower = upper
    for copy in copies:
        copy.wait()


def attend_kernel(query_rows, tokens, segs, at_ref, recv_ref, *refs):
    out_refs, mixed_ref = refs[:-1], refs[-1]
    sources, _, width = recv_ref.shape
    seg_len = sources * tokens
    query, key, value = (
        recv_ref[:, which * tokens : (which + 1) * tokens].reshape(seg_len, width) for which in range(3)
    )
    sum_total = segs * SUMS
    per = SUMS // sources
    sum_rows = [
        recv_ref[:, 3 * tokens + at * per : 3 * tokens + (at + 1) * per].reshape(SUMS, width)
        for at in range(2 * segs)
    ]
    sum_keys = jnp.concatenate(sum_rows[0::2], axis=0)
    sum_values = jnp.concatenate(sum_rows[1::2], axis=0)
    scale = 1.0 / math.sqrt(HDIM)
    segment = at_ref[0]
    lane = lax.broadcasted_iota(jnp.int32, (1, width), 1)
    nt = (((1,), (1,)), ((), ()))
    for first in range(0, seg_len, query_rows):
        last = first + query_rows
        local_ok = (
            lax.broadcasted_iota(jnp.int32, (query_rows, last), 1)
            <= lax.broadcasted_iota(jnp.int32, (query_rows, last), 0) + first
        )
        summ_seg = lax.broadcasted_iota(jnp.int32, (query_rows, sum_total), 1) // SUMS
        summ_ok = jnp.bitwise_xor(summ_seg, segment) < segment
        mixed = jnp.zeros((query_rows, width), F32)
        for head in range(width // HDIM):
            mine = (lane >= head * HDIM) & (lane < (head + 1) * HDIM)
            rows = jnp.where(mine, query[first:last], jnp.zeros((), BF16))
            local_sc = lax.dot_general(rows, key[:last], nt, preferred_element_type=F32) * scale
            summ_sc = lax.dot_general(rows, sum_keys, nt, preferred_element_type=F32) * scale
            local_sc = jnp.where(local_ok, local_sc, NEG)
            summ_sc = jnp.where(summ_ok, summ_sc, NEG)
            top = jnp.maximum(
                jnp.max(local_sc, axis=-1, keepdims=True), jnp.max(summ_sc, axis=-1, keepdims=True)
            )
            local_ex = jnp.exp(local_sc - top)
            summ_ex = jnp.exp(summ_sc - top)
            inv = 1.0 / (
                jnp.sum(local_ex, axis=-1, keepdims=True) + jnp.sum(summ_ex, axis=-1, keepdims=True)
            )
            got = jnp.dot((local_ex * inv).astype(BF16), value[:last], preferred_element_type=F32)
            got += jnp.dot((summ_ex * inv).astype(BF16), sum_values, preferred_element_type=F32)
            mixed = jnp.where(mine, got, mixed)
        for source in range(first // tokens, last // tokens):
            lower = source * tokens - first
            mixed_ref[source] = mixed[lower : lower + tokens].astype(BF16)
    for other, out_ref in enumerate(out_refs):
        out_ref[...] = mixed_ref[jnp.bitwise_xor(at_ref[1], other)]


def place_kernel(at_ref, *refs):
    in_refs, out_ref = refs[:-1], refs[-1]
    width = in_refs[0].shape[1]
    for other, ref in enumerate(in_refs):
        lower = pl.multiple_of(jnp.bitwise_xor(at_ref[1], other) * width, width)
        out_ref[:, pl.ds(lower, width)] = ref[...]


def ffn_kernel(base, planes, *refs):
    row_refs, (gate_ref, up_ref, down_ref) = refs[:planes], refs[planes : planes + 3]
    out_refs = refs[planes + 3 : 2 * planes + 3]
    buf, x_ref, y_ref, sem = refs[2 * planes + 3 :]
    sources, step, width = row_refs[0].shape
    experts = step // CAP
    copies = []
    for expert in range(experts):
        for which, ref in enumerate((gate_ref, up_ref, down_ref)):
            at = expert * 3 + which
            copy = pltpu.make_async_copy(ref.at[base + expert], buf.at[at], sem.at[at])
            copy.start()
            copies.append(copy)
    total = planes * sources * step
    for plane in range(planes):
        for source in range(sources):
            lower = (plane * sources + source) * step
            y_ref[lower : lower + step] = row_refs[plane][source].astype(F32)
    to = lax.broadcasted_iota(jnp.int32, (total, total), 0)
    frm = lax.broadcasted_iota(jnp.int32, (total, total), 1)
    per = total // experts
    order = (to % per // CAP) * step + (to // per) * CAP + to % CAP
    sort = jnp.where(frm == order, 1.0, 0.0).astype(BF16)
    x_ref[...] = jnp.dot(sort, y_ref[...].astype(BF16), preferred_element_type=F32).astype(BF16)
    nt = (((1,), (1,)), ((), ()))
    for expert in range(experts):
        rows = x_ref[expert * per : (expert + 1) * per]
        copies[expert * 3].wait()
        gate = lax.dot_general(rows, buf[expert * 3], nt, preferred_element_type=F32)
        copies[expert * 3 + 1].wait()
        up = lax.dot_general(rows, buf[expert * 3 + 1], nt, preferred_element_type=F32)
        hidden = (gate / (1.0 + jnp.exp(-gate)) * up).astype(BF16)
        copies[expert * 3 + 2].wait()
        piece = jnp.dot(hidden, buf[expert * 3 + 2], preferred_element_type=F32)
        x_ref[expert * per : (expert + 1) * per] = piece.astype(BF16)
    inverse = (to // step) * CAP + (to % step // CAP) * per + to % CAP
    unsort = jnp.where(frm == inverse, 1.0, 0.0).astype(BF16)
    y_ref[...] = jnp.dot(unsort, x_ref[...], preferred_element_type=F32)
    for plane in range(planes):
        for source in range(sources):
            lower = (plane * sources + source) * step
            out_refs[plane][source] = y_ref[lower : lower + step].astype(BF16)


def mix_kernel(ids_ref, weight_ref, *refs):
    in_refs, out_ref, y_ref = refs[:-2], refs[-2], refs[-1]
    dests, step = in_refs[0].shape[0], in_refs[0].shape[1]
    for dest in range(dests):
        for chunk, ref in enumerate(in_refs):
            lower = (dest * len(in_refs) + chunk) * step
            y_ref[lower : lower + step] = ref[dest].astype(F32)
    rows = y_ref[...].astype(BF16)
    n = ids_ref.shape[1]
    place = lax.broadcasted_iota(jnp.int32, (n, EXPERTS * CAP), 1)
    total = None
    for k, row in enumerate(slots(ids_ref[...])):
        pick = jnp.where(place == as_column(row), 1.0, 0.0).astype(BF16)
        part = as_column(weight_ref[k : k + 1]) * jnp.dot(pick, rows, preferred_element_type=F32)
        total = part if total is None else total + part
    out_ref[...] = total.astype(BF16)


def after(value, earlier):
    return lax.optimization_barrier((value, earlier))[0]


def shape(dims, kind=BF16):
    return jax.ShapeDtypeStruct(dims, kind)


def on_device(
    tokens,
    norm_gain,
    queries,
    attn_keys,
    attn_values,
    expert_ids,
    route_weights,
    gate_proj,
    up_proj,
    down_proj,
):
    exp_count = lax.axis_size("exp")
    seq_count = lax.axis_size("seq")
    local_tokens, features = tokens.shape
    exp_dev, hidden = gate_proj.shape[0], gate_proj.shape[1]
    chunks = CHUNKS
    experts = exp_dev // chunks
    step = experts * CAP
    group = exp_count // SEG_DEV
    seg_len = group * local_tokens
    segs = seq_count * SEG_DEV
    att = queries.shape[1]
    width = att // group

    block = seg_len // SUMS
    *send, sums = pl.pallas_call(
        functools.partial(prep_kernel, block),
        out_shape=[shape((exp_count, step, features))] * chunks
        + [shape((2 * local_tokens // block, att))],
        in_specs=[ANY, VMEM, VMEM, ANY, ANY],
        out_specs=[VMEM] * (chunks + 1),
        scratch_shapes=[
            pltpu.VMEM((local_tokens, features), BF16),
            pltpu.VMEM((local_tokens, att), BF16),
            pltpu.VMEM((local_tokens, att), BF16),
            pltpu.SemaphoreType.DMA((3,)),
        ],
        compiler_params=params(56),
        cost_estimate=LITTLE,
        name="prep",
    )(tokens, norm_gain.reshape(1, -1), expert_ids.T, attn_keys, attn_values)

    def device(segment, j):
        return (segment // SEG_DEV) * exp_count + (segment % SEG_DEV) * group + j

    parts = [sums]
    for other in range(1, segs):
        pairs = []
        for segment in range(segs):
            for j in range(group):
                pairs.append((device(segment, j), device(segment ^ other, j)))
        parts.append(lax.ppermute(sums, ("seq", "exp"), pairs))
    packed_rows = 3 * local_tokens + segs * 2 * local_tokens // block
    packed = pl.pallas_call(
        pack_kernel,
        out_shape=shape((group, packed_rows, width)),
        in_specs=[ANY] * 3 + [VMEM] * segs,
        out_specs=VMEM,
        scratch_shapes=[pltpu.SemaphoreType.DMA((3 * group,))],
        compiler_params=params(56),
        cost_estimate=LITTLE,
        name="pack",
    )(queries, attn_keys, attn_values, *parts)
    recv = [lax.all_to_all(send[0], "exp", 0, 0, tiled=True)]
    recv[0] = after(recv[0], parts)
    for rows in send[1:]:
        recv.append(lax.all_to_all(after(rows, recv[-1]), "exp", 0, 0, tiled=True))
    arrived = []
    for rows in recv:
        planes = [rows]
        for other in range(1, seq_count):
            pairs = [(i, i ^ other) for i in range(seq_count)]
            planes.append(lax.ppermute(rows, "seq", pairs))
        arrived.append(planes)
    segment = lax.axis_index("seq") * SEG_DEV + lax.axis_index("exp") // group
    place = lax.axis_index("exp") % group
    position = jnp.stack([segment, place]).astype(jnp.int32)
    done, mine = [], []
    for chunk in range(chunks):
        planes = [after(arrived[chunk][0], recv[-1])] + arrived[chunk][1:]
        total = seq_count * exp_count * step
        pieces = pl.pallas_call(
            functools.partial(ffn_kernel, chunk * experts, seq_count),
            out_shape=[shape((exp_count, step, features))] * seq_count,
            in_specs=[VMEM] * seq_count + [ANY] * 3,
            out_specs=[VMEM] * seq_count,
            scratch_shapes=[
                pltpu.VMEM((experts * 3, hidden, features), BF16),
                pltpu.VMEM((total, features), BF16),
                pltpu.VMEM((total, features), F32),
                pltpu.SemaphoreType.DMA((experts * 3,)),
            ],
            compiler_params=params(44),
            cost_estimate=LITTLE,
            name="experts",
        )(*planes, gate_proj, up_proj, down_proj)
        done.append(pieces)
    packed = after(packed, done[0][0])
    halves = [[half * group + j for j in range(group)] for half in range(SEG_DEV)]
    got = lax.all_to_all(packed, "exp", 0, 0, axis_index_groups=halves, tiled=True)
    for chunk, pieces in enumerate(done):
        summed = after(after(pieces[0], done[-1][0]), got).astype(F32)
        for other in range(1, seq_count):
            pairs = [(i, i ^ other) for i in range(seq_count)]
            summed = summed + lax.ppermute(pieces[other], "seq", pairs).astype(F32)
        mine.append(summed.astype(BF16))
    got = after(got, mine[0])
    head_out = pl.pallas_call(
        functools.partial(attend_kernel, min(256, seg_len), local_tokens, segs),
        out_shape=[shape((local_tokens, width))] * group,
        in_specs=[SMEM, VMEM],
        out_specs=[VMEM] * group,
        scratch_shapes=[pltpu.VMEM((group, local_tokens, width), BF16)],
        compiler_params=params(48),
        cost_estimate=LITTLE,
        name="attend",
    )(position, got)
    heads = [
        rows
        if other == 0
        else lax.ppermute(rows, "exp", [(i, i ^ other) for i in range(exp_count)])
        for other, rows in enumerate(head_out)
    ]
    attention = pl.pallas_call(
        place_kernel,
        out_shape=shape((local_tokens, att)),
        in_specs=[SMEM] + [VMEM] * group,
        out_specs=VMEM,
        compiler_params=params(32),
        cost_estimate=LITTLE,
        name="place",
    )(position, *heads)

    mine[-1] = after(mine[-1], heads[1:4])
    back = [lax.all_to_all(rows, "exp", 0, 0, tiled=True) for rows in mine]
    expert_mix = pl.pallas_call(
        mix_kernel,
        out_shape=shape((local_tokens, features)),
        in_specs=[VMEM] * (2 + chunks),
        out_specs=VMEM,
        scratch_shapes=[pltpu.VMEM((EXPERTS * CAP, features), F32)],
        compiler_params=params(32),
        cost_estimate=LITTLE,
        name="mix",
    )(expert_ids.T, route_weights.T, *back)
    return (attention, expert_mix)


def solution(mesh):
    return jax.shard_map(
        on_device,
        mesh=mesh,
        in_specs=(
            P(("seq", "exp"), None),
            P(),
            P(("seq", "exp"), None),
            P(("seq", "exp"), None),
            P(("seq", "exp"), None),
            P(("seq", "exp"), None),
            P(("seq", "exp"), None),
            P("exp", "seq", None),
            P("exp", "seq", None),
            P("exp", "seq", None),
        ),
        out_specs=(P(("seq", "exp"), None), P(("seq", "exp"), None)),
        check_vma=False,
    )
```

```python
import functools
import math

import jax
import jax.numpy as jnp
from jax import lax
from jax.experimental import pallas as pl
from jax.experimental.pallas import tpu as pltpu
from jax.sharding import PartitionSpec as P

EXPERTS = 64
HDIM = 64
SUMS = 64
SEG_DEV = 2
CAP = 2
CHUNKS = 2

EPS = 1e-05
NEG = -1e30
F32 = jnp.float32
BF16 = jnp.bfloat16

VMEM = pl.BlockSpec(memory_space=pltpu.VMEM)
ANY = pl.BlockSpec(memory_space=pl.ANY)
LITTLE = pl.CostEstimate(flops=1000, bytes_accessed=1000, transcendentals=0)
SMEM = pl.BlockSpec(memory_space=pltpu.SMEM)


def params(mib):
    return pltpu.CompilerParams(vmem_limit_bytes=mib * 2**20)


def as_column(row):
    n = row.shape[1]
    eye = lax.broadcasted_iota(jnp.int32, (n, n), 0) == lax.broadcasted_iota(jnp.int32, (n, n), 1)
    return jnp.sum(jnp.where(eye, row, jnp.zeros((), row.dtype)), axis=1, keepdims=True)


def slots(ids):
    n = ids.shape[1]
    rows = [ids[0:1], ids[1:2]]
    columns = [as_column(row) for row in rows]
    earlier = lax.broadcasted_iota(jnp.int32, (n, n), 0) < lax.broadcasted_iota(jnp.int32, (n, n), 1)
    found = []
    for row in rows:
        same = (columns[0] == row) | (columns[1] == row)
        before = jnp.sum(jnp.where(same & earlier, 1, 0), axis=0, keepdims=True)
        found.append(row * CAP + before)
    return found


def prep_kernel(block, tok_hbm, gain_ref, ids_ref, k_hbm, v_hbm, *refs):
    out_refs, sum_ref, (tok_ref, k_ref, v_ref, sem) = refs[:-5], refs[-5], refs[-4:]
    copies = [
        pltpu.make_async_copy(frm, to, sem.at[at])
        for at, (frm, to) in enumerate(((tok_hbm, tok_ref), (k_hbm, k_ref), (v_hbm, v_ref)))
    ]
    for copy in copies:
        copy.start()
    n = tok_ref.shape[0]
    first, second = slots(ids_ref[...])
    place = lax.broadcasted_iota(jnp.int32, (EXPERTS * CAP, n), 0)
    pick = jnp.where((place == first) | (place == second), 1.0, 0.0).astype(BF16)
    copies[0].wait()
    values = tok_ref[...].astype(F32)
    inv_rms = lax.rsqrt(jnp.mean(values * values, axis=-1, keepdims=True) + EPS)
    normed = (values * inv_rms * gain_ref[...]).astype(BF16)
    rows = jnp.dot(pick, normed, preferred_element_type=F32)
    dests, step = out_refs[0].shape[0], out_refs[0].shape[1]
    for dest in range(dests):
        for chunk, out_ref in enumerate(out_refs):
            lower = (dest * len(out_refs) + chunk) * step
            out_ref[dest] = rows[lower : lower + step].astype(BF16)
    count = n // block
    row = lax.broadcasted_iota(jnp.int32, (count, n), 0)
    column = lax.broadcasted_iota(jnp.int32, (count, n), 1)
    member = jnp.where(column // block == row, 1.0, 0.0).astype(BF16)
    for which, ref in enumerate((k_ref, v_ref)):
        copies[which + 1].wait()
        summed = jnp.dot(member, ref[...], preferred_element_type=F32) * (1.0 / math.sqrt(block))
        sum_ref[which * count : (which + 1) * count] = summed.astype(BF16)


def pack_kernel(q_hbm, k_hbm, v_hbm, *refs):
    sum_refs, out_ref, sem = refs[:-2], refs[-2], refs[-1]
    dests, _, width = out_ref.shape
    tokens = q_hbm.shape[0]
    copies = []
    for dest in range(dests):
        for which, ref in enumerate((q_hbm, k_hbm, v_hbm)):
            copies.append(
                pltpu.make_async_copy(
                    ref.at[:, pl.ds(dest * width, width)],
                    out_ref.at[dest, pl.ds(which * tokens, tokens)],
                    sem.at[dest * 3 + which],
                )
            )
    for copy in copies:
        copy.start()
    for dest in range(dests):
        lower = 3 * tokens
        for ref in sum_refs:
            upper = lower + ref.shape[0]
            out_ref[dest, lower:upper] = ref[:, dest * width : (dest + 1) * width]
            lower = upper
    for copy in copies:
        copy.wait()


def attend_kernel(query_rows, tokens, segs, at_ref, recv_ref, *refs):
    out_refs, mixed_ref = refs[:-1], refs[-1]
    sources, _, width = recv_ref.shape
    seg_len = sources * tokens
    query, key, value = (
        recv_ref[:, which * tokens : (which + 1) * tokens].reshape(seg_len, width) for which in range(3)
    )
    sum_total = segs * SUMS
    per = SUMS // sources
    sum_rows = [
        recv_ref[:, 3 * tokens + at * per : 3 * tokens + (at + 1) * per].reshape(SUMS, width)
        for at in range(2 * segs)
    ]
    sum_keys = jnp.concatenate(sum_rows[0::2], axis=0)
    sum_values = jnp.concatenate(sum_rows[1::2], axis=0)
    scale = 1.0 / math.sqrt(HDIM)
    segment = at_ref[0]
    lane = lax.broadcasted_iota(jnp.int32, (1, width), 1)
    nt = (((1,), (1,)), ((), ()))
    for first in range(0, seg_len, query_rows):
        last = first + query_rows
        local_ok = (
            lax.broadcasted_iota(jnp.int32, (query_rows, last), 1)
            <= lax.broadcasted_iota(jnp.int32, (query_rows, last), 0) + first
        )
        summ_seg = lax.broadcasted_iota(jnp.int32, (query_rows, sum_total), 1) // SUMS
        summ_ok = jnp.bitwise_xor(summ_seg, segment) < segment
        mixed = jnp.zeros((query_rows, width), F32)
        for head in range(width // HDIM):
            mine = (lane >= head * HDIM) & (lane < (head + 1) * HDIM)
            rows = jnp.where(mine, query[first:last], jnp.zeros((), BF16))
            local_sc = lax.dot_general(rows, key[:last], nt, preferred_element_type=F32) * scale
            summ_sc = lax.dot_general(rows, sum_keys, nt, preferred_element_type=F32) * scale
            local_sc = jnp.where(local_ok, local_sc, NEG)
            summ_sc = jnp.where(summ_ok, summ_sc, NEG)
            top = jnp.maximum(
                jnp.max(local_sc, axis=-1, keepdims=True), jnp.max(summ_sc, axis=-1, keepdims=True)
            )
            local_ex = jnp.exp(local_sc - top)
            summ_ex = jnp.exp(summ_sc - top)
            inv = 1.0 / (
                jnp.sum(local_ex, axis=-1, keepdims=True) + jnp.sum(summ_ex, axis=-1, keepdims=True)
            )
            got = jnp.dot((local_ex * inv).astype(BF16), value[:last], preferred_element_type=F32)
            got += jnp.dot((summ_ex * inv).astype(BF16), sum_values, preferred_element_type=F32)
            mixed = jnp.where(mine, got, mixed)
        for source in range(first // tokens, last // tokens):
            lower = source * tokens - first
            mixed_ref[source] = mixed[lower : lower + tokens].astype(BF16)
    for other, out_ref in enumerate(out_refs):
        out_ref[...] = mixed_ref[jnp.bitwise_xor(at_ref[1], other)]


def place_kernel(at_ref, *refs):
    in_refs, out_ref = refs[:-1], refs[-1]
    width = in_refs[0].shape[1]
    for other, ref in enumerate(in_refs):
        lower = pl.multiple_of(jnp.bitwise_xor(at_ref[1], other) * width, width)
        out_ref[:, pl.ds(lower, width)] = ref[...]


def ffn_kernel(base, planes, *refs):
    row_refs, (gate_ref, up_ref, down_ref) = refs[:planes], refs[planes : planes + 3]
    out_refs = refs[planes + 3 : 2 * planes + 3]
    buf, x_ref, y_ref, sem = refs[2 * planes + 3 :]
    sources, step, width = row_refs[0].shape
    experts = step // CAP
    copies = []
    for expert in range(experts):
        for which, ref in enumerate((gate_ref, up_ref, down_ref)):
            at = expert * 3 + which
            copy = pltpu.make_async_copy(ref.at[base + expert], buf.at[at], sem.at[at])
            copy.start()
            copies.append(copy)
    total = planes * sources * step
    for plane in range(planes):
        for source in range(sources):
            lower = (plane * sources + source) * step
            y_ref[lower : lower + step] = row_refs[plane][source].astype(F32)
    to = lax.broadcasted_iota(jnp.int32, (total, total), 0)
    frm = lax.broadcasted_iota(jnp.int32, (total, total), 1)
    per = total // experts
    order = (to % per // CAP) * step + (to // per) * CAP + to % CAP
    sort = jnp.where(frm == order, 1.0, 0.0).astype(BF16)
    x_ref[...] = jnp.dot(sort, y_ref[...].astype(BF16), preferred_element_type=F32).astype(BF16)
    nt = (((1,), (1,)), ((), ()))
    for expert in range(experts):
        rows = x_ref[expert * per : (expert + 1) * per]
        copies[expert * 3].wait()
        gate = lax.dot_general(rows, buf[expert * 3], nt, preferred_element_type=F32)
        copies[expert * 3 + 1].wait()
        up = lax.dot_general(rows, buf[expert * 3 + 1], nt, preferred_element_type=F32)
        hidden = (gate / (1.0 + jnp.exp(-gate)) * up).astype(BF16)
        copies[expert * 3 + 2].wait()
        piece = jnp.dot(hidden, buf[expert * 3 + 2], preferred_element_type=F32)
        x_ref[expert * per : (expert + 1) * per] = piece.astype(BF16)
    inverse = (to // step) * CAP + (to % step // CAP) * per + to % CAP
    unsort = jnp.where(frm == inverse, 1.0, 0.0).astype(BF16)
    y_ref[...] = jnp.dot(unsort, x_ref[...], preferred_element_type=F32)
    for plane in range(planes):
        for source in range(sources):
            lower = (plane * sources + source) * step
            out_refs[plane][source] = y_ref[lower : lower + step].astype(BF16)


def mix_kernel(ids_ref, weight_ref, *refs):
    in_refs, out_ref, y_ref = refs[:-2], refs[-2], refs[-1]
    dests, step = in_refs[0].shape[0], in_refs[0].shape[1]
    for dest in range(dests):
        for chunk, ref in enumerate(in_refs):
            lower = (dest * len(in_refs) + chunk) * step
            y_ref[lower : lower + step] = ref[dest].astype(F32)
    rows = y_ref[...].astype(BF16)
    n = ids_ref.shape[1]
    place = lax.broadcasted_iota(jnp.int32, (n, EXPERTS * CAP), 1)
    total = None
    for k, row in enumerate(slots(ids_ref[...])):
        pick = jnp.where(place == as_column(row), 1.0, 0.0).astype(BF16)
        part = as_column(weight_ref[k : k + 1]) * jnp.dot(pick, rows, preferred_element_type=F32)
        total = part if total is None else total + part
    out_ref[...] = total.astype(BF16)


def after(value, earlier):
    return lax.optimization_barrier((value, earlier))[0]


def shape(dims, kind=BF16):
    return jax.ShapeDtypeStruct(dims, kind)


def on_device(
    tokens,
    norm_gain,
    queries,
    attn_keys,
    attn_values,
    expert_ids,
    route_weights,
    gate_proj,
    up_proj,
    down_proj,
):
    exp_count = lax.axis_size("exp")
    seq_count = lax.axis_size("seq")
    local_tokens, features = tokens.shape
    exp_dev, hidden = gate_proj.shape[0], gate_proj.shape[1]
    chunks = CHUNKS
    experts = exp_dev // chunks
    step = experts * CAP
    group = exp_count // SEG_DEV
    seg_len = group * local_tokens
    segs = seq_count * SEG_DEV
    att = queries.shape[1]
    width = att // group

    block = seg_len // SUMS
    *send, sums = pl.pallas_call(
        functools.partial(prep_kernel, block),
        out_shape=[shape((exp_count, step, features))] * chunks
        + [shape((2 * local_tokens // block, att))],
        in_specs=[ANY, VMEM, VMEM, ANY, ANY],
        out_specs=[VMEM] * (chunks + 1),
        scratch_shapes=[
            pltpu.VMEM((local_tokens, features), BF16),
            pltpu.VMEM((local_tokens, att), BF16),
            pltpu.VMEM((local_tokens, att), BF16),
            pltpu.SemaphoreType.DMA((3,)),
        ],
        compiler_params=params(56),
        cost_estimate=LITTLE,
        name="prep",
    )(tokens, norm_gain.reshape(1, -1), expert_ids.T, attn_keys, attn_values)

    def device(segment, j):
        return (segment // SEG_DEV) * exp_count + (segment % SEG_DEV) * group + j

    parts = [sums]
    for other in range(1, segs):
        pairs = []
        for segment in range(segs):
            for j in range(group):
                pairs.append((device(segment, j), device(segment ^ other, j)))
        parts.append(lax.ppermute(sums, ("seq", "exp"), pairs))
    packed_rows = 3 * local_tokens + segs * 2 * local_tokens // block
    packed = pl.pallas_call(
        pack_kernel,
        out_shape=shape((group, packed_rows, width)),
        in_specs=[ANY] * 3 + [VMEM] * segs,
        out_specs=VMEM,
        scratch_shapes=[pltpu.SemaphoreType.DMA((3 * group,))],
        compiler_params=params(56),
        cost_estimate=LITTLE,
        name="pack",
    )(queries, attn_keys, attn_values, *parts)
    recv = [lax.all_to_all(send[0], "exp", 0, 0, tiled=True)]
    for rows in send[1:]:
        recv.append(lax.all_to_all(after(rows, recv[-1]), "exp", 0, 0, tiled=True))
    arrived = []
    for rows in recv:
        planes = [rows]
        for other in range(1, seq_count):
            pairs = [(i, i ^ other) for i in range(seq_count)]
            planes.append(lax.ppermute(rows, "seq", pairs))
        arrived.append(planes)
    segment = lax.axis_index("seq") * SEG_DEV + lax.axis_index("exp") // group
    place = lax.axis_index("exp") % group
    position = jnp.stack([segment, place]).astype(jnp.int32)
    done, mine = [], []
    for chunk in range(chunks):
        planes = [after(after(arrived[chunk][0], recv[-1]), parts)] + arrived[chunk][1:]
        total = seq_count * exp_count * step
        pieces = pl.pallas_call(
            functools.partial(ffn_kernel, chunk * experts, seq_count),
            out_shape=[shape((exp_count, step, features))] * seq_count,
            in_specs=[VMEM] * seq_count + [ANY] * 3,
            out_specs=[VMEM] * seq_count,
            scratch_shapes=[
                pltpu.VMEM((experts * 3, hidden, features), BF16),
                pltpu.VMEM((total, features), BF16),
                pltpu.VMEM((total, features), F32),
                pltpu.SemaphoreType.DMA((experts * 3,)),
            ],
            compiler_params=params(44),
            cost_estimate=pl.CostEstimate(
                flops=6 * total * hidden * features,
                bytes_accessed=3 * experts * 3 * hidden * features * 2,
                transcendentals=total * hidden,
            ),
            name="experts",
        )(*planes, gate_proj, up_proj, down_proj)
        done.append(pieces)
    packed = after(packed, recv[-1])
    halves = [[half * group + j for j in range(group)] for half in range(SEG_DEV)]
    got = lax.all_to_all(packed, "exp", 0, 0, axis_index_groups=halves, tiled=True)
    for chunk, pieces in enumerate(done):
        summed = after(after(pieces[0], done[-1][0]), got).astype(F32)
        for other in range(1, seq_count):
            pairs = [(i, i ^ other) for i in range(seq_count)]
            summed = summed + lax.ppermute(pieces[other], "seq", pairs).astype(F32)
        mine.append(summed.astype(BF16))
    got = after(got, mine[0])
    head_out = pl.pallas_call(
        functools.partial(attend_kernel, min(256, seg_len), local_tokens, segs),
        out_shape=[shape((local_tokens, width))] * group,
        in_specs=[SMEM, VMEM],
        out_specs=[VMEM] * group,
        scratch_shapes=[pltpu.VMEM((group, local_tokens, width), BF16)],
        compiler_params=params(48),
        cost_estimate=LITTLE,
        name="attend",
    )(position, got)
    heads = [
        rows
        if other == 0
        else lax.ppermute(rows, "exp", [(i, i ^ other) for i in range(exp_count)])
        for other, rows in enumerate(head_out)
    ]
    attention = pl.pallas_call(
        place_kernel,
        out_shape=shape((local_tokens, att)),
        in_specs=[SMEM] + [VMEM] * group,
        out_specs=VMEM,
        compiler_params=params(32),
        cost_estimate=LITTLE,
        name="place",
    )(position, *heads)

    mine[-1] = after(mine[-1], heads[1:4])
    back = [lax.all_to_all(rows, "exp", 0, 0, tiled=True) for rows in mine]
    expert_mix = pl.pallas_call(
        mix_kernel,
        out_shape=shape((local_tokens, features)),
        in_specs=[VMEM] * (2 + chunks),
        out_specs=VMEM,
        scratch_shapes=[pltpu.VMEM((EXPERTS * CAP, features), F32)],
        compiler_params=params(32),
        cost_estimate=LITTLE,
        name="mix",
    )(expert_ids.T, route_weights.T, *back)
    return (attention, expert_mix)


def solution(mesh):
    return jax.shard_map(
        on_device,
        mesh=mesh,
        in_specs=(
            P(("seq", "exp"), None),
            P(),
            P(("seq", "exp"), None),
            P(("seq", "exp"), None),
            P(("seq", "exp"), None),
            P(("seq", "exp"), None),
            P(("seq", "exp"), None),
            P("exp", "seq", None),
            P("exp", "seq", None),
            P("exp", "seq", None),
        ),
        out_specs=(P(("seq", "exp"), None), P(("seq", "exp"), None)),
        check_vma=False,
    )
```

```python
import functools
import math

import jax
import jax.numpy as jnp
from jax import lax
from jax.experimental import pallas as pl
from jax.experimental.pallas import tpu as pltpu
from jax.sharding import PartitionSpec as P

EXPERTS = 64
HDIM = 64
SUMS = 64
SEG_DEV = 2
CAP = 2
CHUNKS = 2
FLIGHT = 2

EPS = 1e-05
NEG = -1e30
F32 = jnp.float32
BF16 = jnp.bfloat16

VMEM = pl.BlockSpec(memory_space=pltpu.VMEM)
ANY = pl.BlockSpec(memory_space=pl.ANY)
LITTLE = pl.CostEstimate(flops=1000, bytes_accessed=1000, transcendentals=0)
SMEM = pl.BlockSpec(memory_space=pltpu.SMEM)


def params(mib):
    return pltpu.CompilerParams(vmem_limit_bytes=mib * 2**20)


def as_column(row):
    n = row.shape[1]
    eye = lax.broadcasted_iota(jnp.int32, (n, n), 0) == lax.broadcasted_iota(jnp.int32, (n, n), 1)
    return jnp.sum(jnp.where(eye, row, jnp.zeros((), row.dtype)), axis=1, keepdims=True)


def slots(ids):
    n = ids.shape[1]
    rows = [ids[0:1], ids[1:2]]
    columns = [as_column(row) for row in rows]
    earlier = lax.broadcasted_iota(jnp.int32, (n, n), 0) < lax.broadcasted_iota(jnp.int32, (n, n), 1)
    found = []
    for row in rows:
        same = (columns[0] == row) | (columns[1] == row)
        before = jnp.sum(jnp.where(same & earlier, 1, 0), axis=0, keepdims=True)
        found.append(row * CAP + before)
    return found


def prep_kernel(tok_hbm, gain_ref, ids_ref, *refs):
    out_refs, (tok_ref, sem) = refs[:-2], refs[-2:]
    copy = pltpu.make_async_copy(tok_hbm, tok_ref, sem.at[0])
    copy.start()
    n = tok_ref.shape[0]
    first, second = slots(ids_ref[...])
    place = lax.broadcasted_iota(jnp.int32, (EXPERTS * CAP, n), 0)
    pick = jnp.where((place == first) | (place == second), 1.0, 0.0).astype(BF16)
    copy.wait()
    values = tok_ref[...].astype(F32)
    inv_rms = lax.rsqrt(jnp.mean(values * values, axis=-1, keepdims=True) + EPS)
    normed = (values * inv_rms * gain_ref[...]).astype(BF16)
    rows = jnp.dot(pick, normed, preferred_element_type=F32)
    dests, step = out_refs[0].shape[0], out_refs[0].shape[1]
    for dest in range(dests):
        for chunk, out_ref in enumerate(out_refs):
            lower = (dest * len(out_refs) + chunk) * step
            out_ref[dest] = rows[lower : lower + step].astype(BF16)


def sums_kernel(block, recv_ref, out_ref):
    sources, rows, width = recv_ref.shape
    tokens = rows // 3
    total = sources * tokens
    row = lax.broadcasted_iota(jnp.int32, (SUMS, total), 0)
    column = lax.broadcasted_iota(jnp.int32, (SUMS, total), 1)
    member = jnp.where(column // block == row, 1.0, 0.0).astype(BF16)
    for which in range(2):
        values = recv_ref[:, (which + 1) * tokens : (which + 2) * tokens].reshape(total, width)
        summed = jnp.dot(member, values, preferred_element_type=F32) * (1.0 / math.sqrt(block))
        out_ref[which * SUMS : (which + 1) * SUMS] = summed.astype(BF16)


def pack_kernel(q_hbm, k_hbm, v_hbm, out_ref, sem):
    dests, _, width = out_ref.shape
    tokens = q_hbm.shape[0]
    copies = []
    for dest in range(dests):
        for which, ref in enumerate((q_hbm, k_hbm, v_hbm)):
            copies.append(
                pltpu.make_async_copy(
                    ref.at[:, pl.ds(dest * width, width)],
                    out_ref.at[dest, pl.ds(which * tokens, tokens)],
                    sem.at[dest * 3 + which],
                )
            )
    for copy in copies:
        copy.start()
    for copy in copies:
        copy.wait()


def attend_kernel(query_rows, tokens, segs, at_ref, recv_ref, *refs):
    sum_refs, out_refs, mixed_ref = refs[:segs], refs[segs:-1], refs[-1]
    sources, _, width = recv_ref.shape
    seg_len = sources * tokens
    query, key, value = (
        recv_ref[:, which * tokens : (which + 1) * tokens].reshape(seg_len, width) for which in range(3)
    )
    sum_total = segs * SUMS
    sum_keys = jnp.concatenate([ref[:SUMS] for ref in sum_refs], axis=0)
    sum_values = jnp.concatenate([ref[SUMS:] for ref in sum_refs], axis=0)
    scale = 1.0 / math.sqrt(HDIM)
    segment = at_ref[0]
    lane = lax.broadcasted_iota(jnp.int32, (1, width), 1)
    nt = (((1,), (1,)), ((), ()))
    for first in range(0, seg_len, query_rows):
        last = first + query_rows
        local_ok = (
            lax.broadcasted_iota(jnp.int32, (query_rows, last), 1)
            <= lax.broadcasted_iota(jnp.int32, (query_rows, last), 0) + first
        )
        summ_seg = lax.broadcasted_iota(jnp.int32, (query_rows, sum_total), 1) // SUMS
        summ_ok = jnp.bitwise_xor(summ_seg, segment) < segment
        mixed = jnp.zeros((query_rows, width), F32)
        for head in range(width // HDIM):
            mine = (lane >= head * HDIM) & (lane < (head + 1) * HDIM)
            rows = jnp.where(mine, query[first:last], jnp.zeros((), BF16))
            local_sc = lax.dot_general(rows, key[:last], nt, preferred_element_type=F32) * scale
            summ_sc = lax.dot_general(rows, sum_keys, nt, preferred_element_type=F32) * scale
            local_sc = jnp.where(local_ok, local_sc, NEG)
            summ_sc = jnp.where(summ_ok, summ_sc, NEG)
            top = jnp.maximum(
                jnp.max(local_sc, axis=-1, keepdims=True), jnp.max(summ_sc, axis=-1, keepdims=True)
            )
            local_ex = jnp.exp(local_sc - top)
            summ_ex = jnp.exp(summ_sc - top)
            inv = 1.0 / (
                jnp.sum(local_ex, axis=-1, keepdims=True) + jnp.sum(summ_ex, axis=-1, keepdims=True)
            )
            got = jnp.dot((local_ex * inv).astype(BF16), value[:last], preferred_element_type=F32)
            got += jnp.dot((summ_ex * inv).astype(BF16), sum_values, preferred_element_type=F32)
            mixed = jnp.where(mine, got, mixed)
        for source in range(first // tokens, last // tokens):
            lower = source * tokens - first
            mixed_ref[source] = mixed[lower : lower + tokens].astype(BF16)
    for other, out_ref in enumerate(out_refs):
        out_ref[...] = mixed_ref[jnp.bitwise_xor(at_ref[1], other)]


def place_kernel(at_ref, *refs):
    in_refs, out_ref = refs[:-1], refs[-1]
    width = in_refs[0].shape[1]
    for other, ref in enumerate(in_refs):
        lower = pl.multiple_of(jnp.bitwise_xor(at_ref[1], other) * width, width)
        out_ref[:, pl.ds(lower, width)] = ref[...]


def ffn_kernel(base, planes, *refs):
    row_refs, (gate_ref, up_ref, down_ref) = refs[:planes], refs[planes : planes + 3]
    out_refs = refs[planes + 3 : 2 * planes + 3]
    buf, x_ref, y_ref, sem = refs[2 * planes + 3 :]
    sources, step, width = row_refs[0].shape
    experts = step // CAP
    copies = []
    for expert in range(experts):
        for which, ref in enumerate((gate_ref, up_ref, down_ref)):
            at = expert * 3 + which
            copy = pltpu.make_async_copy(ref.at[base + expert], buf.at[at], sem.at[at])
            copies.append(copy)
    for copy in copies[:FLIGHT]:
        copy.start()

    def weight(at):
        copies[at].wait()
        if at + FLIGHT < len(copies):
            copies[at + FLIGHT].start()
        return buf[at]

    total = planes * sources * step
    for plane in range(planes):
        for source in range(sources):
            lower = (plane * sources + source) * step
            y_ref[lower : lower + step] = row_refs[plane][source].astype(F32)
    to = lax.broadcasted_iota(jnp.int32, (total, total), 0)
    frm = lax.broadcasted_iota(jnp.int32, (total, total), 1)
    per = total // experts
    order = (to % per // CAP) * step + (to // per) * CAP + to % CAP
    sort = jnp.where(frm == order, 1.0, 0.0).astype(BF16)
    x_ref[...] = jnp.dot(sort, y_ref[...].astype(BF16), preferred_element_type=F32).astype(BF16)
    nt = (((1,), (1,)), ((), ()))
    for expert in range(experts):
        rows = x_ref[expert * per : (expert + 1) * per]
        gate = lax.dot_general(rows, weight(expert * 3), nt, preferred_element_type=F32)
        up = lax.dot_general(rows, weight(expert * 3 + 1), nt, preferred_element_type=F32)
        hidden = (gate / (1.0 + jnp.exp(-gate)) * up).astype(BF16)
        piece = jnp.dot(hidden, weight(expert * 3 + 2), preferred_element_type=F32)
        x_ref[expert * per : (expert + 1) * per] = piece.astype(BF16)
    inverse = (to // step) * CAP + (to % step // CAP) * per + to % CAP
    unsort = jnp.where(frm == inverse, 1.0, 0.0).astype(BF16)
    y_ref[...] = jnp.dot(unsort, x_ref[...], preferred_element_type=F32)
    for plane in range(planes):
        for source in range(sources):
            lower = (plane * sources + source) * step
            out_refs[plane][source] = y_ref[lower : lower + step].astype(BF16)


def mix_kernel(ids_ref, weight_ref, *refs):
    in_refs, out_ref, y_ref = refs[:-2], refs[-2], refs[-1]
    dests, step = in_refs[0].shape[0], in_refs[0].shape[1]
    for dest in range(dests):
        for chunk, ref in enumerate(in_refs):
            lower = (dest * len(in_refs) + chunk) * step
            y_ref[lower : lower + step] = ref[dest].astype(F32)
    rows = y_ref[...].astype(BF16)
    n = ids_ref.shape[1]
    place = lax.broadcasted_iota(jnp.int32, (n, EXPERTS * CAP), 1)
    total = None
    for k, row in enumerate(slots(ids_ref[...])):
        pick = jnp.where(place == as_column(row), 1.0, 0.0).astype(BF16)
        part = as_column(weight_ref[k : k + 1]) * jnp.dot(pick, rows, preferred_element_type=F32)
        total = part if total is None else total + part
    out_ref[...] = total.astype(BF16)


def after(value, earlier):
    return lax.optimization_barrier((value, earlier))[0]


def shape(dims, kind=BF16):
    return jax.ShapeDtypeStruct(dims, kind)


def on_device(
    tokens,
    norm_gain,
    queries,
    attn_keys,
    attn_values,
    expert_ids,
    route_weights,
    gate_proj,
    up_proj,
    down_proj,
):
    exp_count = lax.axis_size("exp")
    seq_count = lax.axis_size("seq")
    local_tokens, features = tokens.shape
    exp_dev, hidden = gate_proj.shape[0], gate_proj.shape[1]
    chunks = CHUNKS
    experts = exp_dev // chunks
    step = experts * CAP
    group = exp_count // SEG_DEV
    seg_len = group * local_tokens
    segs = seq_count * SEG_DEV
    att = queries.shape[1]
    width = att // group

    send = pl.pallas_call(
        prep_kernel,
        out_shape=[shape((exp_count, step, features))] * chunks,
        in_specs=[ANY, VMEM, VMEM],
        out_specs=[VMEM] * chunks,
        scratch_shapes=[pltpu.VMEM((local_tokens, features), BF16), pltpu.SemaphoreType.DMA((1,))],
        compiler_params=params(56),
        cost_estimate=LITTLE,
        name="prep",
    )(tokens, norm_gain.reshape(1, -1), expert_ids.T)

    def device(segment, j):
        return (segment // SEG_DEV) * exp_count + (segment % SEG_DEV) * group + j

    packed = pl.pallas_call(
        pack_kernel,
        out_shape=shape((group, 3 * local_tokens, width)),
        in_specs=[ANY] * 3,
        out_specs=VMEM,
        scratch_shapes=[pltpu.SemaphoreType.DMA((3 * group,))],
        compiler_params=params(56),
        cost_estimate=LITTLE,
        name="pack",
    )(queries, attn_keys, attn_values)
    recv = [lax.all_to_all(send[0], "exp", 0, 0, tiled=True)]
    for rows in send[1:]:
        recv.append(lax.all_to_all(after(rows, recv[-1]), "exp", 0, 0, tiled=True))
    arrived = []
    for rows in recv:
        planes = [rows]
        for other in range(1, seq_count):
            pairs = [(i, i ^ other) for i in range(seq_count)]
            planes.append(lax.ppermute(rows, "seq", pairs))
        arrived.append(planes)
    segment = lax.axis_index("seq") * SEG_DEV + lax.axis_index("exp") // group
    place = lax.axis_index("exp") % group
    position = jnp.stack([segment, place]).astype(jnp.int32)
    done, mine = [], []
    for chunk in range(chunks):
        planes = [after(arrived[chunk][0], recv[-1])] + arrived[chunk][1:]
        total = seq_count * exp_count * step
        pieces = pl.pallas_call(
            functools.partial(ffn_kernel, chunk * experts, seq_count),
            out_shape=[shape((exp_count, step, features))] * seq_count,
            in_specs=[VMEM] * seq_count + [ANY] * 3,
            out_specs=[VMEM] * seq_count,
            scratch_shapes=[
                pltpu.VMEM((experts * 3, hidden, features), BF16),
                pltpu.VMEM((total, features), BF16),
                pltpu.VMEM((total, features), F32),
                pltpu.SemaphoreType.DMA((experts * 3,)),
            ],
            compiler_params=params(44),
            cost_estimate=pl.CostEstimate(
                flops=6 * total * hidden * features,
                bytes_accessed=3 * experts * 3 * hidden * features * 2,
                transcendentals=total * hidden,
            ),
            name="experts",
        )(*planes, gate_proj, up_proj, down_proj)
        done.append(pieces)
    packed = after(after(packed, recv[-1]), arrived[0])
    halves = [[half * group + j for j in range(group)] for half in range(SEG_DEV)]
    got = lax.all_to_all(packed, "exp", 0, 0, axis_index_groups=halves, tiled=True)
    for chunk, pieces in enumerate(done):
        summed = after(after(pieces[0], done[-1][0]), got).astype(F32)
        for other in range(1, seq_count):
            pairs = [(i, i ^ other) for i in range(seq_count)]
            summed = summed + lax.ppermute(pieces[other], "seq", pairs).astype(F32)
        mine.append(summed.astype(BF16))
    got = after(got, mine[0])
    sums = pl.pallas_call(
        functools.partial(sums_kernel, seg_len // SUMS),
        out_shape=shape((2 * SUMS, width)),
        in_specs=[VMEM],
        out_specs=VMEM,
        compiler_params=params(32),
        cost_estimate=LITTLE,
        name="sums",
    )(got)
    parts = [sums]
    for other in range(1, segs):
        pairs = []
        for frm in range(segs):
            for j in range(group):
                pairs.append((device(frm, j), device(frm ^ other, j)))
        parts.append(lax.ppermute(sums, ("seq", "exp"), pairs))
    head_out = pl.pallas_call(
        functools.partial(attend_kernel, min(256, seg_len), local_tokens, segs),
        out_shape=[shape((local_tokens, width))] * group,
        in_specs=[SMEM, VMEM] + [VMEM] * segs,
        out_specs=[VMEM] * group,
        scratch_shapes=[pltpu.VMEM((group, local_tokens, width), BF16)],
        compiler_params=params(48),
        cost_estimate=LITTLE,
        name="attend",
    )(position, got, *parts)
    heads = [
        rows
        if other == 0
        else lax.ppermute(rows, "exp", [(i, i ^ other) for i in range(exp_count)])
        for other, rows in enumerate(head_out)
    ]
    attention = pl.pallas_call(
        place_kernel,
        out_shape=shape((local_tokens, att)),
        in_specs=[SMEM] + [VMEM] * group,
        out_specs=VMEM,
        compiler_params=params(32),
        cost_estimate=LITTLE,
        name="place",
    )(position, *heads)

    back = [lax.all_to_all(rows, "exp", 0, 0, tiled=True) for rows in mine]
    expert_mix = pl.pallas_call(
        mix_kernel,
        out_shape=shape((local_tokens, features)),
        in_specs=[VMEM] * (2 + chunks),
        out_specs=VMEM,
        scratch_shapes=[pltpu.VMEM((EXPERTS * CAP, features), F32)],
        compiler_params=params(32),
        cost_estimate=LITTLE,
        name="mix",
    )(expert_ids.T, route_weights.T, *back)
    return (attention, expert_mix)


def solution(mesh):
    return jax.shard_map(
        on_device,
        mesh=mesh,
        in_specs=(
            P(("seq", "exp"), None),
            P(),
            P(("seq", "exp"), None),
            P(("seq", "exp"), None),
            P(("seq", "exp"), None),
            P(("seq", "exp"), None),
            P(("seq", "exp"), None),
            P("exp", "seq", None),
            P("exp", "seq", None),
            P("exp", "seq", None),
        ),
        out_specs=(P(("seq", "exp"), None), P(("seq", "exp"), None)),
        check_vma=False,
    )
```

```python
import functools
import math

import jax
import jax.numpy as jnp
from jax import lax
from jax.experimental import pallas as pl
from jax.experimental.pallas import tpu as pltpu
from jax.sharding import PartitionSpec as P

EXPERTS = 64
HDIM = 64
SUMS = 64
SEG_DEV = 2
CAP = 2
CHUNKS = 2

EPS = 1e-05
NEG = -1e30
F32 = jnp.float32
BF16 = jnp.bfloat16

VMEM = pl.BlockSpec(memory_space=pltpu.VMEM)
ANY = pl.BlockSpec(memory_space=pl.ANY)
LITTLE = pl.CostEstimate(flops=1000, bytes_accessed=1000, transcendentals=0)
SMEM = pl.BlockSpec(memory_space=pltpu.SMEM)


def params(mib):
    return pltpu.CompilerParams(vmem_limit_bytes=mib * 2**20)


def as_column(row):
    n = row.shape[1]
    eye = lax.broadcasted_iota(jnp.int32, (n, n), 0) == lax.broadcasted_iota(jnp.int32, (n, n), 1)
    return jnp.sum(jnp.where(eye, row, jnp.zeros((), row.dtype)), axis=1, keepdims=True)


def slots(ids):
    n = ids.shape[1]
    rows = [ids[0:1], ids[1:2]]
    columns = [as_column(row) for row in rows]
    earlier = lax.broadcasted_iota(jnp.int32, (n, n), 0) < lax.broadcasted_iota(jnp.int32, (n, n), 1)
    found = []
    for row in rows:
        same = (columns[0] == row) | (columns[1] == row)
        before = jnp.sum(jnp.where(same & earlier, 1, 0), axis=0, keepdims=True)
        found.append(row * CAP + before)
    return found


def prep_kernel(block, tok_hbm, gain_ref, ids_ref, k_hbm, v_hbm, *refs):
    out_refs, sum_ref, (tok_ref, k_ref, v_ref, sem) = refs[:-5], refs[-5], refs[-4:]
    copies = [
        pltpu.make_async_copy(frm, to, sem.at[at])
        for at, (frm, to) in enumerate(((tok_hbm, tok_ref), (k_hbm, k_ref), (v_hbm, v_ref)))
    ]
    for copy in copies:
        copy.start()
    n = tok_ref.shape[0]
    first, second = slots(ids_ref[...])
    place = lax.broadcasted_iota(jnp.int32, (EXPERTS * CAP, n), 0)
    pick = jnp.where((place == first) | (place == second), 1.0, 0.0).astype(BF16)
    copies[0].wait()
    values = tok_ref[...].astype(F32)
    inv_rms = lax.rsqrt(jnp.mean(values * values, axis=-1, keepdims=True) + EPS)
    normed = (values * inv_rms * gain_ref[...]).astype(BF16)
    rows = jnp.dot(pick, normed, preferred_element_type=F32)
    dests, step = out_refs[0].shape[0], out_refs[0].shape[1]
    for dest in range(dests):
        for chunk, out_ref in enumerate(out_refs):
            lower = (dest * len(out_refs) + chunk) * step
            out_ref[dest] = rows[lower : lower + step].astype(BF16)
    count = n // block
    row = lax.broadcasted_iota(jnp.int32, (count, n), 0)
    column = lax.broadcasted_iota(jnp.int32, (count, n), 1)
    member = jnp.where(column // block == row, 1.0, 0.0).astype(BF16)
    for which, ref in enumerate((k_ref, v_ref)):
        copies[which + 1].wait()
        summed = jnp.dot(member, ref[...], preferred_element_type=F32) * (1.0 / math.sqrt(block))
        sum_ref[which * count : (which + 1) * count] = summed.astype(BF16)


def pack_kernel(q_hbm, k_hbm, v_hbm, *refs):
    sum_refs, out_ref, sem = refs[:-2], refs[-2], refs[-1]
    dests, _, width = out_ref.shape
    tokens = q_hbm.shape[0]
    copies = []
    for dest in range(dests):
        for which, ref in enumerate((q_hbm, k_hbm, v_hbm)):
            copies.append(
                pltpu.make_async_copy(
                    ref.at[:, pl.ds(dest * width, width)],
                    out_ref.at[dest, pl.ds(which * tokens, tokens)],
                    sem.at[dest * 3 + which],
                )
            )
    for copy in copies:
        copy.start()
    for dest in range(dests):
        lower = 3 * tokens
        for ref in sum_refs:
            upper = lower + ref.shape[0]
            out_ref[dest, lower:upper] = ref[:, dest * width : (dest + 1) * width]
            lower = upper
    for copy in copies:
        copy.wait()


def attend_kernel(query_rows, tokens, segs, at_ref, recv_ref, *refs):
    out_refs, mixed_ref = refs[:-1], refs[-1]
    sources, _, width = recv_ref.shape
    seg_len = sources * tokens
    query, key, value = (
        recv_ref[:, which * tokens : (which + 1) * tokens].reshape(seg_len, width) for which in range(3)
    )
    sum_total = segs * SUMS
    per = SUMS // sources
    sum_rows = [
        recv_ref[:, 3 * tokens + at * per : 3 * tokens + (at + 1) * per].reshape(SUMS, width)
        for at in range(2 * segs)
    ]
    sum_keys = jnp.concatenate(sum_rows[0::2], axis=0)
    sum_values = jnp.concatenate(sum_rows[1::2], axis=0)
    scale = 1.0 / math.sqrt(HDIM)
    segment = at_ref[0]
    lane = lax.broadcasted_iota(jnp.int32, (1, width), 1)
    nt = (((1,), (1,)), ((), ()))
    for first in range(0, seg_len, query_rows):
        last = first + query_rows
        local_ok = (
            lax.broadcasted_iota(jnp.int32, (query_rows, last), 1)
            <= lax.broadcasted_iota(jnp.int32, (query_rows, last), 0) + first
        )
        summ_seg = lax.broadcasted_iota(jnp.int32, (query_rows, sum_total), 1) // SUMS
        summ_ok = jnp.bitwise_xor(summ_seg, segment) < segment
        mixed = jnp.zeros((query_rows, width), F32)
        for head in range(width // HDIM):
            mine = (lane >= head * HDIM) & (lane < (head + 1) * HDIM)
            rows = jnp.where(mine, query[first:last], jnp.zeros((), BF16))
            local_sc = lax.dot_general(rows, key[:last], nt, preferred_element_type=F32) * scale
            summ_sc = lax.dot_general(rows, sum_keys, nt, preferred_element_type=F32) * scale
            local_sc = jnp.where(local_ok, local_sc, NEG)
            summ_sc = jnp.where(summ_ok, summ_sc, NEG)
            top = jnp.maximum(
                jnp.max(local_sc, axis=-1, keepdims=True), jnp.max(summ_sc, axis=-1, keepdims=True)
            )
            local_ex = jnp.exp(local_sc - top)
            summ_ex = jnp.exp(summ_sc - top)
            inv = 1.0 / (
                jnp.sum(local_ex, axis=-1, keepdims=True) + jnp.sum(summ_ex, axis=-1, keepdims=True)
            )
            got = jnp.dot((local_ex * inv).astype(BF16), value[:last], preferred_element_type=F32)
            got += jnp.dot((summ_ex * inv).astype(BF16), sum_values, preferred_element_type=F32)
            mixed = jnp.where(mine, got, mixed)
        for source in range(first // tokens, last // tokens):
            lower = source * tokens - first
            mixed_ref[source] = mixed[lower : lower + tokens].astype(BF16)
    for other, out_ref in enumerate(out_refs):
        out_ref[...] = mixed_ref[jnp.bitwise_xor(at_ref[1], other)]


def place_kernel(at_ref, *refs):
    in_refs, out_ref = refs[:-1], refs[-1]
    width = in_refs[0].shape[1]
    for other, ref in enumerate(in_refs):
        lower = pl.multiple_of(jnp.bitwise_xor(at_ref[1], other) * width, width)
        out_ref[:, pl.ds(lower, width)] = ref[...]


def ffn_kernel(base, planes, *refs):
    row_refs, (gate_ref, up_ref, down_ref) = refs[:planes], refs[planes : planes + 3]
    out_refs = refs[planes + 3 : 2 * planes + 3]
    buf, x_ref, y_ref, sem = refs[2 * planes + 3 :]
    sources, step, width = row_refs[0].shape
    experts = step // CAP
    copies = []
    for expert in range(experts):
        for which, ref in enumerate((gate_ref, up_ref, down_ref)):
            at = expert * 3 + which
            copy = pltpu.make_async_copy(ref.at[base + expert], buf.at[at], sem.at[at])
            copy.start()
            copies.append(copy)
    total = planes * sources * step
    for plane in range(planes):
        for source in range(sources):
            lower = (plane * sources + source) * step
            y_ref[lower : lower + step] = row_refs[plane][source].astype(F32)
    to = lax.broadcasted_iota(jnp.int32, (total, total), 0)
    frm = lax.broadcasted_iota(jnp.int32, (total, total), 1)
    per = total // experts
    order = (to % per // CAP) * step + (to // per) * CAP + to % CAP
    sort = jnp.where(frm == order, 1.0, 0.0).astype(BF16)
    x_ref[...] = jnp.dot(sort, y_ref[...].astype(BF16), preferred_element_type=F32).astype(BF16)
    nt = (((1,), (1,)), ((), ()))
    for expert in range(experts):
        rows = x_ref[expert * per : (expert + 1) * per]
        copies[expert * 3].wait()
        gate = lax.dot_general(rows, buf[expert * 3], nt, preferred_element_type=F32)
        copies[expert * 3 + 1].wait()
        up = lax.dot_general(rows, buf[expert * 3 + 1], nt, preferred_element_type=F32)
        hidden = (gate / (1.0 + jnp.exp(-gate)) * up).astype(BF16)
        copies[expert * 3 + 2].wait()
        piece = jnp.dot(hidden, buf[expert * 3 + 2], preferred_element_type=F32)
        x_ref[expert * per : (expert + 1) * per] = piece.astype(BF16)
    inverse = (to // step) * CAP + (to % step // CAP) * per + to % CAP
    unsort = jnp.where(frm == inverse, 1.0, 0.0).astype(BF16)
    y_ref[...] = jnp.dot(unsort, x_ref[...], preferred_element_type=F32)
    for plane in range(planes):
        for source in range(sources):
            lower = (plane * sources + source) * step
            out_refs[plane][source] = y_ref[lower : lower + step].astype(BF16)


def mix_kernel(ids_ref, weight_ref, *refs):
    in_refs, out_ref, y_ref = refs[:-2], refs[-2], refs[-1]
    dests, step = in_refs[0].shape[0], in_refs[0].shape[1]
    for dest in range(dests):
        for chunk, ref in enumerate(in_refs):
            lower = (dest * len(in_refs) + chunk) * step
            y_ref[lower : lower + step] = ref[dest].astype(F32)
    rows = y_ref[...].astype(BF16)
    n = ids_ref.shape[1]
    place = lax.broadcasted_iota(jnp.int32, (n, EXPERTS * CAP), 1)
    total = None
    for k, row in enumerate(slots(ids_ref[...])):
        pick = jnp.where(place == as_column(row), 1.0, 0.0).astype(BF16)
        part = as_column(weight_ref[k : k + 1]) * jnp.dot(pick, rows, preferred_element_type=F32)
        total = part if total is None else total + part
    out_ref[...] = total.astype(BF16)


def after(value, earlier):
    return lax.optimization_barrier((value, earlier))[0]


def shape(dims, kind=BF16):
    return jax.ShapeDtypeStruct(dims, kind)


def on_device(
    tokens,
    norm_gain,
    queries,
    attn_keys,
    attn_values,
    expert_ids,
    route_weights,
    gate_proj,
    up_proj,
    down_proj,
):
    exp_count = lax.axis_size("exp")
    seq_count = lax.axis_size("seq")
    local_tokens, features = tokens.shape
    exp_dev, hidden = gate_proj.shape[0], gate_proj.shape[1]
    chunks = CHUNKS
    experts = exp_dev // chunks
    step = experts * CAP
    group = exp_count // SEG_DEV
    seg_len = group * local_tokens
    segs = seq_count * SEG_DEV
    att = queries.shape[1]
    width = att // group

    block = seg_len // SUMS
    *send, sums = pl.pallas_call(
        functools.partial(prep_kernel, block),
        out_shape=[shape((exp_count, step, features))] * chunks
        + [shape((2 * local_tokens // block, att))],
        in_specs=[ANY, VMEM, VMEM, ANY, ANY],
        out_specs=[VMEM] * (chunks + 1),
        scratch_shapes=[
            pltpu.VMEM((local_tokens, features), BF16),
            pltpu.VMEM((local_tokens, att), BF16),
            pltpu.VMEM((local_tokens, att), BF16),
            pltpu.SemaphoreType.DMA((3,)),
        ],
        compiler_params=params(56),
        cost_estimate=LITTLE,
        name="prep",
    )(tokens, norm_gain.reshape(1, -1), expert_ids.T, attn_keys, attn_values)

    def device(segment, j):
        return (segment // SEG_DEV) * exp_count + (segment % SEG_DEV) * group + j

    parts = [sums]
    for other in range(1, segs):
        pairs = []
        for segment in range(segs):
            for j in range(group):
                pairs.append((device(segment, j), device(segment ^ other, j)))
        parts.append(lax.ppermute(sums, ("seq", "exp"), pairs))
    packed_rows = 3 * local_tokens + segs * 2 * local_tokens // block
    packed = pl.pallas_call(
        pack_kernel,
        out_shape=shape((group, packed_rows, width)),
        in_specs=[ANY] * 3 + [VMEM] * segs,
        out_specs=VMEM,
        scratch_shapes=[pltpu.SemaphoreType.DMA((3 * group,))],
        compiler_params=params(56),
        cost_estimate=LITTLE,
        name="pack",
    )(queries, attn_keys, attn_values, *parts)
    recv = [lax.all_to_all(after(send[0], parts), "exp", 0, 0, tiled=True)]
    for rows in send[1:]:
        recv.append(lax.all_to_all(after(rows, recv[-1]), "exp", 0, 0, tiled=True))
    arrived = []
    for rows in recv:
        planes = [rows]
        for other in range(1, seq_count):
            pairs = [(i, i ^ other) for i in range(seq_count)]
            planes.append(lax.ppermute(rows, "seq", pairs))
        arrived.append(planes)
    segment = lax.axis_index("seq") * SEG_DEV + lax.axis_index("exp") // group
    place = lax.axis_index("exp") % group
    position = jnp.stack([segment, place]).astype(jnp.int32)
    done, mine = [], []
    for chunk in range(chunks):
        planes = [after(arrived[chunk][0], recv[-1] if chunk == 0 else pieces[0])] + arrived[chunk][1:]
        total = seq_count * exp_count * step
        pieces = pl.pallas_call(
            functools.partial(ffn_kernel, chunk * experts, seq_count),
            out_shape=[shape((exp_count, step, features))] * seq_count,
            in_specs=[VMEM] * seq_count + [ANY] * 3,
            out_specs=[VMEM] * seq_count,
            scratch_shapes=[
                pltpu.VMEM((experts * 3, hidden, features), BF16),
                pltpu.VMEM((total, features), BF16),
                pltpu.VMEM((total, features), F32),
                pltpu.SemaphoreType.DMA((experts * 3,)),
            ],
            compiler_params=params(44),
            cost_estimate=pl.CostEstimate(
                flops=6 * total * hidden * features,
                bytes_accessed=3 * experts * 3 * hidden * features * 2,
                transcendentals=total * hidden,
            ),
            name="experts",
        )(*planes, gate_proj, up_proj, down_proj)
        done.append(pieces)
    packed = after(after(packed, recv[-1]), arrived[0])
    halves = [[half * group + j for j in range(group)] for half in range(SEG_DEV)]
    got = lax.all_to_all(packed, "exp", 0, 0, axis_index_groups=halves, tiled=True)
    for chunk, pieces in enumerate(done):
        summed = after(after(pieces[0], done[-1][0]), got).astype(F32)
        for other in range(1, seq_count):
            pairs = [(i, i ^ other) for i in range(seq_count)]
            summed = summed + lax.ppermute(pieces[other], "seq", pairs).astype(F32)
        mine.append(summed.astype(BF16))
    got = after(got, mine[0])
    head_out = pl.pallas_call(
        functools.partial(attend_kernel, min(256, seg_len), local_tokens, segs),
        out_shape=[shape((local_tokens, width))] * group,
        in_specs=[SMEM, VMEM],
        out_specs=[VMEM] * group,
        scratch_shapes=[pltpu.VMEM((group, local_tokens, width), BF16)],
        compiler_params=params(48),
        cost_estimate=LITTLE,
        name="attend",
    )(position, got)
    heads = [
        rows
        if other == 0
        else lax.ppermute(rows, "exp", [(i, i ^ other) for i in range(exp_count)])
        for other, rows in enumerate(head_out)
    ]
    attention = pl.pallas_call(
        place_kernel,
        out_shape=shape((local_tokens, att)),
        in_specs=[SMEM] + [VMEM] * group,
        out_specs=VMEM,
        compiler_params=params(32),
        cost_estimate=LITTLE,
        name="place",
    )(position, *heads)

    mine[-1] = after(mine[-1], heads[1:4])
    back = [lax.all_to_all(rows, "exp", 0, 0, tiled=True) for rows in mine]
    expert_mix = pl.pallas_call(
        mix_kernel,
        out_shape=shape((local_tokens, features)),
        in_specs=[VMEM] * (2 + chunks),
        out_specs=VMEM,
        scratch_shapes=[pltpu.VMEM((EXPERTS * CAP, features), F32)],
        compiler_params=params(32),
        cost_estimate=LITTLE,
        name="mix",
    )(expert_ids.T, route_weights.T, *back)
    return (attention, expert_mix)


def solution(mesh):
    return jax.shard_map(
        on_device,
        mesh=mesh,
        in_specs=(
            P(("seq", "exp"), None),
            P(),
            P(("seq", "exp"), None),
            P(("seq", "exp"), None),
            P(("seq", "exp"), None),
            P(("seq", "exp"), None),
            P(("seq", "exp"), None),
            P("exp", "seq", None),
            P("exp", "seq", None),
            P("exp", "seq", None),
        ),
        out_specs=(P(("seq", "exp"), None), P(("seq", "exp"), None)),
        check_vma=False,
    )
```

```python
import functools
import math

import jax
import jax.numpy as jnp
from jax import lax
from jax.experimental import pallas as pl
from jax.experimental.pallas import tpu as pltpu
from jax.sharding import PartitionSpec as P

EXPERTS = 64
HDIM = 64
SUMS = 64
SEG_DEV = 2
CAP = 2
CHUNKS = 2

EPS = 1e-05
NEG = -1e30
F32 = jnp.float32
BF16 = jnp.bfloat16

VMEM = pl.BlockSpec(memory_space=pltpu.VMEM)
ANY = pl.BlockSpec(memory_space=pl.ANY)
LITTLE = pl.CostEstimate(flops=1000, bytes_accessed=1000, transcendentals=0)
SMEM = pl.BlockSpec(memory_space=pltpu.SMEM)


def params(mib):
    return pltpu.CompilerParams(vmem_limit_bytes=mib * 2**20)


def as_column(row):
    n = row.shape[1]
    eye = lax.broadcasted_iota(jnp.int32, (n, n), 0) == lax.broadcasted_iota(jnp.int32, (n, n), 1)
    return jnp.sum(jnp.where(eye, row, jnp.zeros((), row.dtype)), axis=1, keepdims=True)


def slots(ids):
    n = ids.shape[1]
    rows = [ids[0:1], ids[1:2]]
    columns = [as_column(row) for row in rows]
    earlier = lax.broadcasted_iota(jnp.int32, (n, n), 0) < lax.broadcasted_iota(jnp.int32, (n, n), 1)
    found = []
    for row in rows:
        same = (columns[0] == row) | (columns[1] == row)
        before = jnp.sum(jnp.where(same & earlier, 1, 0), axis=0, keepdims=True)
        found.append(row * CAP + before)
    return found


def prep_kernel(block, tok_hbm, gain_ref, ids_ref, k_hbm, v_hbm, *refs):
    out_refs, sum_ref, (tok_ref, k_ref, v_ref, sem) = refs[:-5], refs[-5], refs[-4:]
    copies = [
        pltpu.make_async_copy(frm, to, sem.at[at])
        for at, (frm, to) in enumerate(((tok_hbm, tok_ref), (k_hbm, k_ref), (v_hbm, v_ref)))
    ]
    for copy in copies:
        copy.start()
    n = tok_ref.shape[0]
    first, second = slots(ids_ref[...])
    place = lax.broadcasted_iota(jnp.int32, (EXPERTS * CAP, n), 0)
    pick = jnp.where((place == first) | (place == second), 1.0, 0.0).astype(BF16)
    copies[0].wait()
    values = tok_ref[...].astype(F32)
    inv_rms = lax.rsqrt(jnp.mean(values * values, axis=-1, keepdims=True) + EPS)
    normed = (values * inv_rms * gain_ref[...]).astype(BF16)
    rows = jnp.dot(pick, normed, preferred_element_type=F32)
    dests, step = out_refs[0].shape[0], out_refs[0].shape[1]
    for dest in range(dests):
        for chunk, out_ref in enumerate(out_refs):
            lower = (dest * len(out_refs) + chunk) * step
            out_ref[dest] = rows[lower : lower + step].astype(BF16)
    count = n // block
    row = lax.broadcasted_iota(jnp.int32, (count, n), 0)
    column = lax.broadcasted_iota(jnp.int32, (count, n), 1)
    member = jnp.where(column // block == row, 1.0, 0.0).astype(BF16)
    for which, ref in enumerate((k_ref, v_ref)):
        copies[which + 1].wait()
        summed = jnp.dot(member, ref[...], preferred_element_type=F32) * (1.0 / math.sqrt(block))
        sum_ref[which * count : (which + 1) * count] = summed.astype(BF16)


def pack_kernel(q_hbm, k_hbm, v_hbm, out_ref, sem):
    dests, _, width = out_ref.shape
    tokens = q_hbm.shape[0]
    copies = []
    for dest in range(dests):
        for which, ref in enumerate((q_hbm, k_hbm, v_hbm)):
            copies.append(
                pltpu.make_async_copy(
                    ref.at[:, pl.ds(dest * width, width)],
                    out_ref.at[dest, pl.ds(which * tokens, tokens)],
                    sem.at[dest * 3 + which],
                )
            )
    for copy in copies:
        copy.start()
    for copy in copies:
        copy.wait()


def attend_kernel(query_rows, tokens, segs, at_ref, recv_ref, sum_hbm, *refs):
    out_refs, (mixed_ref, sum_ref, sem) = refs[:-3], refs[-3:]
    width = recv_ref.shape[2]
    columns = pl.ds(pl.multiple_of(at_ref[1] * width, width), width)
    copy = pltpu.make_async_copy(sum_hbm.at[:, :, columns], sum_ref, sem.at[0])
    copy.start()
    sources, _, width = recv_ref.shape
    seg_len = sources * tokens
    query, key, value = (
        recv_ref[:, which * tokens : (which + 1) * tokens].reshape(seg_len, width) for which in range(3)
    )
    sum_total = segs * SUMS
    per = SUMS // sources
    copy.wait()
    sum_keys = sum_ref[:, :per].reshape(sum_total, width)
    sum_values = sum_ref[:, per:].reshape(sum_total, width)
    scale = 1.0 / math.sqrt(HDIM)
    segment = at_ref[0]
    lane = lax.broadcasted_iota(jnp.int32, (1, width), 1)
    nt = (((1,), (1,)), ((), ()))
    for first in range(0, seg_len, query_rows):
        last = first + query_rows
        local_ok = (
            lax.broadcasted_iota(jnp.int32, (query_rows, last), 1)
            <= lax.broadcasted_iota(jnp.int32, (query_rows, last), 0) + first
        )
        summ_seg = lax.broadcasted_iota(jnp.int32, (query_rows, sum_total), 1) // SUMS
        summ_ok = summ_seg < segment
        mixed = jnp.zeros((query_rows, width), F32)
        for head in range(width // HDIM):
            mine = (lane >= head * HDIM) & (lane < (head + 1) * HDIM)
            rows = jnp.where(mine, query[first:last], jnp.zeros((), BF16))
            local_sc = lax.dot_general(rows, key[:last], nt, preferred_element_type=F32) * scale
            summ_sc = lax.dot_general(rows, sum_keys, nt, preferred_element_type=F32) * scale
            local_sc = jnp.where(local_ok, local_sc, NEG)
            summ_sc = jnp.where(summ_ok, summ_sc, NEG)
            top = jnp.maximum(
                jnp.max(local_sc, axis=-1, keepdims=True), jnp.max(summ_sc, axis=-1, keepdims=True)
            )
            local_ex = jnp.exp(local_sc - top)
            summ_ex = jnp.exp(summ_sc - top)
            inv = 1.0 / (
                jnp.sum(local_ex, axis=-1, keepdims=True) + jnp.sum(summ_ex, axis=-1, keepdims=True)
            )
            got = jnp.dot((local_ex * inv).astype(BF16), value[:last], preferred_element_type=F32)
            got += jnp.dot((summ_ex * inv).astype(BF16), sum_values, preferred_element_type=F32)
            mixed = jnp.where(mine, got, mixed)
        for source in range(first // tokens, last // tokens):
            lower = source * tokens - first
            mixed_ref[source] = mixed[lower : lower + tokens].astype(BF16)
    for other, out_ref in enumerate(out_refs):
        out_ref[...] = mixed_ref[jnp.bitwise_xor(at_ref[1], other)]


def place_kernel(at_ref, *refs):
    in_refs, out_ref = refs[:-1], refs[-1]
    width = in_refs[0].shape[1]
    for other, ref in enumerate(in_refs):
        lower = pl.multiple_of(jnp.bitwise_xor(at_ref[1], other) * width, width)
        out_ref[:, pl.ds(lower, width)] = ref[...]


def ffn_kernel(base, planes, *refs):
    row_refs, (gate_ref, up_ref, down_ref) = refs[:planes], refs[planes : planes + 3]
    out_refs = refs[planes + 3 : 2 * planes + 3]
    buf, x_ref, y_ref, sem = refs[2 * planes + 3 :]
    sources, step, width = row_refs[0].shape
    experts = step // CAP
    copies = []
    for expert in range(experts):
        for which, ref in enumerate((gate_ref, up_ref, down_ref)):
            at = expert * 3 + which
            copy = pltpu.make_async_copy(ref.at[base + expert], buf.at[at], sem.at[at])
            copy.start()
            copies.append(copy)
    total = planes * sources * step
    for plane in range(planes):
        for source in range(sources):
            lower = (plane * sources + source) * step
            y_ref[lower : lower + step] = row_refs[plane][source].astype(F32)
    to = lax.broadcasted_iota(jnp.int32, (total, total), 0)
    frm = lax.broadcasted_iota(jnp.int32, (total, total), 1)
    per = total // experts
    order = (to % per // CAP) * step + (to // per) * CAP + to % CAP
    sort = jnp.where(frm == order, 1.0, 0.0).astype(BF16)
    x_ref[...] = jnp.dot(sort, y_ref[...].astype(BF16), preferred_element_type=F32).astype(BF16)
    nt = (((1,), (1,)), ((), ()))
    for expert in range(experts):
        rows = x_ref[expert * per : (expert + 1) * per]
        copies[expert * 3].wait()
        gate = lax.dot_general(rows, buf[expert * 3], nt, preferred_element_type=F32)
        copies[expert * 3 + 1].wait()
        up = lax.dot_general(rows, buf[expert * 3 + 1], nt, preferred_element_type=F32)
        hidden = (gate / (1.0 + jnp.exp(-gate)) * up).astype(BF16)
        copies[expert * 3 + 2].wait()
        piece = jnp.dot(hidden, buf[expert * 3 + 2], preferred_element_type=F32)
        x_ref[expert * per : (expert + 1) * per] = piece.astype(BF16)
    inverse = (to // step) * CAP + (to % step // CAP) * per + to % CAP
    unsort = jnp.where(frm == inverse, 1.0, 0.0).astype(BF16)
    y_ref[...] = jnp.dot(unsort, x_ref[...], preferred_element_type=F32)
    for plane in range(planes):
        for source in range(sources):
            lower = (plane * sources + source) * step
            out_refs[plane][source] = y_ref[lower : lower + step].astype(BF16)


def mix_kernel(ids_ref, weight_ref, *refs):
    in_refs, out_ref, y_ref = refs[:-2], refs[-2], refs[-1]
    dests, step = in_refs[0].shape[0], in_refs[0].shape[1]
    for dest in range(dests):
        for chunk, ref in enumerate(in_refs):
            lower = (dest * len(in_refs) + chunk) * step
            y_ref[lower : lower + step] = ref[dest].astype(F32)
    rows = y_ref[...].astype(BF16)
    n = ids_ref.shape[1]
    place = lax.broadcasted_iota(jnp.int32, (n, EXPERTS * CAP), 1)
    total = None
    for k, row in enumerate(slots(ids_ref[...])):
        pick = jnp.where(place == as_column(row), 1.0, 0.0).astype(BF16)
        part = as_column(weight_ref[k : k + 1]) * jnp.dot(pick, rows, preferred_element_type=F32)
        total = part if total is None else total + part
    out_ref[...] = total.astype(BF16)


def after(value, earlier):
    return lax.optimization_barrier((value, earlier))[0]


def shape(dims, kind=BF16):
    return jax.ShapeDtypeStruct(dims, kind)


def on_device(
    tokens,
    norm_gain,
    queries,
    attn_keys,
    attn_values,
    expert_ids,
    route_weights,
    gate_proj,
    up_proj,
    down_proj,
):
    exp_count = lax.axis_size("exp")
    seq_count = lax.axis_size("seq")
    local_tokens, features = tokens.shape
    exp_dev, hidden = gate_proj.shape[0], gate_proj.shape[1]
    chunks = CHUNKS
    experts = exp_dev // chunks
    step = experts * CAP
    group = exp_count // SEG_DEV
    seg_len = group * local_tokens
    segs = seq_count * SEG_DEV
    att = queries.shape[1]
    width = att // group

    block = seg_len // SUMS
    *send, sums = pl.pallas_call(
        functools.partial(prep_kernel, block),
        out_shape=[shape((exp_count, step, features))] * chunks
        + [shape((2 * local_tokens // block, att))],
        in_specs=[ANY, VMEM, VMEM, ANY, ANY],
        out_specs=[VMEM] * (chunks + 1),
        scratch_shapes=[
            pltpu.VMEM((local_tokens, features), BF16),
            pltpu.VMEM((local_tokens, att), BF16),
            pltpu.VMEM((local_tokens, att), BF16),
            pltpu.SemaphoreType.DMA((3,)),
        ],
        compiler_params=params(56),
        cost_estimate=LITTLE,
        name="prep",
    )(tokens, norm_gain.reshape(1, -1), expert_ids.T, attn_keys, attn_values)

    gathered = lax.all_gather(sums, ("seq", "exp"), axis=0)
    packed = pl.pallas_call(
        pack_kernel,
        out_shape=shape((group, 3 * local_tokens, width)),
        in_specs=[ANY] * 3,
        out_specs=VMEM,
        scratch_shapes=[pltpu.SemaphoreType.DMA((3 * group,))],
        compiler_params=params(56),
        cost_estimate=LITTLE,
        name="pack",
    )(queries, attn_keys, attn_values)
    recv = [lax.all_to_all(send[0], "exp", 0, 0, tiled=True)]
    for rows in send[1:]:
        recv.append(lax.all_to_all(after(rows, recv[-1]), "exp", 0, 0, tiled=True))
    arrived = []
    for rows in recv:
        planes = [rows]
        for other in range(1, seq_count):
            pairs = [(i, i ^ other) for i in range(seq_count)]
            planes.append(lax.ppermute(rows, "seq", pairs))
        arrived.append(planes)
    segment = lax.axis_index("seq") * SEG_DEV + lax.axis_index("exp") // group
    place = lax.axis_index("exp") % group
    position = jnp.stack([segment, place]).astype(jnp.int32)
    done, mine = [], []
    for chunk in range(chunks):
        planes = [after(arrived[chunk][0], recv[-1] if chunk == 0 else pieces[0])] + arrived[chunk][1:]
        total = seq_count * exp_count * step
        pieces = pl.pallas_call(
            functools.partial(ffn_kernel, chunk * experts, seq_count),
            out_shape=[shape((exp_count, step, features))] * seq_count,
            in_specs=[VMEM] * seq_count + [ANY] * 3,
            out_specs=[VMEM] * seq_count,
            scratch_shapes=[
                pltpu.VMEM((experts * 3, hidden, features), BF16),
                pltpu.VMEM((total, features), BF16),
                pltpu.VMEM((total, features), F32),
                pltpu.SemaphoreType.DMA((experts * 3,)),
            ],
            compiler_params=params(44),
            cost_estimate=pl.CostEstimate(
                flops=6 * total * hidden * features,
                bytes_accessed=3 * experts * 3 * hidden * features * 2,
                transcendentals=total * hidden,
            ),
            name="experts",
        )(*planes, gate_proj, up_proj, down_proj)
        done.append(pieces)
    packed = after(after(packed, recv[-1]), arrived[0])
    halves = [[half * group + j for j in range(group)] for half in range(SEG_DEV)]
    got = lax.all_to_all(packed, "exp", 0, 0, axis_index_groups=halves, tiled=True)
    for chunk, pieces in enumerate(done):
        summed = after(after(pieces[0], done[-1][0]), got).astype(F32)
        for other in range(1, seq_count):
            pairs = [(i, i ^ other) for i in range(seq_count)]
            summed = summed + lax.ppermute(pieces[other], "seq", pairs).astype(F32)
        mine.append(summed.astype(BF16))
    got = after(got, mine[0])
    head_out = pl.pallas_call(
        functools.partial(attend_kernel, min(256, seg_len), local_tokens, segs),
        out_shape=[shape((local_tokens, width))] * group,
        in_specs=[SMEM, VMEM, ANY],
        out_specs=[VMEM] * group,
        scratch_shapes=[
            pltpu.VMEM((group, local_tokens, width), BF16),
            pltpu.VMEM((segs * group, sums.shape[0], width), BF16),
            pltpu.SemaphoreType.DMA((1,)),
        ],
        compiler_params=params(48),
        cost_estimate=LITTLE,
        name="attend",
    )(position, got, gathered)
    heads = [
        rows
        if other == 0
        else lax.ppermute(rows, "exp", [(i, i ^ other) for i in range(exp_count)])
        for other, rows in enumerate(head_out)
    ]
    attention = pl.pallas_call(
        place_kernel,
        out_shape=shape((local_tokens, att)),
        in_specs=[SMEM] + [VMEM] * group,
        out_specs=VMEM,
        compiler_params=params(32),
        cost_estimate=LITTLE,
        name="place",
    )(position, *heads)

    mine[-1] = after(mine[-1], heads[1:4])
    back = [lax.all_to_all(rows, "exp", 0, 0, tiled=True) for rows in mine]
    expert_mix = pl.pallas_call(
        mix_kernel,
        out_shape=shape((local_tokens, features)),
        in_specs=[VMEM] * (2 + chunks),
        out_specs=VMEM,
        scratch_shapes=[pltpu.VMEM((EXPERTS * CAP, features), F32)],
        compiler_params=params(32),
        cost_estimate=LITTLE,
        name="mix",
    )(expert_ids.T, route_weights.T, *back)
    return (attention, expert_mix)


def solution(mesh):
    return jax.shard_map(
        on_device,
        mesh=mesh,
        in_specs=(
            P(("seq", "exp"), None),
            P(),
            P(("seq", "exp"), None),
            P(("seq", "exp"), None),
            P(("seq", "exp"), None),
            P(("seq", "exp"), None),
            P(("seq", "exp"), None),
            P("exp", "seq", None),
            P("exp", "seq", None),
            P("exp", "seq", None),
        ),
        out_specs=(P(("seq", "exp"), None), P(("seq", "exp"), None)),
        check_vma=False,
    )
```

```python
import functools
import math

import jax
import jax.numpy as jnp
from jax import lax
from jax.experimental import pallas as pl
from jax.experimental.pallas import tpu as pltpu
from jax.sharding import PartitionSpec as P

EXPERTS = 64
HDIM = 64
SUMS = 64
SEG_DEV = 2
CAP = 2
CHUNKS = 2

EPS = 1e-05
NEG = -1e30
F32 = jnp.float32
BF16 = jnp.bfloat16

VMEM = pl.BlockSpec(memory_space=pltpu.VMEM)
ANY = pl.BlockSpec(memory_space=pl.ANY)
LITTLE = pl.CostEstimate(flops=1000, bytes_accessed=1000, transcendentals=0)
SMEM = pl.BlockSpec(memory_space=pltpu.SMEM)


def params(mib):
    return pltpu.CompilerParams(vmem_limit_bytes=mib * 2**20)


def as_column(row):
    n = row.shape[1]
    eye = lax.broadcasted_iota(jnp.int32, (n, n), 0) == lax.broadcasted_iota(jnp.int32, (n, n), 1)
    return jnp.sum(jnp.where(eye, row, jnp.zeros((), row.dtype)), axis=1, keepdims=True)


def slots(ids):
    n = ids.shape[1]
    rows = [ids[0:1], ids[1:2]]
    columns = [as_column(row) for row in rows]
    earlier = lax.broadcasted_iota(jnp.int32, (n, n), 0) < lax.broadcasted_iota(jnp.int32, (n, n), 1)
    found = []
    for row in rows:
        same = (columns[0] == row) | (columns[1] == row)
        before = jnp.sum(jnp.where(same & earlier, 1, 0), axis=0, keepdims=True)
        found.append(row * CAP + before)
    return found


def prep_kernel(tok_hbm, gain_ref, ids_ref, *refs):
    out_refs, (tok_ref, sem) = refs[:-2], refs[-2:]
    copy = pltpu.make_async_copy(tok_hbm, tok_ref, sem.at[0])
    copy.start()
    n = tok_ref.shape[0]
    first, second = slots(ids_ref[...])
    place = lax.broadcasted_iota(jnp.int32, (EXPERTS * CAP, n), 0)
    pick = jnp.where((place == first) | (place == second), 1.0, 0.0).astype(BF16)
    copy.wait()
    values = tok_ref[...].astype(F32)
    inv_rms = lax.rsqrt(jnp.mean(values * values, axis=-1, keepdims=True) + EPS)
    normed = (values * inv_rms * gain_ref[...]).astype(BF16)
    rows = jnp.dot(pick, normed, preferred_element_type=F32)
    dests, step = out_refs[0].shape[0], out_refs[0].shape[1]
    for dest in range(dests):
        for chunk, out_ref in enumerate(out_refs):
            lower = (dest * len(out_refs) + chunk) * step
            out_ref[dest] = rows[lower : lower + step].astype(BF16)


def sums_kernel(block, recv_ref, out_ref):
    sources, rows, width = recv_ref.shape
    tokens = rows // 3
    total = sources * tokens
    row = lax.broadcasted_iota(jnp.int32, (SUMS, total), 0)
    column = lax.broadcasted_iota(jnp.int32, (SUMS, total), 1)
    member = jnp.where(column // block == row, 1.0, 0.0).astype(BF16)
    for which in range(2):
        values = recv_ref[:, (which + 1) * tokens : (which + 2) * tokens].reshape(total, width)
        summed = jnp.dot(member, values, preferred_element_type=F32) * (1.0 / math.sqrt(block))
        out_ref[which * SUMS : (which + 1) * SUMS] = summed.astype(BF16)


def pack_kernel(q_hbm, k_hbm, v_hbm, out_ref, sem):
    dests, _, width = out_ref.shape
    tokens = q_hbm.shape[0]
    copies = []
    for dest in range(dests):
        for which, ref in enumerate((q_hbm, k_hbm, v_hbm)):
            copies.append(
                pltpu.make_async_copy(
                    ref.at[:, pl.ds(dest * width, width)],
                    out_ref.at[dest, pl.ds(which * tokens, tokens)],
                    sem.at[dest * 3 + which],
                )
            )
    for copy in copies:
        copy.start()
    for copy in copies:
        copy.wait()


def attend_kernel(query_rows, tokens, segs, at_ref, recv_ref, *refs):
    sum_refs, out_refs, mixed_ref = refs[:segs], refs[segs:-1], refs[-1]
    sources, _, width = recv_ref.shape
    seg_len = sources * tokens
    query, key, value = (
        recv_ref[:, which * tokens : (which + 1) * tokens].reshape(seg_len, width) for which in range(3)
    )
    sum_total = segs * SUMS
    sum_keys = jnp.concatenate([ref[:SUMS] for ref in sum_refs], axis=0)
    sum_values = jnp.concatenate([ref[SUMS:] for ref in sum_refs], axis=0)
    scale = 1.0 / math.sqrt(HDIM)
    segment = at_ref[0]
    lane = lax.broadcasted_iota(jnp.int32, (1, width), 1)
    nt = (((1,), (1,)), ((), ()))
    for first in range(0, seg_len, query_rows):
        last = first + query_rows
        local_ok = (
            lax.broadcasted_iota(jnp.int32, (query_rows, last), 1)
            <= lax.broadcasted_iota(jnp.int32, (query_rows, last), 0) + first
        )
        summ_seg = lax.broadcasted_iota(jnp.int32, (query_rows, sum_total), 1) // SUMS
        summ_ok = jnp.bitwise_xor(summ_seg, segment) < segment
        mixed = jnp.zeros((query_rows, width), F32)
        for head in range(width // HDIM):
            mine = (lane >= head * HDIM) & (lane < (head + 1) * HDIM)
            rows = jnp.where(mine, query[first:last], jnp.zeros((), BF16))
            local_sc = lax.dot_general(rows, key[:last], nt, preferred_element_type=F32) * scale
            summ_sc = lax.dot_general(rows, sum_keys, nt, preferred_element_type=F32) * scale
            local_sc = jnp.where(local_ok, local_sc, NEG)
            summ_sc = jnp.where(summ_ok, summ_sc, NEG)
            top = jnp.maximum(
                jnp.max(local_sc, axis=-1, keepdims=True), jnp.max(summ_sc, axis=-1, keepdims=True)
            )
            local_ex = jnp.exp(local_sc - top)
            summ_ex = jnp.exp(summ_sc - top)
            inv = 1.0 / (
                jnp.sum(local_ex, axis=-1, keepdims=True) + jnp.sum(summ_ex, axis=-1, keepdims=True)
            )
            got = jnp.dot((local_ex * inv).astype(BF16), value[:last], preferred_element_type=F32)
            got += jnp.dot((summ_ex * inv).astype(BF16), sum_values, preferred_element_type=F32)
            mixed = jnp.where(mine, got, mixed)
        for source in range(first // tokens, last // tokens):
            lower = source * tokens - first
            mixed_ref[source] = mixed[lower : lower + tokens].astype(BF16)
    for other, out_ref in enumerate(out_refs):
        out_ref[...] = mixed_ref[jnp.bitwise_xor(at_ref[1], other)]


def place_kernel(at_ref, *refs):
    in_refs, out_ref = refs[:-1], refs[-1]
    width = in_refs[0].shape[1]
    for other, ref in enumerate(in_refs):
        lower = pl.multiple_of(jnp.bitwise_xor(at_ref[1], other) * width, width)
        out_ref[:, pl.ds(lower, width)] = ref[...]


def ffn_kernel(base, planes, *refs):
    row_refs, (gate_ref, up_ref, down_ref) = refs[:planes], refs[planes : planes + 3]
    out_refs = refs[planes + 3 : 2 * planes + 3]
    buf, x_ref, y_ref, sem = refs[2 * planes + 3 :]
    sources, step, width = row_refs[0].shape
    experts = step // CAP
    copies = []
    for expert in range(experts):
        for which, ref in enumerate((gate_ref, up_ref, down_ref)):
            at = expert * 3 + which
            copy = pltpu.make_async_copy(ref.at[base + expert], buf.at[at], sem.at[at])
            copy.start()
            copies.append(copy)
    total = planes * sources * step
    for plane in range(planes):
        for source in range(sources):
            lower = (plane * sources + source) * step
            y_ref[lower : lower + step] = row_refs[plane][source].astype(F32)
    to = lax.broadcasted_iota(jnp.int32, (total, total), 0)
    frm = lax.broadcasted_iota(jnp.int32, (total, total), 1)
    per = total // experts
    order = (to % per // CAP) * step + (to // per) * CAP + to % CAP
    sort = jnp.where(frm == order, 1.0, 0.0).astype(BF16)
    x_ref[...] = jnp.dot(sort, y_ref[...].astype(BF16), preferred_element_type=F32).astype(BF16)
    nt = (((1,), (1,)), ((), ()))
    for expert in range(experts):
        rows = x_ref[expert * per : (expert + 1) * per]
        copies[expert * 3].wait()
        gate = lax.dot_general(rows, buf[expert * 3], nt, preferred_element_type=F32)
        copies[expert * 3 + 1].wait()
        up = lax.dot_general(rows, buf[expert * 3 + 1], nt, preferred_element_type=F32)
        hidden = (gate / (1.0 + jnp.exp(-gate)) * up).astype(BF16)
        copies[expert * 3 + 2].wait()
        piece = jnp.dot(hidden, buf[expert * 3 + 2], preferred_element_type=F32)
        x_ref[expert * per : (expert + 1) * per] = piece.astype(BF16)
    inverse = (to // step) * CAP + (to % step // CAP) * per + to % CAP
    unsort = jnp.where(frm == inverse, 1.0, 0.0).astype(BF16)
    y_ref[...] = jnp.dot(unsort, x_ref[...], preferred_element_type=F32)
    for plane in range(planes):
        for source in range(sources):
            lower = (plane * sources + source) * step
            out_refs[plane][source] = y_ref[lower : lower + step].astype(BF16)


def mix_kernel(ids_ref, weight_ref, *refs):
    in_refs, out_ref, y_ref = refs[:-2], refs[-2], refs[-1]
    dests, step = in_refs[0].shape[0], in_refs[0].shape[1]
    for dest in range(dests):
        for chunk, ref in enumerate(in_refs):
            lower = (dest * len(in_refs) + chunk) * step
            y_ref[lower : lower + step] = ref[dest].astype(F32)
    rows = y_ref[...].astype(BF16)
    n = ids_ref.shape[1]
    place = lax.broadcasted_iota(jnp.int32, (n, EXPERTS * CAP), 1)
    total = None
    for k, row in enumerate(slots(ids_ref[...])):
        pick = jnp.where(place == as_column(row), 1.0, 0.0).astype(BF16)
        part = as_column(weight_ref[k : k + 1]) * jnp.dot(pick, rows, preferred_element_type=F32)
        total = part if total is None else total + part
    out_ref[...] = total.astype(BF16)


def after(value, earlier):
    return lax.optimization_barrier((value, earlier))[0]


def shape(dims, kind=BF16):
    return jax.ShapeDtypeStruct(dims, kind)


def on_device(
    tokens,
    norm_gain,
    queries,
    attn_keys,
    attn_values,
    expert_ids,
    route_weights,
    gate_proj,
    up_proj,
    down_proj,
):
    exp_count = lax.axis_size("exp")
    seq_count = lax.axis_size("seq")
    local_tokens, features = tokens.shape
    exp_dev, hidden = gate_proj.shape[0], gate_proj.shape[1]
    chunks = CHUNKS
    experts = exp_dev // chunks
    step = experts * CAP
    group = exp_count // SEG_DEV
    seg_len = group * local_tokens
    segs = seq_count * SEG_DEV
    att = queries.shape[1]
    width = att // group

    send = pl.pallas_call(
        prep_kernel,
        out_shape=[shape((exp_count, step, features))] * chunks,
        in_specs=[ANY, VMEM, VMEM],
        out_specs=[VMEM] * chunks,
        scratch_shapes=[pltpu.VMEM((local_tokens, features), BF16), pltpu.SemaphoreType.DMA((1,))],
        compiler_params=params(56),
        cost_estimate=LITTLE,
        name="prep",
    )(tokens, norm_gain.reshape(1, -1), expert_ids.T)

    def device(segment, j):
        return (segment // SEG_DEV) * exp_count + (segment % SEG_DEV) * group + j

    packed = pl.pallas_call(
        pack_kernel,
        out_shape=shape((group, 3 * local_tokens, width)),
        in_specs=[ANY] * 3,
        out_specs=VMEM,
        scratch_shapes=[pltpu.SemaphoreType.DMA((3 * group,))],
        compiler_params=params(56),
        cost_estimate=LITTLE,
        name="pack",
    )(queries, attn_keys, attn_values)
    recv = [lax.all_to_all(send[0], "exp", 0, 0, tiled=True)]
    for rows in send[1:]:
        recv.append(lax.all_to_all(after(rows, recv[-1]), "exp", 0, 0, tiled=True))
    arrived = []
    for rows in recv:
        planes = [rows]
        for other in range(1, seq_count):
            pairs = [(i, i ^ other) for i in range(seq_count)]
            planes.append(lax.ppermute(rows, "seq", pairs))
        arrived.append(planes)
    segment = lax.axis_index("seq") * SEG_DEV + lax.axis_index("exp") // group
    place = lax.axis_index("exp") % group
    position = jnp.stack([segment, place]).astype(jnp.int32)
    done, mine = [], []
    for chunk in range(chunks):
        planes = [after(arrived[chunk][0], recv[-1] if chunk == 0 else pieces[0])] + arrived[chunk][1:]
        total = seq_count * exp_count * step
        pieces = pl.pallas_call(
            functools.partial(ffn_kernel, chunk * experts, seq_count),
            out_shape=[shape((exp_count, step, features))] * seq_count,
            in_specs=[VMEM] * seq_count + [ANY] * 3,
            out_specs=[VMEM] * seq_count,
            scratch_shapes=[
                pltpu.VMEM((experts * 3, hidden, features), BF16),
                pltpu.VMEM((total, features), BF16),
                pltpu.VMEM((total, features), F32),
                pltpu.SemaphoreType.DMA((experts * 3,)),
            ],
            compiler_params=params(44),
            cost_estimate=pl.CostEstimate(
                flops=6 * total * hidden * features,
                bytes_accessed=3 * experts * 3 * hidden * features * 2,
                transcendentals=total * hidden,
            ),
            name="experts",
        )(*planes, gate_proj, up_proj, down_proj)
        done.append(pieces)
    packed = after(after(packed, recv[-1]), arrived[0])
    halves = [[half * group + j for j in range(group)] for half in range(SEG_DEV)]
    got = lax.all_to_all(packed, "exp", 0, 0, axis_index_groups=halves, tiled=True)
    sums = pl.pallas_call(
        functools.partial(sums_kernel, seg_len // SUMS),
        out_shape=shape((2 * SUMS, width)),
        in_specs=[VMEM],
        out_specs=VMEM,
        compiler_params=params(32),
        cost_estimate=LITTLE,
        name="sums",
    )(got)
    parts = [sums]
    for other in range(1, segs):
        pairs = []
        for frm in range(segs):
            for j in range(group):
                pairs.append((device(frm, j), device(frm ^ other, j)))
        parts.append(lax.ppermute(sums, ("seq", "exp"), pairs))
    for chunk, pieces in enumerate(done):
        summed = after(after(pieces[0], done[-1][0]), got).astype(F32)
        for other in range(1, seq_count):
            pairs = [(i, i ^ other) for i in range(seq_count)]
            summed = summed + lax.ppermute(pieces[other], "seq", pairs).astype(F32)
        mine.append(summed.astype(BF16))
    got = after(got, mine[0])
    head_out = pl.pallas_call(
        functools.partial(attend_kernel, min(256, seg_len), local_tokens, segs),
        out_shape=[shape((local_tokens, width))] * group,
        in_specs=[SMEM, VMEM] + [VMEM] * segs,
        out_specs=[VMEM] * group,
        scratch_shapes=[pltpu.VMEM((group, local_tokens, width), BF16)],
        compiler_params=params(48),
        cost_estimate=LITTLE,
        name="attend",
    )(position, got, *parts)
    heads = [
        rows
        if other == 0
        else lax.ppermute(rows, "exp", [(i, i ^ other) for i in range(exp_count)])
        for other, rows in enumerate(head_out)
    ]
    attention = pl.pallas_call(
        place_kernel,
        out_shape=shape((local_tokens, att)),
        in_specs=[SMEM] + [VMEM] * group,
        out_specs=VMEM,
        compiler_params=params(32),
        cost_estimate=LITTLE,
        name="place",
    )(position, *heads)

    mine[-1] = after(mine[-1], parts)
    back = [lax.all_to_all(rows, "exp", 0, 0, tiled=True) for rows in mine]
    expert_mix = pl.pallas_call(
        mix_kernel,
        out_shape=shape((local_tokens, features)),
        in_specs=[VMEM] * (2 + chunks),
        out_specs=VMEM,
        scratch_shapes=[pltpu.VMEM((EXPERTS * CAP, features), F32)],
        compiler_params=params(32),
        cost_estimate=LITTLE,
        name="mix",
    )(expert_ids.T, route_weights.T, *back)
    return (attention, expert_mix)


def solution(mesh):
    return jax.shard_map(
        on_device,
        mesh=mesh,
        in_specs=(
            P(("seq", "exp"), None),
            P(),
            P(("seq", "exp"), None),
            P(("seq", "exp"), None),
            P(("seq", "exp"), None),
            P(("seq", "exp"), None),
            P(("seq", "exp"), None),
            P("exp", "seq", None),
            P("exp", "seq", None),
            P("exp", "seq", None),
        ),
        out_specs=(P(("seq", "exp"), None), P(("seq", "exp"), None)),
        check_vma=False,
    )
```
